32 devices in a mesh: slab: 4 (over y, core), plane: 8 (over z, x).
Axes of the slice: x: 2, y: 2, z: 4, core: 2. Of those that a mesh axis runs over, the one named last changes fastest.
Arguments:
- start_disp: float32 [3, 64, 128, 128], P(None, 'slab', 'plane'), may hold values from -6 to 6
- load: float32 [3, 64, 128, 128], P(None, 'slab', 'plane'), may hold values from -6 to 6
- shift: float32 [64, 128, 128], P('slab', 'plane'), may hold values from 0.25 to 2
- coarse: float32 [3, 32, 64, 128], P(None, 'slab', 'plane'), may hold values from -6 to 6
- aggregate: int32 [64, 128], P('slab', 'plane'), may hold values from 0 to 2047, as said below
- consistency: float32 [64, 128, 128], P('slab', 'plane'), may hold values from 0.5 to 2
Outputs:
- displacement: float32 [3, 64, 128, 128], P(None, 'slab', 'plane')
- recovered: float32 [6, 64, 128, 128], P(None, 'slab', 'plane')
- indicator: float32 [64, 128, 128], P('slab', 'plane')
The draws below stay inside these ranges and needn't reach their ends.
Inputs may be any that keep to these rules, and one draw needn't show every extreme that they name: aggregate[i, j] = a * 64 + b with |a - i // 2| <= 1 and |b - j // 2| <= 1.
All inputs are finite; a program needn't handle non-finite values.
Results may differ from the reference program's by a relative error of at most 0.000029.
Values sent between devices are 32-bit elements; how exact they have to be, the bound alone decides.
A program may use at most 64 MiB of HBM per device.

```python
import math
import jax
import jax.numpy as jnp

CZ = 128
DEGREE = 4
NX = 64
NY = 128
KX = 32
KY = 64


def draw_aggregate(key, part):
    key = jax.random.fold_in(key, 7)
    key_a, key_b = jax.random.split(key)
    ix = jnp.arange(NX)[:, None]
    iy = jnp.arange(NY)[None, :]
    step_a = jax.random.randint(key_a, (NX, NY), -1, 2)
    step_b = jax.random.randint(key_b, (NX, NY), -1, 2)
    corner = (ix == 0) & (iy == 0) | (ix == NX - 1) & (iy == NY - 1)
    step_a = jnp.where(corner, 0, step_a)
    step_b = jnp.where(corner, 0, step_b)
    row_a = jnp.clip(ix // 2 + step_a, 0, NX // 2 - 1)
    row_b = jnp.clip(iy // 2 + step_b, 0, NY // 2 - 1)
    return (row_a * (NY // 2) + row_b).astype(jnp.int32)


def levels(stream_key, extent, cuts, smallest, high):
    def one(dim, parts):
        heights = jax.random.uniform(jax.random.fold_in(jax.random.fold_in(stream_key, 6), dim), (parts,), jnp.float32, smallest / len(cuts), high / len(cuts))
        return jnp.repeat(jnp.exp(heights), extent[dim] // parts).reshape((-1,) + (1,) * (len(extent) - dim - 1))

    factor_of = one(*cuts[0])
    for cut in cuts[1:]:
        factor_of = factor_of * one(*cut)
    return factor_of


def bell_draw(own_key, dims, width, bound, shards=(), kind=jnp.bfloat16):
    values = width * jax.random.normal(own_key, dims, jnp.float32)
    if shards:
        values = values * levels(own_key, dims, shards, -0.22, 0.18)
    return jnp.clip(values, -bound, bound).astype(kind)


def setup_inputs(seed: int = 0) -> dict:
    splits = jax.random.split(jax.random.key(seed), 7)
    return {
        "start_disp": bell_draw(splits[0], (3, NX, NY, CZ), 1.0, 6.0, ((1, 4), (2, 8)), jnp.float32),
        "load": bell_draw(splits[1], (3, NX, NY, CZ), 1.0, 6.0, ((1, 4), (2, 8)), jnp.float32),
        "shift": jnp.clip(0.25 + 1.75 * jax.random.uniform(splits[2], (NX, NY, CZ), jnp.float32) ** levels(splits[2], (NX, NY, CZ), ((0, 4), (1, 8)), -0.2, 0.2), 0.25, 2.0),
        "coarse": bell_draw(splits[3], (3, KX, KY, CZ), 1.0, 6.0, ((1, 4), (2, 8)), jnp.float32),
        "aggregate": draw_aggregate(jax.random.fold_in(splits[6], 71), 0),
        "consistency": jnp.clip(jnp.exp(math.log(2.0) - 1.3862944 * jax.random.uniform(splits[5], (NX, NY, CZ), jnp.float32) ** levels(splits[5], (NX, NY, CZ), ((0, 4), (1, 8)), -0.2, 0.2)), 0.5, 2.0),
    }


THETA = 4.5
DELTA_C = 3.5


def stiff_apply(padded, shift_part):
    zpad = jnp.pad(padded, ((0, 0), (0, 0), (0, 0), (1, 1)))
    along_z = zpad[..., :-2] + zpad[..., 1:-1] + zpad[..., 2:]
    along_x = along_z[:, :-2] + along_z[:, 1:-1] + along_z[:, 2:]
    boxed = along_x[:, :, :-2] + along_x[:, :, 1:-1] + along_x[:, :, 2:]
    centre = padded[:, 1:-1, 1:-1]
    return (3.0 + shift_part) * centre - boxed / 3.0


def element_stress(corners, consist):
    zpad = jnp.pad(corners, ((0, 0), (0, 0), (0, 0), (0, 1)))
    diff_x = zpad[:, 1:] - zpad[:, :-1]
    grad_x = 0.25 * (diff_x[:, :, :-1, :-1] + diff_x[:, :, 1:, :-1] + diff_x[:, :, :-1, 1:] + diff_x[:, :, 1:, 1:])
    diff_y = zpad[:, :, 1:] - zpad[:, :, :-1]
    grad_y = 0.25 * (diff_y[:, :-1, :, :-1] + diff_y[:, 1:, :, :-1] + diff_y[:, :-1, :, 1:] + diff_y[:, 1:, :, 1:])
    diff_z = zpad[..., 1:] - zpad[..., :-1]
    grad_z = 0.25 * (diff_z[:, :-1, :-1] + diff_z[:, 1:, :-1] + diff_z[:, :-1, 1:] + diff_z[:, 1:, 1:])
    exx = grad_x[0]
    eyy = grad_y[1]
    ezz = grad_z[2]
    exy = 0.5 * (grad_y[0] + grad_x[1])
    eyz = 0.5 * (grad_z[1] + grad_y[2])
    ezx = 0.5 * (grad_x[2] + grad_z[0])
    trace = exx + eyy + ezz
    sxx = exx - trace / 3.0
    syy = eyy - trace / 3.0
    szz = ezz - trace / 3.0
    equiv = (2.0 / 3.0) * (sxx * sxx + syy * syy + szz * szz + 2.0 * (exy * exy + eyz * eyz + ezx * ezx))
    visc = consist * (0.01 + 3.0 * equiv) ** ((0.15 - 1.0) / 2.0)
    sig = [2.0 * visc * sxx + 4.0 * trace, 2.0 * visc * syy + 4.0 * trace, 2.0 * visc * szz + 4.0 * trace,
           2.0 * visc * exy, 2.0 * visc * eyz, 2.0 * visc * ezx]
    norm_sq = sig[0] * sig[0] + sig[1] * sig[1] + sig[2] * sig[2] + 2.0 * (sig[3] * sig[3] + sig[4] * sig[4] + sig[5] * sig[5])
    return jnp.stack(sig + [norm_sq], 0)


def finish_nodes(total, count):
    rec = total[:6] / count
    norm_rec = rec[0] * rec[0] + rec[1] * rec[1] + rec[2] * rec[2] + 2.0 * (rec[3] * rec[3] + rec[4] * rec[4] + rec[5] * rec[5])
    return rec, total[6] / count - norm_rec


def reference(start_disp, load, shift, coarse, aggregate, consistency):
    table = coarse.reshape(3, KX * KY, CZ)
    moved = jnp.take(table, aggregate.reshape(-1), axis=1).reshape(3, NX, NY, CZ)
    disp = start_disp + moved
    pad_xy = ((0, 0), (1, 1), (1, 1), (0, 0))

    def stiff(field):
        return stiff_apply(jnp.pad(field, pad_xy), shift)

    sigma = THETA / DELTA_C
    resid = load - stiff(disp)
    direction = resid / THETA
    rho = 1.0 / sigma
    for step in range(DEGREE):
        disp = disp + direction
        if step < DEGREE - 1:
            resid = resid - stiff(direction)
            rho_new = 1.0 / (2.0 * sigma - rho)
            direction = (rho_new * rho) * direction + (2.0 * rho_new / DELTA_C) * resid
            rho = rho_new
    corners = jnp.pad(disp, ((0, 0), (0, 1), (0, 1), (0, 0)))
    ix = jnp.arange(NX)[:, None, None]
    iy = jnp.arange(NY)[None, :, None]
    iz = jnp.arange(CZ)[None, None, :]
    valid = ((ix <= NX - 2) & (iy <= NY - 2) & (iz <= CZ - 2)).astype(jnp.float32)
    elem = element_stress(corners, consistency) * valid
    front = jnp.pad(elem, ((0, 0), (1, 0), (1, 0), (1, 0)))
    sum_x = front[:, 1:] + front[:, :-1]
    sum_y = sum_x[:, :, 1:] + sum_x[:, :, :-1]
    total = sum_y[..., 1:] + sum_y[..., :-1]
    count = (((ix >= 1).astype(jnp.float32) + (ix <= NX - 2).astype(jnp.float32))
             * ((iy >= 1).astype(jnp.float32) + (iy <= NY - 2).astype(jnp.float32))
             * ((iz >= 1).astype(jnp.float32) + (iz <= CZ - 2).astype(jnp.float32)))
    rec, indic = finish_nodes(total, count)
    return disp, rec, indic
```

```python
import functools

import jax
import jax.numpy as jnp
from jax import lax
from jax.experimental import pallas as pl
from jax.experimental.pallas import tpu as pltpu
from jax.sharding import PartitionSpec as P

DEGREE = 4
THETA = 4.5
DELTA_C = 3.5
SIGMA = THETA / DELTA_C
MESH = pl.DeviceIdType.MESH
OFF = 8
SIDES = ((0, 1), (0, -1), (1, 1), (1, -1), (-1, 1), (-1, -1), (1, 0), (-1, 0))
LOW_SIDES = ((0, 1), (1, 1), (1, 0))


def edge(step, first, count):
    if step > 0:
        return pl.ds(first + count - 1, 1), pl.ds(first - 1, 1)
    if step < 0:
        return pl.ds(first, 1), pl.ds(first + count, 1)
    return pl.ds(first, count), pl.ds(first, count)


def box_z(x):
    lane = lax.broadcasted_iota(jnp.int32, x.shape, x.ndim - 1)
    depth = x.shape[-1]
    below = jnp.where(lane == 0, 0.0, pltpu.roll(x, 1, x.ndim - 1))
    above = jnp.where(lane == depth - 1, 0.0, pltpu.roll(x, depth - 1, x.ndim - 1))
    return x + below + above


def next_z(x):
    return pltpu.roll(x, x.shape[-1] - 1, x.ndim - 1)


def previous_z(x):
    return pltpu.roll(x, 1, x.ndim - 1)


def smooth(sizes, refs):
    nx, ny, depth, kx, ky, slabs, planes = sizes
    (start_hbm, load_hbm, shift_hbm, coarse_hbm, agg_hbm, cons_hbm,
     start, load, shift, table, agg, cons, fields, resid,
     in_sem, send_sem, recv_sem) = refs
    slab = lax.axis_index("slab")
    plane = lax.axis_index("plane")

    def exists(step_x, step_y):
        x, y = slab + step_x, plane + step_y
        return (x >= 0) & (x < slabs) & (y >= 0) & (y < planes)

    loads = [
        pltpu.make_async_copy(coarse_hbm, table.at[:, pl.ds(1, kx), pl.ds(0, ky)], in_sem.at[0]),
        pltpu.make_async_copy(agg_hbm, agg, in_sem.at[1]),
        pltpu.make_async_copy(start_hbm, start, in_sem.at[2]),
        pltpu.make_async_copy(cons_hbm, cons.at[pl.ds(1, nx), pl.ds(OFF, ny)], in_sem.at[3]),
        pltpu.make_async_copy(load_hbm, load, in_sem.at[4]),
        pltpu.make_async_copy(shift_hbm, shift, in_sem.at[5]),
    ]
    for copy in loads:
        copy.start()

    zero_table = jnp.zeros((3, 8, depth), jnp.float32)
    for a in range(kx + 2):
        table[:, a, ky:ky + 8, :] = zero_table
    table[:, 0, 0:ky, :] = zero_table
    table[:, kx + 1, 0:ky, :] = zero_table

    barrier = pltpu.get_barrier_semaphore()
    for step_x, step_y in SIDES:
        @pl.when(exists(step_x, step_y))
        def _():
            pl.semaphore_signal(
                barrier, inc=1, device_id=(slab + step_x, plane + step_y), device_id_type=MESH
            )

    zero_row = jnp.zeros((nx + 2, depth), jnp.float32)
    for step_x, step_y in ((0, 1), (0, -1), (1, 0), (-1, 0)):
        @pl.when(jnp.logical_not(exists(-step_x, -step_y)))
        def _():
            for phase in range(DEGREE + 1):
                for c in range(3):
                    if step_y:
                        row = OFF - 1 if step_y > 0 else OFF + ny
                        for i in range(nx + 2):
                            fields[phase, c, i, row:row + 1, :] = zero_row[0:1]
                    else:
                        i = 0 if step_x > 0 else nx + 1
                        for at in range(0, ny + 16, 8):
                            fields[phase, c, i, at:at + 8, :] = zero_row[0:8]

    near_x = 1 + (slab > 0).astype(jnp.int32) + (slab < slabs - 1).astype(jnp.int32)
    near_y = 1 + (plane > 0).astype(jnp.int32) + (plane < planes - 1).astype(jnp.int32)
    pl.semaphore_wait(barrier, near_x * near_y - 1)

    def remote(source, target, phase, side):
        step_x, step_y = SIDES[side]
        return pltpu.make_async_remote_copy(
            src_ref=source, dst_ref=target,
            send_sem=send_sem.at[phase, side], recv_sem=recv_sem.at[phase, side],
            device_id=(slab + step_x, plane + step_y), device_id_type=MESH,
        )

    def start_all(make, phase, sides=SIDES):
        for side, (step_x, step_y) in enumerate(SIDES):
            if (step_x, step_y) in sides:
                @pl.when(exists(step_x, step_y))
                def _():
                    remote(*make(step_x, step_y), phase, side).start()

    def wait_arrived(make, phase, sides=SIDES):
        for side, (step_x, step_y) in enumerate(SIDES):
            if (step_x, step_y) in sides:
                @pl.when(exists(-step_x, -step_y))
                def _():
                    remote(*make(step_x, step_y), phase, side).wait_recv()

    def wait_sent(make, phase, sides=SIDES):
        for side, (step_x, step_y) in enumerate(SIDES):
            if (step_x, step_y) in sides:
                @pl.when(exists(step_x, step_y))
                def _():
                    remote(*make(step_x, step_y), phase, side).wait_send()

    def coarse_edge(step_x, step_y):
        from_x, to_x = edge(step_x, 1, kx)
        from_y, to_y = edge(step_y, 0, ky)
        from_x = pl.ds(from_x.start - 1, from_x.size)
        if step_y > 0:
            to_y = pl.ds(ky + 7, 1)
        return coarse_hbm.at[:, from_x, from_y], table.at[:, to_x, to_y]

    def cons_edge(step_x, step_y):
        from_x, to_x = edge(step_x, 1, nx)
        from_y, to_y = edge(step_y, OFF, ny)
        return (
            cons_hbm.at[pl.ds(from_x.start - 1, from_x.size), pl.ds(from_y.start - OFF, from_y.size)],
            cons.at[to_x, to_y],
        )

    def field_edge(phase):
        def make(step_x, step_y):
            from_x, to_x = edge(step_x, 1, nx)
            from_y, to_y = edge(step_y, OFF, ny)
            return fields.at[phase, :, from_x, from_y], fields.at[phase, :, to_x, to_y]
        return make

    last = DEGREE + 1
    start_all(coarse_edge, last)

    loads[1].wait()
    cols = ky * planes
    whole = agg[...]
    if cols & (cols - 1) == 0:
        row_a = lax.shift_right_logical(whole, cols.bit_length() - 1)
    else:
        row_a = lax.div(whole, cols)
    place = (row_a - (slab * kx - 1)) * (ky + 8)
    col_b = whole - row_a * cols - plane * ky
    place = (place + jnp.where(col_b < 0, ky + 7, col_b)).astype(jnp.float32)
    deep = (kx + 2) * (ky + 8)
    own = lax.broadcasted_iota(jnp.int32, (ny, ny), 0) == lax.broadcasted_iota(jnp.int32, (ny, ny), 1)
    slots = lax.broadcasted_iota(jnp.int32, (ny, deep), 1).astype(jnp.float32)
    picks = []
    for i in range(nx):
        column = jnp.sum(jnp.where(own, place[i:i + 1, :], 0.0), axis=1, keepdims=True)
        picks.append((column == slots).astype(jnp.bfloat16))
    pick = jnp.concatenate(picks, axis=0)
    loads[0].wait()
    loads[2].wait()
    wait_arrived(coarse_edge, last)
    for c in range(3):
        rest = table[c].reshape(deep, depth)
        moved = None
        for _ in range(3):
            part = rest.astype(jnp.bfloat16)
            rest = rest - part.astype(jnp.float32)
            piece = jnp.dot(pick, part, preferred_element_type=jnp.float32)
            moved = piece if moved is None else moved + piece
        fields[0, c, 1:nx + 1, OFF:OFF + ny, :] = start[c] + moved.reshape(nx, ny, depth)

    start_all(field_edge(0), 0)
    start_all(cons_edge, last + 1, LOW_SIDES)
    loads[4].wait()
    loads[5].wait()

    rows = 4
    rho = 1.0 / SIGMA
    for phase in range(DEGREE):
        wait_arrived(field_edge(phase), phase)
        if phase:
            rho_new = 1.0 / (2.0 * SIGMA - rho)
            keep, gain = rho_new * rho, 2.0 * rho_new / DELTA_C
            rho = rho_new

        def chunk(n, carry):
            c = n // (nx // rows)
            first = (n % (nx // rows)) * rows
            span = pl.ds(first, rows + 2)
            along_y = (
                fields[phase, c, span, pl.ds(OFF - 1, ny), :]
                + fields[phase, c, span, pl.ds(OFF, ny), :]
                + fields[phase, c, span, pl.ds(OFF + 1, ny), :]
            )
            boxed = box_z(along_y[:-2] + along_y[1:-1] + along_y[2:])
            centre = fields[phase, c, pl.ds(first + 1, rows), pl.ds(OFF, ny), :]
            here = pl.ds(first, rows)
            applied = (3.0 + shift[here]) * centre - boxed * (1.0 / 3.0)
            if phase == 0:
                left = load[c, here] - applied
                direction = left * (1.0 / THETA)
            else:
                left = resid[c, here] - applied
                direction = keep * centre + gain * left
            inner = (c, pl.ds(first + 1, rows), pl.ds(OFF, ny))
            if phase < DEGREE - 1:
                resid[c, here] = left
            else:
                for earlier in range(DEGREE):
                    direction = direction + fields[(earlier,) + inner]
            fields[(phase + 1,) + inner] = direction
            return carry

        lax.fori_loop(0, 3 * (nx // rows), chunk, 0)
        start_all(field_edge(phase + 1), phase + 1)

    loads[3].wait()
    wait_arrived(cons_edge, last + 1, LOW_SIDES)
    wait_arrived(field_edge(DEGREE), DEGREE)

    def finish():
        wait_sent(coarse_edge, last)
        wait_sent(cons_edge, last + 1, LOW_SIDES)
        for phase in range(DEGREE + 1):
            wait_sent(field_edge(phase), phase)

    return finish


def stresses(sizes, field, cons, disp_out, rec_out, ind_out):
    nx, ny, depth, kx, ky, slabs, planes = sizes
    first_x = lax.axis_index("slab") * nx
    first_y = lax.axis_index("plane") * ny
    total_x, total_y = nx * slabs, ny * planes
    tall = ny + 8
    lane = lax.broadcasted_iota(jnp.int32, (tall, depth), 1)
    node_y = first_y - 1 + lax.broadcasted_iota(jnp.int32, (tall, depth), 0)
    valid_y = (node_y >= 0) & (node_y <= total_y - 2) & (lane <= depth - 2)
    lane = lax.broadcasted_iota(jnp.int32, (ny, depth), 1)
    node_y = first_y + lax.broadcasted_iota(jnp.int32, (ny, depth), 0)

    def half(ok):
        return jnp.where(ok, 0.5, 1.0)

    scale_y = half((node_y >= 1) & (node_y <= total_y - 2)) * half((lane >= 1) & (lane <= depth - 2))

    for c in range(3):
        disp_out[c] = field[c, 1:nx + 1, OFF:OFF + ny, :]

    def corner_sums(c, i):
        low = field[c, i, pl.ds(OFF - 1, tall), :]
        high = field[c, i, pl.ds(OFF, tall), :]
        return low + high, high - low

    def element_row(i):
        grad_x, grad_y, grad_z = [], [], []
        for c in range(3):
            sum_a, diff_a = corner_sums(c, i)
            sum_b, diff_b = corner_sums(c, i + 1)
            gx, gy, gz = sum_b - sum_a, diff_a + diff_b, sum_a + sum_b
            grad_x.append(0.25 * (gx + next_z(gx)))
            grad_y.append(0.25 * (gy + next_z(gy)))
            grad_z.append(0.25 * (next_z(gz) - gz))
        exx, eyy, ezz = grad_x[0], grad_y[1], grad_z[2]
        exy = 0.5 * (grad_y[0] + grad_x[1])
        eyz = 0.5 * (grad_z[1] + grad_y[2])
        ezx = 0.5 * (grad_x[2] + grad_z[0])
        trace = exx + eyy + ezz
        third = trace * (1.0 / 3.0)
        sxx, syy, szz = exx - third, eyy - third, ezz - third
        equiv = (2.0 / 3.0) * (
            sxx * sxx + syy * syy + szz * szz + 2.0 * (exy * exy + eyz * eyz + ezx * ezx)
        )
        visc = cons[i, pl.ds(OFF - 1, tall), :] * jnp.exp(-0.425 * jnp.log(0.01 + 3.0 * equiv))
        twice = 2.0 * visc
        bulk = 4.0 * trace
        sig = [twice * sxx + bulk, twice * syy + bulk, twice * szz + bulk,
               twice * exy, twice * eyz, twice * ezx]
        norm_sq = (
            sig[0] * sig[0] + sig[1] * sig[1] + sig[2] * sig[2]
            + 2.0 * (sig[3] * sig[3] + sig[4] * sig[4] + sig[5] * sig[5])
        )
        node_x = first_x - 1 + i
        valid = valid_y & (node_x >= 0) & (node_x <= total_x - 2)
        summed = []
        for one in sig + [norm_sq]:
            one = jnp.where(valid, one, 0.0)
            one = one[0:ny] + one[1:ny + 1]
            summed.append(one + previous_z(one))
        return tuple(summed)

    def row(i, before):
        after = element_row(i)
        node_x = first_x + i - 1
        inside = ((node_x >= 1) & (node_x <= total_x - 2)).astype(jnp.float32)
        scale = scale_y * (1.0 - 0.5 * inside)
        total = [(a + b) * scale for a, b in zip(before, after)]
        rec = total[:6]
        for n in range(6):
            rec_out[n, i - 1] = rec[n]
        ind_out[i - 1] = total[6] - (
            rec[0] * rec[0] + rec[1] * rec[1] + rec[2] * rec[2]
            + 2.0 * (rec[3] * rec[3] + rec[4] * rec[4] + rec[5] * rec[5])
        )
        return after

    lax.fori_loop(1, nx + 1, row, element_row(0))


def whole_kernel(sizes, *refs):
    inputs, outs, scratch = refs[:6], refs[6:9], refs[9:]
    finish = smooth(sizes, inputs + scratch)
    fields, cons = scratch[6], scratch[5]
    stresses(sizes, fields.at[DEGREE], cons, *outs)
    finish()


def body(sizes, *blocks):
    nx, ny, depth, kx, ky, slabs, planes = sizes
    any_spec = pl.BlockSpec(memory_space=pl.ANY)
    vmem_spec = pl.BlockSpec(memory_space=pltpu.VMEM)
    f32 = jnp.float32
    return pl.pallas_call(
        functools.partial(whole_kernel, sizes),
        out_shape=(
            jax.ShapeDtypeStruct((3, nx, ny, depth), f32),
            jax.ShapeDtypeStruct((6, nx, ny, depth), f32),
            jax.ShapeDtypeStruct((nx, ny, depth), f32),
        ),
        in_specs=[any_spec] * 6,
        out_specs=(vmem_spec,) * 3,
        scratch_shapes=[
            pltpu.VMEM((3, nx, ny, depth), f32),
            pltpu.VMEM((3, nx, ny, depth), f32),
            pltpu.VMEM((nx, ny, depth), f32),
            pltpu.VMEM((3, kx + 2, ky + 8, depth), f32),
            pltpu.VMEM((nx, ny), jnp.int32),
            pltpu.VMEM((nx + 1, ny + 16, depth), f32),
            pltpu.VMEM((DEGREE + 1, 3, nx + 2, ny + 16, depth), f32),
            pltpu.VMEM((3, nx, ny, depth), f32),
            pltpu.SemaphoreType.DMA((6,)),
            pltpu.SemaphoreType.DMA((DEGREE + 3, len(SIDES))),
            pltpu.SemaphoreType.DMA((DEGREE + 3, len(SIDES))),
        ],
        compiler_params=pltpu.CompilerParams(
            collective_id=0, has_side_effects=True, vmem_limit_bytes=32 * 1024 * 1024
        ),
    )(*blocks)


def solution(mesh):
    in_specs = (
        P(None, "slab", "plane", None),
        P(None, "slab", "plane", None),
        P("slab", "plane", None),
        P(None, "slab", "plane", None),
        P("slab", "plane"),
        P("slab", "plane", None),
    )
    out_specs = (
        P(None, "slab", "plane", None),
        P(None, "slab", "plane", None),
        P("slab", "plane", None),
    )
    slabs, planes = mesh.shape["slab"], mesh.shape["plane"]

    def run(start_disp, load, shift, coarse, aggregate, consistency):
        sizes = (
            start_disp.shape[1] // slabs, start_disp.shape[2] // planes, start_disp.shape[3],
            coarse.shape[1] // slabs, coarse.shape[2] // planes, slabs, planes,
        )
        return jax.shard_map(
            functools.partial(body, sizes), mesh=mesh, in_specs=in_specs, out_specs=out_specs,
            check_vma=False,
        )(start_disp, load, shift, coarse, aggregate, consistency)

    return run
```

```python
import functools

import jax
import jax.numpy as jnp
from jax import lax
from jax.experimental import pallas as pl
from jax.experimental.pallas import tpu as pltpu
from jax.sharding import PartitionSpec as P

DEGREE = 4
THETA = 4.5
DELTA_C = 3.5
SIGMA = THETA / DELTA_C
MESH = pl.DeviceIdType.MESH
OFF = 8
SIDES = ((0, 1), (0, -1), (1, 1), (1, -1), (-1, 1), (-1, -1), (1, 0), (-1, 0))
VMEM_BYTES = 56 * 1024 * 1024
ROWS_OUT = 4
LOW_SIDES = ((0, 1), (1, 1), (1, 0))


def edge(step, first, count):
    if step > 0:
        return pl.ds(first + count - 1, 1), pl.ds(first - 1, 1)
    if step < 0:
        return pl.ds(first, 1), pl.ds(first + count, 1)
    return pl.ds(first, count), pl.ds(first, count)


def box_z(x):
    lane = lax.broadcasted_iota(jnp.int32, x.shape, x.ndim - 1)
    depth = x.shape[-1]
    below = jnp.where(lane == 0, 0.0, pltpu.roll(x, 1, x.ndim - 1))
    above = jnp.where(lane == depth - 1, 0.0, pltpu.roll(x, depth - 1, x.ndim - 1))
    return x + below + above


def next_z(x):
    return pltpu.roll(x, x.shape[-1] - 1, x.ndim - 1)


def previous_z(x):
    return pltpu.roll(x, 1, x.ndim - 1)


def smooth(sizes, *refs):
    nx, ny, depth, kx, ky, slabs, planes = sizes
    (start_hbm, load_hbm, shift_hbm, coarse_hbm, agg_hbm, cons_hbm, final, cons,
     start, load, shift, table, agg, earlier, resid, in_sem, send_sem, recv_sem) = refs
    fields = [earlier.at[n] for n in range(DEGREE)] + [final]
    slab = lax.axis_index("slab")
    plane = lax.axis_index("plane")

    def exists(step_x, step_y):
        x, y = slab + step_x, plane + step_y
        return (x >= 0) & (x < slabs) & (y >= 0) & (y < planes)

    loads = [
        pltpu.make_async_copy(coarse_hbm, table.at[:, pl.ds(1, kx), pl.ds(0, ky)], in_sem.at[0]),
        pltpu.make_async_copy(agg_hbm, agg, in_sem.at[1]),
        pltpu.make_async_copy(start_hbm, start, in_sem.at[2]),
        pltpu.make_async_copy(cons_hbm, cons.at[pl.ds(1, nx), pl.ds(OFF, ny)], in_sem.at[3]),
        pltpu.make_async_copy(load_hbm, load, in_sem.at[4]),
        pltpu.make_async_copy(shift_hbm, shift, in_sem.at[5]),
    ]
    for copy in loads:
        copy.start()

    zero_table = jnp.zeros((3, 8, depth), jnp.float32)
    for a in range(kx + 2):
        table[:, a, ky:ky + 8, :] = zero_table
    table[:, 0, 0:ky, :] = zero_table
    table[:, kx + 1, 0:ky, :] = zero_table

    barrier = pltpu.get_barrier_semaphore()
    for step_x, step_y in SIDES:
        @pl.when(exists(step_x, step_y))
        def _():
            pl.semaphore_signal(
                barrier, inc=1, device_id=(slab + step_x, plane + step_y), device_id_type=MESH
            )

    zero_row = jnp.zeros((nx + 2, depth), jnp.float32)
    for step_x, step_y in ((0, 1), (0, -1), (1, 0), (-1, 0)):
        @pl.when(jnp.logical_not(exists(-step_x, -step_y)))
        def _():
            for phase in range(DEGREE + 1):
                for c in range(3):
                    if step_y:
                        row = OFF - 1 if step_y > 0 else OFF + ny
                        for i in range(nx + 2):
                            fields[phase][c, i, row:row + 1, :] = zero_row[0:1]
                    else:
                        i = 0 if step_x > 0 else nx + 1
                        for at in range(0, ny + 16, 8):
                            fields[phase][c, i, at:at + 8, :] = zero_row[0:8]

    near_x = 1 + (slab > 0).astype(jnp.int32) + (slab < slabs - 1).astype(jnp.int32)
    near_y = 1 + (plane > 0).astype(jnp.int32) + (plane < planes - 1).astype(jnp.int32)
    pl.semaphore_wait(barrier, near_x * near_y - 1)

    def remote(source, target, phase, side):
        step_x, step_y = SIDES[side]
        return pltpu.make_async_remote_copy(
            src_ref=source, dst_ref=target,
            send_sem=send_sem.at[phase, side], recv_sem=recv_sem.at[phase, side],
            device_id=(slab + step_x, plane + step_y), device_id_type=MESH,
        )

    def start_all(make, phase, sides=SIDES):
        for side, (step_x, step_y) in enumerate(SIDES):
            if (step_x, step_y) in sides:
                @pl.when(exists(step_x, step_y))
                def _():
                    remote(*make(step_x, step_y), phase, side).start()

    def wait_arrived(make, phase, sides=SIDES):
        for side, (step_x, step_y) in enumerate(SIDES):
            if (step_x, step_y) in sides:
                @pl.when(exists(-step_x, -step_y))
                def _():
                    remote(*make(step_x, step_y), phase, side).wait_recv()

    def wait_sent(make, phase, sides=SIDES):
        for side, (step_x, step_y) in enumerate(SIDES):
            if (step_x, step_y) in sides:
                @pl.when(exists(step_x, step_y))
                def _():
                    remote(*make(step_x, step_y), phase, side).wait_send()

    def coarse_edge(step_x, step_y):
        from_x, to_x = edge(step_x, 1, kx)
        from_y, to_y = edge(step_y, 0, ky)
        from_x = pl.ds(from_x.start - 1, from_x.size)
        if step_y > 0:
            to_y = pl.ds(ky + 7, 1)
        return coarse_hbm.at[:, from_x, from_y], table.at[:, to_x, to_y]

    def cons_edge(step_x, step_y):
        from_x, to_x = edge(step_x, 1, nx)
        from_y, to_y = edge(step_y, OFF, ny)
        return (
            cons_hbm.at[pl.ds(from_x.start - 1, from_x.size), pl.ds(from_y.start - OFF, from_y.size)],
            cons.at[to_x, to_y],
        )

    def field_edge(phase):
        def make(step_x, step_y):
            from_x, to_x = edge(step_x, 1, nx)
            from_y, to_y = edge(step_y, OFF, ny)
            return fields[phase].at[:, from_x, from_y], fields[phase].at[:, to_x, to_y]
        return make

    last = DEGREE + 1
    start_all(coarse_edge, last)

    loads[1].wait()
    cols = ky * planes
    whole = agg[...]
    if cols & (cols - 1) == 0:
        row_a = lax.shift_right_logical(whole, cols.bit_length() - 1)
    else:
        row_a = lax.div(whole, cols)
    place = (row_a - (slab * kx - 1)) * (ky + 8)
    col_b = whole - row_a * cols - plane * ky
    place = (place + jnp.where(col_b < 0, ky + 7, col_b)).astype(jnp.float32)
    deep = (kx + 2) * (ky + 8)
    own = lax.broadcasted_iota(jnp.int32, (ny, ny), 0) == lax.broadcasted_iota(jnp.int32, (ny, ny), 1)
    slots = lax.broadcasted_iota(jnp.int32, (ny, deep), 1).astype(jnp.float32)
    picks = []
    for i in range(nx):
        column = jnp.sum(jnp.where(own, place[i:i + 1, :], 0.0), axis=1, keepdims=True)
        picks.append((column == slots).astype(jnp.bfloat16))
    pick = jnp.concatenate(picks, axis=0)
    loads[0].wait()
    loads[2].wait()
    wait_arrived(coarse_edge, last)
    for c in range(3):
        rest = table[c].reshape(deep, depth)
        moved = None
        for _ in range(3):
            part = rest.astype(jnp.bfloat16)
            rest = rest - part.astype(jnp.float32)
            piece = jnp.dot(pick, part, preferred_element_type=jnp.float32)
            moved = piece if moved is None else moved + piece
        fields[0][c, 1:nx + 1, OFF:OFF + ny, :] = start[c] + moved.reshape(nx, ny, depth)

    start_all(field_edge(0), 0)
    start_all(cons_edge, last + 1, LOW_SIDES)
    loads[4].wait()
    loads[5].wait()

    rows = 4
    rho = 1.0 / SIGMA
    for phase in range(DEGREE):
        wait_arrived(field_edge(phase), phase)
        if phase:
            rho_new = 1.0 / (2.0 * SIGMA - rho)
            keep, gain = rho_new * rho, 2.0 * rho_new / DELTA_C
            rho = rho_new

        def chunk(at, carry):
            c = at // (nx // rows)
            first = (at % (nx // rows)) * rows
            span = pl.ds(first, rows + 2)
            along_y = (
                fields[phase][c, span, pl.ds(OFF - 1, ny), :]
                + fields[phase][c, span, pl.ds(OFF, ny), :]
                + fields[phase][c, span, pl.ds(OFF + 1, ny), :]
            )
            boxed = box_z(along_y[:-2] + along_y[1:-1] + along_y[2:])
            centre = fields[phase][c, pl.ds(first + 1, rows), pl.ds(OFF, ny), :]
            here = pl.ds(first, rows)
            applied = (3.0 + shift[here]) * centre - boxed * (1.0 / 3.0)
            if phase == 0:
                left = load[c, here] - applied
                direction = left * (1.0 / THETA)
            else:
                left = resid[c, here] - applied
                direction = keep * centre + gain * left
            inner = (c, pl.ds(first + 1, rows), pl.ds(OFF, ny))
            if phase < DEGREE - 1:
                resid[c, here] = left
            else:
                for n in range(DEGREE):
                    direction = direction + fields[n][inner]
            fields[phase + 1][inner] = direction
            return carry

        lax.fori_loop(0, 3 * (nx // rows), chunk, 0)
        start_all(field_edge(phase + 1), phase + 1)

    loads[3].wait()
    wait_arrived(cons_edge, last + 1, LOW_SIDES)
    wait_arrived(field_edge(DEGREE), DEGREE)

    wait_sent(coarse_edge, last)
    wait_sent(cons_edge, last + 1, LOW_SIDES)
    for phase in range(DEGREE + 1):
        wait_sent(field_edge(phase), phase)


def stresses(sizes, field, cons, disp_out, rec_out, ind_out, rec, ind, out_sem):
    nx, ny, depth, kx, ky, slabs, planes = sizes
    first_x = lax.axis_index("slab") * nx
    first_y = lax.axis_index("plane") * ny
    total_x, total_y = nx * slabs, ny * planes
    tall = ny + 8
    lane = lax.broadcasted_iota(jnp.int32, (tall, depth), 1)
    node_y = first_y - 1 + lax.broadcasted_iota(jnp.int32, (tall, depth), 0)
    valid_y = (node_y >= 0) & (node_y <= total_y - 2) & (lane <= depth - 2)
    lane = lax.broadcasted_iota(jnp.int32, (ny, depth), 1)
    node_y = first_y + lax.broadcasted_iota(jnp.int32, (ny, depth), 0)

    def half(ok):
        return jnp.where(ok, 0.5, 1.0)

    scale_y = half((node_y >= 1) & (node_y <= total_y - 2)) * half((lane >= 1) & (lane <= depth - 2))

    inner = field.at[:, pl.ds(1, nx), pl.ds(OFF, ny)]
    whole = pltpu.make_async_copy(inner, disp_out, out_sem.at[0])
    whole.start()

    def part(n):
        here = pl.ds(n * ROWS_OUT, ROWS_OUT)
        return (
            pltpu.make_async_copy(rec.at[:, here], rec_out.at[:, here], out_sem.at[1 + 2 * n]),
            pltpu.make_async_copy(ind.at[here], ind_out.at[here], out_sem.at[2 + 2 * n]),
        )

    def corner_sums(c, i):
        low = field[c, i, pl.ds(OFF - 1, tall), :]
        high = field[c, i, pl.ds(OFF, tall), :]
        return low + high, high - low

    def element_row(i):
        grad_x, grad_y, grad_z = [], [], []
        for c in range(3):
            sum_a, diff_a = corner_sums(c, i)
            sum_b, diff_b = corner_sums(c, i + 1)
            gx, gy, gz = sum_b - sum_a, diff_a + diff_b, sum_a + sum_b
            grad_x.append(0.25 * (gx + next_z(gx)))
            grad_y.append(0.25 * (gy + next_z(gy)))
            grad_z.append(0.25 * (next_z(gz) - gz))
        exx, eyy, ezz = grad_x[0], grad_y[1], grad_z[2]
        exy = 0.5 * (grad_y[0] + grad_x[1])
        eyz = 0.5 * (grad_z[1] + grad_y[2])
        ezx = 0.5 * (grad_x[2] + grad_z[0])
        trace = exx + eyy + ezz
        third = trace * (1.0 / 3.0)
        sxx, syy, szz = exx - third, eyy - third, ezz - third
        equiv = (2.0 / 3.0) * (
            sxx * sxx + syy * syy + szz * szz + 2.0 * (exy * exy + eyz * eyz + ezx * ezx)
        )
        visc = cons[i, pl.ds(OFF - 1, tall), :] * jnp.exp(-0.425 * jnp.log(0.01 + 3.0 * equiv))
        twice = 2.0 * visc
        bulk = 4.0 * trace
        sig = [twice * sxx + bulk, twice * syy + bulk, twice * szz + bulk,
               twice * exy, twice * eyz, twice * ezx]
        norm_sq = (
            sig[0] * sig[0] + sig[1] * sig[1] + sig[2] * sig[2]
            + 2.0 * (sig[3] * sig[3] + sig[4] * sig[4] + sig[5] * sig[5])
        )
        node_x = first_x - 1 + i
        valid = valid_y & (node_x >= 0) & (node_x <= total_x - 2)
        summed = []
        for one in sig + [norm_sq]:
            one = jnp.where(valid, one, 0.0)
            one = one[0:ny] + one[1:ny + 1]
            summed.append(one + previous_z(one))
        return tuple(summed)

    def row(i, before):
        after = element_row(i)
        node_x = first_x + i - 1
        inside = ((node_x >= 1) & (node_x <= total_x - 2)).astype(jnp.float32)
        scale = scale_y * (1.0 - 0.5 * inside)
        total = [(a + b) * scale for a, b in zip(before, after)]
        for n in range(6):
            rec[n, i - 1] = total[n]
        ind[i - 1] = total[6] - (
            total[0] * total[0] + total[1] * total[1] + total[2] * total[2]
            + 2.0 * (total[3] * total[3] + total[4] * total[4] + total[5] * total[5])
        )
        return after

    carry = element_row(0)
    for n in range(nx // ROWS_OUT):
        carry = lax.fori_loop(1 + n * ROWS_OUT, 1 + (n + 1) * ROWS_OUT, row, carry)
        for copy in part(n):
            copy.start()
    whole.wait()
    for n in range(nx // ROWS_OUT):
        for copy in part(n):
            copy.wait()


def body(sizes, *blocks):
    nx, ny, depth, kx, ky, slabs, planes = sizes
    hbm = pl.BlockSpec(memory_space=pltpu.HBM)
    vmem = pl.BlockSpec(memory_space=pltpu.VMEM)
    f32 = jnp.float32
    padded = (
        jax.ShapeDtypeStruct((3, nx + 2, ny + 16, depth), f32),
        jax.ShapeDtypeStruct((nx + 1, ny + 16, depth), f32),
    )
    field, cons = pl.pallas_call(
        functools.partial(smooth, sizes),
        out_shape=padded,
        in_specs=[hbm] * 6,
        out_specs=(vmem,) * 2,
        scratch_shapes=[
            pltpu.VMEM((3, nx, ny, depth), f32),
            pltpu.VMEM((3, nx, ny, depth), f32),
            pltpu.VMEM((nx, ny, depth), f32),
            pltpu.VMEM((3, kx + 2, ky + 8, depth), f32),
            pltpu.VMEM((nx, ny), jnp.int32),
            pltpu.VMEM((DEGREE, 3, nx + 2, ny + 16, depth), f32),
            pltpu.VMEM((3, nx, ny, depth), f32),
            pltpu.SemaphoreType.DMA((6,)),
            pltpu.SemaphoreType.DMA((DEGREE + 3, len(SIDES))),
            pltpu.SemaphoreType.DMA((DEGREE + 3, len(SIDES))),
        ],
        compiler_params=pltpu.CompilerParams(
            collective_id=0, has_side_effects=True, vmem_limit_bytes=VMEM_BYTES
        ),
    )(*blocks)
    outs = (
        jax.ShapeDtypeStruct((3, nx, ny, depth), f32),
        jax.ShapeDtypeStruct((6, nx, ny, depth), f32),
        jax.ShapeDtypeStruct((nx, ny, depth), f32),
    )
    return pl.pallas_call(
        functools.partial(stresses, sizes),
        out_shape=outs,
        in_specs=[vmem] * 2,
        out_specs=(hbm,) * 3,
        scratch_shapes=[
            pltpu.VMEM(outs[1].shape, f32),
            pltpu.VMEM(outs[2].shape, f32),
            pltpu.SemaphoreType.DMA((1 + 2 * (nx // ROWS_OUT),)),
        ],
        compiler_params=pltpu.CompilerParams(vmem_limit_bytes=VMEM_BYTES),
    )(field, cons)


def solution(mesh):
    in_specs = (
        P(None, "slab", "plane", None),
        P(None, "slab", "plane", None),
        P("slab", "plane", None),
        P(None, "slab", "plane", None),
        P("slab", "plane"),
        P("slab", "plane", None),
    )
    out_specs = (
        P(None, "slab", "plane", None),
        P(None, "slab", "plane", None),
        P("slab", "plane", None),
    )
    slabs, planes = mesh.shape["slab"], mesh.shape["plane"]

    def run(start_disp, load, shift, coarse, aggregate, consistency):
        sizes = (
            start_disp.shape[1] // slabs, start_disp.shape[2] // planes, start_disp.shape[3],
            coarse.shape[1] // slabs, coarse.shape[2] // planes, slabs, planes,
        )
        return jax.shard_map(
            functools.partial(body, sizes), mesh=mesh, in_specs=in_specs, out_specs=out_specs,
            check_vma=False,
        )(start_disp, load, shift, coarse, aggregate, consistency)

    return run
```

```python
import functools

import jax
import jax.numpy as jnp
from jax import lax
from jax.experimental import pallas as pl
from jax.experimental.pallas import tpu as pltpu
from jax.sharding import PartitionSpec as P

DEGREE = 4
THETA = 4.5
DELTA_C = 3.5
SIGMA = THETA / DELTA_C
MESH = pl.DeviceIdType.MESH
OFF = 8
SIDES = ((0, 1), (0, -1), (1, 1), (1, -1), (-1, 1), (-1, -1), (1, 0), (-1, 0))
VMEM_BYTES = 56 * 1024 * 1024
ROWS_OUT = 4
LOW_SIDES = ((0, 1), (1, 1), (1, 0))


def edge(step, first, count):
    if step > 0:
        return pl.ds(first + count - 1, 1), pl.ds(first - 1, 1)
    if step < 0:
        return pl.ds(first, 1), pl.ds(first + count, 1)
    return pl.ds(first, count), pl.ds(first, count)


def box_z(x):
    lane = lax.broadcasted_iota(jnp.int32, x.shape, x.ndim - 1)
    depth = x.shape[-1]
    below = jnp.where(lane == 0, 0.0, pltpu.roll(x, 1, x.ndim - 1))
    above = jnp.where(lane == depth - 1, 0.0, pltpu.roll(x, depth - 1, x.ndim - 1))
    return x + below + above


def next_z(x):
    return pltpu.roll(x, x.shape[-1] - 1, x.ndim - 1)


def previous_z(x):
    return pltpu.roll(x, 1, x.ndim - 1)


def smooth(sizes, *refs):
    nx, ny, depth, kx, ky, slabs, planes = sizes
    (start_hbm, load_hbm, shift_hbm, coarse_hbm, agg_hbm, cons_hbm, final, cons,
     start, load, shift, table, agg, earlier, resid, in_sem, send_sem, recv_sem) = refs
    fields = [earlier.at[n] for n in range(DEGREE)] + [final]
    slab = lax.axis_index("slab")
    plane = lax.axis_index("plane")

    def exists(step_x, step_y):
        x, y = slab + step_x, plane + step_y
        return (x >= 0) & (x < slabs) & (y >= 0) & (y < planes)

    loads = [
        pltpu.make_async_copy(coarse_hbm, table.at[:, pl.ds(1, kx), pl.ds(0, ky)], in_sem.at[0]),
        pltpu.make_async_copy(agg_hbm, agg, in_sem.at[1]),
        pltpu.make_async_copy(start_hbm, start, in_sem.at[2]),
        pltpu.make_async_copy(cons_hbm, cons.at[pl.ds(1, nx), pl.ds(OFF, ny)], in_sem.at[3]),
        pltpu.make_async_copy(load_hbm, load, in_sem.at[4]),
        pltpu.make_async_copy(shift_hbm, shift, in_sem.at[5]),
    ]
    for copy in loads:
        copy.start()

    zero_table = jnp.zeros((3, 8, depth), jnp.float32)
    for a in range(kx + 2):
        table[:, a, ky:ky + 8, :] = zero_table
    table[:, 0, 0:ky, :] = zero_table
    table[:, kx + 1, 0:ky, :] = zero_table

    barrier = pltpu.get_barrier_semaphore()
    for step_x, step_y in SIDES:
        @pl.when(exists(step_x, step_y))
        def _():
            pl.semaphore_signal(
                barrier, inc=1, device_id=(slab + step_x, plane + step_y), device_id_type=MESH
            )

    zero_row = jnp.zeros((nx + 2, depth), jnp.float32)
    for step_x, step_y in ((0, 1), (0, -1), (1, 0), (-1, 0)):
        @pl.when(jnp.logical_not(exists(-step_x, -step_y)))
        def _():
            for phase in range(DEGREE + 1):
                for c in range(3):
                    if step_y:
                        row = OFF - 1 if step_y > 0 else OFF + ny
                        for i in range(nx + 2):
                            fields[phase][c, i, row:row + 1, :] = zero_row[0:1]
                    else:
                        i = 0 if step_x > 0 else nx + 1
                        for at in range(0, ny + 16, 8):
                            fields[phase][c, i, at:at + 8, :] = zero_row[0:8]

    near_x = 1 + (slab > 0).astype(jnp.int32) + (slab < slabs - 1).astype(jnp.int32)
    near_y = 1 + (plane > 0).astype(jnp.int32) + (plane < planes - 1).astype(jnp.int32)
    pl.semaphore_wait(barrier, near_x * near_y - 1)

    def remote(source, target, phase, side):
        step_x, step_y = SIDES[side]
        return pltpu.make_async_remote_copy(
            src_ref=source, dst_ref=target,
            send_sem=send_sem.at[phase, side], recv_sem=recv_sem.at[phase, side],
            device_id=(slab + step_x, plane + step_y), device_id_type=MESH,
        )

    def start_all(make, phase, sides=SIDES):
        for side, (step_x, step_y) in enumerate(SIDES):
            if (step_x, step_y) in sides:
                @pl.when(exists(step_x, step_y))
                def _():
                    remote(*make(step_x, step_y), phase, side).start()

    def wait_arrived(make, phase, sides=SIDES):
        for side, (step_x, step_y) in enumerate(SIDES):
            if (step_x, step_y) in sides:
                @pl.when(exists(-step_x, -step_y))
                def _():
                    remote(*make(step_x, step_y), phase, side).wait_recv()

    def wait_sent(make, phase, sides=SIDES):
        for side, (step_x, step_y) in enumerate(SIDES):
            if (step_x, step_y) in sides:
                @pl.when(exists(step_x, step_y))
                def _():
                    remote(*make(step_x, step_y), phase, side).wait_send()

    def coarse_edge(step_x, step_y):
        from_x, to_x = edge(step_x, 1, kx)
        from_y, to_y = edge(step_y, 0, ky)
        from_x = pl.ds(from_x.start - 1, from_x.size)
        if step_y > 0:
            to_y = pl.ds(ky + 7, 1)
        return coarse_hbm.at[:, from_x, from_y], table.at[:, to_x, to_y]

    def cons_edge(step_x, step_y):
        from_x, to_x = edge(step_x, 1, nx)
        from_y, to_y = edge(step_y, OFF, ny)
        return (
            cons_hbm.at[pl.ds(from_x.start - 1, from_x.size), pl.ds(from_y.start - OFF, from_y.size)],
            cons.at[to_x, to_y],
        )

    def field_edge(phase):
        def make(step_x, step_y):
            from_x, to_x = edge(step_x, 1, nx)
            from_y, to_y = edge(step_y, OFF, ny)
            return fields[phase].at[:, from_x, from_y], fields[phase].at[:, to_x, to_y]
        return make

    last = DEGREE + 1
    start_all(coarse_edge, last)

    loads[1].wait()
    cols = ky * planes
    whole = agg[...]
    if cols & (cols - 1) == 0:
        row_a = lax.shift_right_logical(whole, cols.bit_length() - 1)
    else:
        row_a = lax.div(whole, cols)
    place = (row_a - (slab * kx - 1)) * (ky + 8)
    col_b = whole - row_a * cols - plane * ky
    place = (place + jnp.where(col_b < 0, ky + 7, col_b)).astype(jnp.float32)
    deep = (kx + 2) * (ky + 8)
    own = lax.broadcasted_iota(jnp.int32, (ny, ny), 0) == lax.broadcasted_iota(jnp.int32, (ny, ny), 1)
    slots = lax.broadcasted_iota(jnp.int32, (ny, deep), 1).astype(jnp.float32)
    picks = []
    for i in range(nx):
        column = jnp.sum(jnp.where(own, place[i:i + 1, :], 0.0), axis=1, keepdims=True)
        picks.append((column == slots).astype(jnp.bfloat16))
    pick = jnp.concatenate(picks, axis=0)
    loads[0].wait()
    loads[2].wait()
    wait_arrived(coarse_edge, last)
    for c in range(3):
        rest = table[c].reshape(deep, depth)
        moved = None
        for _ in range(3):
            part = rest.astype(jnp.bfloat16)
            rest = rest - part.astype(jnp.float32)
            piece = jnp.dot(pick, part, preferred_element_type=jnp.float32)
            moved = piece if moved is None else moved + piece
        fields[0][c, 1:nx + 1, OFF:OFF + ny, :] = start[c] + moved.reshape(nx, ny, depth)

    start_all(field_edge(0), 0)
    start_all(cons_edge, last + 1, LOW_SIDES)
    loads[4].wait()
    loads[5].wait()

    rows = nx
    rho = 1.0 / SIGMA
    for phase in range(DEGREE):
        wait_arrived(field_edge(phase), phase)
        if phase:
            rho_new = 1.0 / (2.0 * SIGMA - rho)
            keep, gain = rho_new * rho, 2.0 * rho_new / DELTA_C
            rho = rho_new

        def chunk(at, carry):
            c = at // (nx // rows)
            first = (at % (nx // rows)) * rows
            span = pl.ds(first, rows + 2)
            along_y = (
                fields[phase][c, span, pl.ds(OFF - 1, ny), :]
                + fields[phase][c, span, pl.ds(OFF, ny), :]
                + fields[phase][c, span, pl.ds(OFF + 1, ny), :]
            )
            boxed = box_z(along_y[:-2] + along_y[1:-1] + along_y[2:])
            centre = fields[phase][c, pl.ds(first + 1, rows), pl.ds(OFF, ny), :]
            here = pl.ds(first, rows)
            applied = (3.0 + shift[here]) * centre - boxed * (1.0 / 3.0)
            if phase == 0:
                left = load[c, here] - applied
                direction = left * (1.0 / THETA)
            else:
                left = resid[c, here] - applied
                direction = keep * centre + gain * left
            inner = (c, pl.ds(first + 1, rows), pl.ds(OFF, ny))
            if phase < DEGREE - 1:
                resid[c, here] = left
            else:
                for n in range(DEGREE):
                    direction = direction + fields[n][inner]
            fields[phase + 1][inner] = direction
            return carry

        lax.fori_loop(0, 3 * (nx // rows), chunk, 0)
        start_all(field_edge(phase + 1), phase + 1)

    loads[3].wait()
    wait_arrived(cons_edge, last + 1, LOW_SIDES)
    wait_arrived(field_edge(DEGREE), DEGREE)

    wait_sent(coarse_edge, last)
    wait_sent(cons_edge, last + 1, LOW_SIDES)
    for phase in range(DEGREE + 1):
        wait_sent(field_edge(phase), phase)


def stresses(sizes, field, cons, disp_out, rec_out, ind_out, rec, ind, out_sem):
    nx, ny, depth, kx, ky, slabs, planes = sizes
    first_x = lax.axis_index("slab") * nx
    first_y = lax.axis_index("plane") * ny
    total_x, total_y = nx * slabs, ny * planes
    tall = ny + 8
    lane = lax.broadcasted_iota(jnp.int32, (tall, depth), 1)
    node_y = first_y - 1 + lax.broadcasted_iota(jnp.int32, (tall, depth), 0)
    valid_y = (node_y >= 0) & (node_y <= total_y - 2) & (lane <= depth - 2)
    lane = lax.broadcasted_iota(jnp.int32, (ny, depth), 1)
    node_y = first_y + lax.broadcasted_iota(jnp.int32, (ny, depth), 0)

    def half(ok):
        return jnp.where(ok, 0.5, 1.0)

    scale_y = half((node_y >= 1) & (node_y <= total_y - 2)) * half((lane >= 1) & (lane <= depth - 2))

    inner = field.at[:, pl.ds(1, nx), pl.ds(OFF, ny)]
    whole = pltpu.make_async_copy(inner, disp_out, out_sem.at[0])
    whole.start()

    def part(n):
        here = pl.ds(n * ROWS_OUT, ROWS_OUT)
        return (
            pltpu.make_async_copy(rec.at[:, here], rec_out.at[:, here], out_sem.at[1 + 2 * n]),
            pltpu.make_async_copy(ind.at[here], ind_out.at[here], out_sem.at[2 + 2 * n]),
        )

    def corner_sums(c, i):
        low = field[c, i, pl.ds(OFF - 1, tall), :]
        high = field[c, i, pl.ds(OFF, tall), :]
        return low + high, high - low

    def element_row(i):
        grad_x, grad_y, grad_z = [], [], []
        for c in range(3):
            sum_a, diff_a = corner_sums(c, i)
            sum_b, diff_b = corner_sums(c, i + 1)
            gx, gy, gz = sum_b - sum_a, diff_a + diff_b, sum_a + sum_b
            grad_x.append(0.25 * (gx + next_z(gx)))
            grad_y.append(0.25 * (gy + next_z(gy)))
            grad_z.append(0.25 * (next_z(gz) - gz))
        exx, eyy, ezz = grad_x[0], grad_y[1], grad_z[2]
        exy = 0.5 * (grad_y[0] + grad_x[1])
        eyz = 0.5 * (grad_z[1] + grad_y[2])
        ezx = 0.5 * (grad_x[2] + grad_z[0])
        trace = exx + eyy + ezz
        third = trace * (1.0 / 3.0)
        sxx, syy, szz = exx - third, eyy - third, ezz - third
        equiv = (2.0 / 3.0) * (
            sxx * sxx + syy * syy + szz * szz + 2.0 * (exy * exy + eyz * eyz + ezx * ezx)
        )
        visc = cons[i, pl.ds(OFF - 1, tall), :] * jnp.exp(-0.425 * jnp.log(0.01 + 3.0 * equiv))
        twice = 2.0 * visc
        bulk = 4.0 * trace
        sig = [twice * sxx + bulk, twice * syy + bulk, twice * szz + bulk,
               twice * exy, twice * eyz, twice * ezx]
        norm_sq = (
            sig[0] * sig[0] + sig[1] * sig[1] + sig[2] * sig[2]
            + 2.0 * (sig[3] * sig[3] + sig[4] * sig[4] + sig[5] * sig[5])
        )
        node_x = first_x - 1 + i
        valid = valid_y & (node_x >= 0) & (node_x <= total_x - 2)
        summed = []
        for one in sig + [norm_sq]:
            one = jnp.where(valid, one, 0.0)
            one = one[0:ny] + one[1:ny + 1]
            summed.append(one + previous_z(one))
        return tuple(summed)

    def row(i, before):
        after = element_row(i)
        node_x = first_x + i - 1
        inside = ((node_x >= 1) & (node_x <= total_x - 2)).astype(jnp.float32)
        scale = scale_y * (1.0 - 0.5 * inside)
        total = [(a + b) * scale for a, b in zip(before, after)]
        for n in range(6):
            rec[n, i - 1] = total[n]
        ind[i - 1] = total[6] - (
            total[0] * total[0] + total[1] * total[1] + total[2] * total[2]
            + 2.0 * (total[3] * total[3] + total[4] * total[4] + total[5] * total[5])
        )
        return after

    carry = element_row(0)
    for n in range(nx // ROWS_OUT):
        carry = lax.fori_loop(1 + n * ROWS_OUT, 1 + (n + 1) * ROWS_OUT, row, carry, unroll=True)
        for copy in part(n):
            copy.start()
    whole.wait()
    for n in range(nx // ROWS_OUT):
        for copy in part(n):
            copy.wait()


def body(sizes, *blocks):
    nx, ny, depth, kx, ky, slabs, planes = sizes
    hbm = pl.BlockSpec(memory_space=pltpu.HBM)
    vmem = pl.BlockSpec(memory_space=pltpu.VMEM)
    f32 = jnp.float32
    padded = (
        jax.ShapeDtypeStruct((3, nx + 2, ny + 16, depth), f32),
        jax.ShapeDtypeStruct((nx + 1, ny + 16, depth), f32),
    )
    field, cons = pl.pallas_call(
        functools.partial(smooth, sizes),
        out_shape=padded,
        in_specs=[hbm] * 6,
        out_specs=(vmem,) * 2,
        scratch_shapes=[
            pltpu.VMEM((3, nx, ny, depth), f32),
            pltpu.VMEM((3, nx, ny, depth), f32),
            pltpu.VMEM((nx, ny, depth), f32),
            pltpu.VMEM((3, kx + 2, ky + 8, depth), f32),
            pltpu.VMEM((nx, ny), jnp.int32),
            pltpu.VMEM((DEGREE, 3, nx + 2, ny + 16, depth), f32),
            pltpu.VMEM((3, nx, ny, depth), f32),
            pltpu.SemaphoreType.DMA((6,)),
            pltpu.SemaphoreType.DMA((DEGREE + 3, len(SIDES))),
            pltpu.SemaphoreType.DMA((DEGREE + 3, len(SIDES))),
        ],
        compiler_params=pltpu.CompilerParams(
            collective_id=0, has_side_effects=True, vmem_limit_bytes=VMEM_BYTES
        ),
    )(*blocks)
    outs = (
        jax.ShapeDtypeStruct((3, nx, ny, depth), f32),
        jax.ShapeDtypeStruct((6, nx, ny, depth), f32),
        jax.ShapeDtypeStruct((nx, ny, depth), f32),
    )
    return pl.pallas_call(
        functools.partial(stresses, sizes),
        out_shape=outs,
        in_specs=[vmem] * 2,
        out_specs=(hbm,) * 3,
        scratch_shapes=[
            pltpu.VMEM(outs[1].shape, f32),
            pltpu.VMEM(outs[2].shape, f32),
            pltpu.SemaphoreType.DMA((1 + 2 * (nx // ROWS_OUT),)),
        ],
        compiler_params=pltpu.CompilerParams(vmem_limit_bytes=VMEM_BYTES),
    )(field, cons)


def solution(mesh):
    in_specs = (
        P(None, "slab", "plane", None),
        P(None, "slab", "plane", None),
        P("slab", "plane", None),
        P(None, "slab", "plane", None),
        P("slab", "plane"),
        P("slab", "plane", None),
    )
    out_specs = (
        P(None, "slab", "plane", None),
        P(None, "slab", "plane", None),
        P("slab", "plane", None),
    )
    slabs, planes = mesh.shape["slab"], mesh.shape["plane"]

    def run(start_disp, load, shift, coarse, aggregate, consistency):
        sizes = (
            start_disp.shape[1] // slabs, start_disp.shape[2] // planes, start_disp.shape[3],
            coarse.shape[1] // slabs, coarse.shape[2] // planes, slabs, planes,
        )
        return jax.shard_map(
            functools.partial(body, sizes), mesh=mesh, in_specs=in_specs, out_specs=out_specs,
            check_vma=False,
        )(start_disp, load, shift, coarse, aggregate, consistency)

    return run
```

```python
import functools

import jax
import jax.numpy as jnp
from jax import lax
from jax.experimental import pallas as pl
from jax.experimental.pallas import tpu as pltpu
from jax.sharding import PartitionSpec as P

DEGREE = 4
THETA = 4.5
DELTA_C = 3.5
SIGMA = THETA / DELTA_C
MESH = pl.DeviceIdType.MESH
OFF = 8
SIDES = ((0, 1), (0, -1), (1, 1), (1, -1), (-1, 1), (-1, -1), (1, 0), (-1, 0))
VMEM_BYTES = 56 * 1024 * 1024
ROWS_OUT = 4
LOW_SIDES = ((0, 1), (1, 1), (1, 0))


def edge(step, first, count):
    if step > 0:
        return pl.ds(first + count - 1, 1), pl.ds(first - 1, 1)
    if step < 0:
        return pl.ds(first, 1), pl.ds(first + count, 1)
    return pl.ds(first, count), pl.ds(first, count)


def box_z(x):
    lane = lax.broadcasted_iota(jnp.int32, x.shape, x.ndim - 1)
    depth = x.shape[-1]
    below = jnp.where(lane == 0, 0.0, pltpu.roll(x, 1, x.ndim - 1))
    above = jnp.where(lane == depth - 1, 0.0, pltpu.roll(x, depth - 1, x.ndim - 1))
    return x + below + above


def next_z(x):
    return pltpu.roll(x, x.shape[-1] - 1, x.ndim - 1)


def previous_z(x):
    return pltpu.roll(x, 1, x.ndim - 1)


def smooth(sizes, *refs):
    nx, ny, depth, kx, ky, slabs, planes = sizes
    (start_hbm, load_hbm, shift_hbm, coarse_hbm, agg_hbm, cons_hbm, final, cons,
     start, load, shift, table, agg, earlier, resid, halo_x, halo_y, border_y,
     in_sem, send_sem, recv_sem) = refs
    fields = [earlier.at[n] for n in range(DEGREE)] + [final]
    slab = lax.axis_index("slab")
    plane = lax.axis_index("plane")

    def exists(step_x, step_y):
        x, y = slab + step_x, plane + step_y
        return (x >= 0) & (x < slabs) & (y >= 0) & (y < planes)

    loads = [
        pltpu.make_async_copy(coarse_hbm, table.at[:, pl.ds(1, kx), pl.ds(0, ky)], in_sem.at[0]),
        pltpu.make_async_copy(agg_hbm, agg, in_sem.at[1]),
        pltpu.make_async_copy(start_hbm, start, in_sem.at[2]),
        pltpu.make_async_copy(cons_hbm, cons.at[pl.ds(1, nx), pl.ds(OFF, ny)], in_sem.at[3]),
        pltpu.make_async_copy(load_hbm, load, in_sem.at[4]),
        pltpu.make_async_copy(shift_hbm, shift, in_sem.at[5]),
    ]
    for copy in loads:
        copy.start()

    zero_table = jnp.zeros((3, 8, depth), jnp.float32)
    for a in range(kx + 2):
        table[:, a, ky:ky + 8, :] = zero_table
    table[:, 0, 0:ky, :] = zero_table
    table[:, kx + 1, 0:ky, :] = zero_table

    zero_side = jnp.zeros((3, ny + 16, depth), jnp.float32)
    for phase in range(DEGREE):
        for side in range(2):
            halo_x[phase, side] = zero_side
            halo_y[phase, side] = jnp.zeros((3, nx + 16, depth), jnp.float32)

    barrier = pltpu.get_barrier_semaphore()
    for step_x, step_y in SIDES:
        @pl.when(exists(step_x, step_y))
        def _():
            pl.semaphore_signal(
                barrier, inc=1, device_id=(slab + step_x, plane + step_y), device_id_type=MESH
            )

    for field in fields[:DEGREE]:
        field[:, 0] = zero_side
        field[:, nx + 1] = zero_side
        for i in range(1, nx + 1):
            field[:, i, 0:OFF, :] = zero_side[:, 0:OFF]
            field[:, i, OFF + ny:OFF + ny + 8, :] = zero_side[:, 0:8]

    near_x = 1 + (slab > 0).astype(jnp.int32) + (slab < slabs - 1).astype(jnp.int32)
    near_y = 1 + (plane > 0).astype(jnp.int32) + (plane < planes - 1).astype(jnp.int32)
    pl.semaphore_wait(barrier, near_x * near_y - 1)

    def remote(source, target, phase, side):
        step_x, step_y = SIDES[side]
        return pltpu.make_async_remote_copy(
            src_ref=source, dst_ref=target,
            send_sem=send_sem.at[phase, side], recv_sem=recv_sem.at[phase, side],
            device_id=(slab + step_x, plane + step_y), device_id_type=MESH,
        )

    def start_all(make, phase, sides=SIDES):
        for side, (step_x, step_y) in enumerate(SIDES):
            if (step_x, step_y) in sides:
                @pl.when(exists(step_x, step_y))
                def _():
                    remote(*make(step_x, step_y), phase, side).start()

    def wait_arrived(make, phase, sides=SIDES):
        for side, (step_x, step_y) in enumerate(SIDES):
            if (step_x, step_y) in sides:
                @pl.when(exists(-step_x, -step_y))
                def _():
                    remote(*make(step_x, step_y), phase, side).wait_recv()

    def wait_sent(make, phase, sides=SIDES):
        for side, (step_x, step_y) in enumerate(SIDES):
            if (step_x, step_y) in sides:
                @pl.when(exists(step_x, step_y))
                def _():
                    remote(*make(step_x, step_y), phase, side).wait_send()

    def coarse_edge(step_x, step_y):
        from_x, to_x = edge(step_x, 1, kx)
        from_y, to_y = edge(step_y, 0, ky)
        from_x = pl.ds(from_x.start - 1, from_x.size)
        if step_y > 0:
            to_y = pl.ds(ky + 7, 1)
        return coarse_hbm.at[:, from_x, from_y], table.at[:, to_x, to_y]

    def cons_edge(step_x, step_y):
        from_x, to_x = edge(step_x, 1, nx)
        from_y, to_y = edge(step_y, OFF, ny)
        return (
            cons_hbm.at[pl.ds(from_x.start - 1, from_x.size), pl.ds(from_y.start - OFF, from_y.size)],
            cons.at[to_x, to_y],
        )

    def field_edge(step_x, step_y):
        from_x, to_x = edge(step_x, 1, nx)
        from_y, to_y = edge(step_y, OFF, ny)
        return final.at[:, from_x, from_y], final.at[:, to_x, to_y]

    def halo_edge(phase):
        def make(step_x, step_y):
            row = nx if step_x > 0 else 1
            to_x, to_y = int(step_x < 0), int(step_y < 0)
            if step_y == 0:
                return (
                    fields[phase].at[:, row, pl.ds(OFF, ny)],
                    halo_x.at[phase, to_x, :, pl.ds(OFF, ny)],
                )
            border = border_y.at[phase, 1 - to_y]
            if step_x == 0:
                return border, halo_y.at[phase, to_y, :, pl.ds(OFF, nx)]
            corner = OFF - 1 if step_y > 0 else OFF + ny
            return border.at[:, pl.ds(row - 1, 1)], halo_x.at[phase, to_x, :, pl.ds(corner, 1)]
        return make

    def column(ref, side, tall, first):
        lines = ref.reshape(ref.shape[0] * tall, depth)
        return lines, pl.ds(first + side * (ny - 1), nx, stride=tall)

    def field_column(phase, c, side):
        return column(fields[phase].at[c], side, ny + 16, ny + 16 + OFF)

    def fill_border(phase):
        for c in range(3):
            for side in range(2):
                lines, where = field_column(phase, c, side)
                border_y[phase, side, c] = lines[where, :]

    last = DEGREE + 1
    start_all(coarse_edge, last)

    loads[1].wait()
    cols = ky * planes
    whole = agg[...]
    if cols & (cols - 1) == 0:
        row_a = lax.shift_right_logical(whole, cols.bit_length() - 1)
    else:
        row_a = lax.div(whole, cols)
    place = (row_a - (slab * kx - 1)) * (ky + 8)
    col_b = whole - row_a * cols - plane * ky
    place = (place + jnp.where(col_b < 0, ky + 7, col_b)).astype(jnp.float32)
    deep = (kx + 2) * (ky + 8)
    own = lax.broadcasted_iota(jnp.int32, (ny, ny), 0) == lax.broadcasted_iota(jnp.int32, (ny, ny), 1)
    slots = lax.broadcasted_iota(jnp.int32, (ny, deep), 1).astype(jnp.float32)
    picks = []
    for i in range(nx):
        target = jnp.sum(jnp.where(own, place[i:i + 1, :], 0.0), axis=1, keepdims=True)
        picks.append((target == slots).astype(jnp.bfloat16))
    pick = jnp.concatenate(picks, axis=0)
    loads[0].wait()
    loads[2].wait()
    wait_arrived(coarse_edge, last)
    for c in range(3):
        rest = table[c].reshape(deep, depth)
        moved = None
        for _ in range(3):
            part = rest.astype(jnp.bfloat16)
            rest = rest - part.astype(jnp.float32)
            piece = jnp.dot(pick, part, preferred_element_type=jnp.float32)
            moved = piece if moved is None else moved + piece
        fields[0][c, 1:nx + 1, OFF:OFF + ny, :] = start[c] + moved.reshape(nx, ny, depth)

    fill_border(0)
    start_all(halo_edge(0), 0)
    start_all(cons_edge, last + 1, LOW_SIDES)
    loads[4].wait()
    loads[5].wait()

    rho = 1.0 / SIGMA
    keep, gain = None, 1.0 / THETA
    for phase in range(DEGREE):
        if phase:
            rho_new = 1.0 / (2.0 * SIGMA - rho)
            keep, gain = rho_new * rho, 2.0 * rho_new / DELTA_C
            rho = rho_new

        def own_block(c, carry):
            along_y = (
                fields[phase][c, :, pl.ds(OFF - 1, ny), :]
                + fields[phase][c, :, pl.ds(OFF, ny), :]
                + fields[phase][c, :, pl.ds(OFF + 1, ny), :]
            )
            boxed = box_z(along_y[:-2] + along_y[1:-1] + along_y[2:])
            inner = (c, pl.ds(1, nx), pl.ds(OFF, ny))
            centre = fields[phase][inner]
            applied = (3.0 + shift[...]) * centre - boxed * (1.0 / 3.0)
            if phase == 0:
                left = load[c] - applied
                direction = left * gain
            else:
                left = resid[c] - applied
                direction = keep * centre + gain * left
            if phase < DEGREE - 1:
                resid[c] = left
            else:
                for n in range(DEGREE):
                    direction = direction + fields[n][inner]
            fields[phase + 1][inner] = direction
            return carry

        lax.fori_loop(0, 3, own_block, 0)

        wait_arrived(halo_edge(phase), phase)
        from_y, from_x = {}, {}
        for c in range(3):
            for side in range(2):
                for halo, given, count in ((halo_y, from_y, nx), (halo_x, from_x, ny)):
                    line = (
                        halo[phase, side, c, pl.ds(OFF - 1, count), :]
                        + halo[phase, side, c, pl.ds(OFF, count), :]
                        + halo[phase, side, c, pl.ds(OFF + 1, count), :]
                    )
                    given[c, side] = box_z(line) * (1.0 / 3.0)
        for c in range(3):
            for side in range(2):
                lines, where = field_column(phase + 1, c, side)
                lines[where, :] = lines[where, :] + gain * from_y[c, side]
            for side in range(2):
                at = (c, 1 + side * (nx - 1), pl.ds(OFF, ny))
                fields[phase + 1][at] = fields[phase + 1][at] + gain * from_x[c, side]
        if phase < DEGREE - 1:
            fill_border(phase + 1)
            start_all(halo_edge(phase + 1), phase + 1)
            for c in range(3):
                for side in range(2):
                    lines, where = column(resid.at[c], side, ny, 0)
                    lines[where, :] = lines[where, :] + from_y[c, side]
                for side in range(2):
                    at = (c, side * (nx - 1))
                    resid[at] = resid[at] + from_x[c, side]
        else:
            start_all(field_edge, DEGREE)

    loads[3].wait()
    wait_arrived(cons_edge, last + 1, LOW_SIDES)
    wait_arrived(field_edge, DEGREE)

    wait_sent(coarse_edge, last)
    wait_sent(cons_edge, last + 1, LOW_SIDES)
    for phase in range(DEGREE):
        wait_sent(halo_edge(phase), phase)
    wait_sent(field_edge, DEGREE)


def stresses(sizes, field, cons, disp_out, rec_out, ind_out, rec, ind, out_sem):
    nx, ny, depth, kx, ky, slabs, planes = sizes
    first_x = lax.axis_index("slab") * nx
    first_y = lax.axis_index("plane") * ny
    total_x, total_y = nx * slabs, ny * planes
    tall = ny + 8
    lane = lax.broadcasted_iota(jnp.int32, (tall, depth), 1)
    node_y = first_y - 1 + lax.broadcasted_iota(jnp.int32, (tall, depth), 0)
    valid_y = (node_y >= 0) & (node_y <= total_y - 2) & (lane <= depth - 2)
    lane = lax.broadcasted_iota(jnp.int32, (ny, depth), 1)
    node_y = first_y + lax.broadcasted_iota(jnp.int32, (ny, depth), 0)

    def half(ok):
        return jnp.where(ok, 0.5, 1.0)

    scale_y = half((node_y >= 1) & (node_y <= total_y - 2)) * half((lane >= 1) & (lane <= depth - 2))

    inner = field.at[:, pl.ds(1, nx), pl.ds(OFF, ny)]
    whole = pltpu.make_async_copy(inner, disp_out, out_sem.at[0])
    whole.start()

    def part(n):
        here = pl.ds(n * ROWS_OUT, ROWS_OUT)
        return (
            pltpu.make_async_copy(rec.at[:, here], rec_out.at[:, here], out_sem.at[1 + 2 * n]),
            pltpu.make_async_copy(ind.at[here], ind_out.at[here], out_sem.at[2 + 2 * n]),
        )

    def corner_sums(c, i):
        low = field[c, i, pl.ds(OFF - 1, tall), :]
        high = field[c, i, pl.ds(OFF, tall), :]
        return low + high, high - low

    def element_row(i):
        grad_x, grad_y, grad_z = [], [], []
        for c in range(3):
            sum_a, diff_a = corner_sums(c, i)
            sum_b, diff_b = corner_sums(c, i + 1)
            gx, gy, gz = sum_b - sum_a, diff_a + diff_b, sum_a + sum_b
            grad_x.append(0.25 * (gx + next_z(gx)))
            grad_y.append(0.25 * (gy + next_z(gy)))
            grad_z.append(0.25 * (next_z(gz) - gz))
        exx, eyy, ezz = grad_x[0], grad_y[1], grad_z[2]
        exy = 0.5 * (grad_y[0] + grad_x[1])
        eyz = 0.5 * (grad_z[1] + grad_y[2])
        ezx = 0.5 * (grad_x[2] + grad_z[0])
        trace = exx + eyy + ezz
        third = trace * (1.0 / 3.0)
        sxx, syy, szz = exx - third, eyy - third, ezz - third
        equiv = (2.0 / 3.0) * (
            sxx * sxx + syy * syy + szz * szz + 2.0 * (exy * exy + eyz * eyz + ezx * ezx)
        )
        visc = cons[i, pl.ds(OFF - 1, tall), :] * jnp.exp(-0.425 * jnp.log(0.01 + 3.0 * equiv))
        twice = 2.0 * visc
        bulk = 4.0 * trace
        sig = [twice * sxx + bulk, twice * syy + bulk, twice * szz + bulk,
               twice * exy, twice * eyz, twice * ezx]
        norm_sq = (
            sig[0] * sig[0] + sig[1] * sig[1] + sig[2] * sig[2]
            + 2.0 * (sig[3] * sig[3] + sig[4] * sig[4] + sig[5] * sig[5])
        )
        node_x = first_x - 1 + i
        valid = valid_y & (node_x >= 0) & (node_x <= total_x - 2)
        summed = []
        for one in sig + [norm_sq]:
            one = jnp.where(valid, one, 0.0)
            one = one[0:ny] + one[1:ny + 1]
            summed.append(one + previous_z(one))
        return tuple(summed)

    def row(i, before):
        after = element_row(i)
        node_x = first_x + i - 1
        inside = ((node_x >= 1) & (node_x <= total_x - 2)).astype(jnp.float32)
        scale = scale_y * (1.0 - 0.5 * inside)
        total = [(a + b) * scale for a, b in zip(before, after)]
        for n in range(6):
            rec[n, i - 1] = total[n]
        ind[i - 1] = total[6] - (
            total[0] * total[0] + total[1] * total[1] + total[2] * total[2]
            + 2.0 * (total[3] * total[3] + total[4] * total[4] + total[5] * total[5])
        )
        return after

    carry = element_row(0)
    for n in range(nx // ROWS_OUT):
        carry = lax.fori_loop(1 + n * ROWS_OUT, 1 + (n + 1) * ROWS_OUT, row, carry, unroll=True)
        for copy in part(n):
            copy.start()
    whole.wait()
    for n in range(nx // ROWS_OUT):
        for copy in part(n):
            copy.wait()


def body(sizes, *blocks):
    nx, ny, depth, kx, ky, slabs, planes = sizes
    hbm = pl.BlockSpec(memory_space=pltpu.HBM)
    vmem = pl.BlockSpec(memory_space=pltpu.VMEM)
    f32 = jnp.float32
    padded = (
        jax.ShapeDtypeStruct((3, nx + 2, ny + 16, depth), f32),
        jax.ShapeDtypeStruct((nx + 1, ny + 16, depth), f32),
    )
    field, cons = pl.pallas_call(
        functools.partial(smooth, sizes),
        out_shape=padded,
        in_specs=[hbm] * 6,
        out_specs=(vmem,) * 2,
        scratch_shapes=[
            pltpu.VMEM((3, nx, ny, depth), f32),
            pltpu.VMEM((3, nx, ny, depth), f32),
            pltpu.VMEM((nx, ny, depth), f32),
            pltpu.VMEM((3, kx + 2, ky + 8, depth), f32),
            pltpu.VMEM((nx, ny), jnp.int32),
            pltpu.VMEM((DEGREE, 3, nx + 2, ny + 16, depth), f32),
            pltpu.VMEM((3, nx, ny, depth), f32),
            pltpu.VMEM((DEGREE, 2, 3, ny + 16, depth), f32),
            pltpu.VMEM((DEGREE, 2, 3, nx + 16, depth), f32),
            pltpu.VMEM((DEGREE, 2, 3, nx, depth), f32),
            pltpu.SemaphoreType.DMA((6,)),
            pltpu.SemaphoreType.DMA((DEGREE + 3, len(SIDES))),
            pltpu.SemaphoreType.DMA((DEGREE + 3, len(SIDES))),
        ],
        compiler_params=pltpu.CompilerParams(
            collective_id=0, has_side_effects=True, vmem_limit_bytes=VMEM_BYTES
        ),
    )(*blocks)
    outs = (
        jax.ShapeDtypeStruct((3, nx, ny, depth), f32),
        jax.ShapeDtypeStruct((6, nx, ny, depth), f32),
        jax.ShapeDtypeStruct((nx, ny, depth), f32),
    )
    return pl.pallas_call(
        functools.partial(stresses, sizes),
        out_shape=outs,
        in_specs=[vmem] * 2,
        out_specs=(hbm,) * 3,
        scratch_shapes=[
            pltpu.VMEM(outs[1].shape, f32),
            pltpu.VMEM(outs[2].shape, f32),
            pltpu.SemaphoreType.DMA((1 + 2 * (nx // ROWS_OUT),)),
        ],
        compiler_params=pltpu.CompilerParams(vmem_limit_bytes=VMEM_BYTES),
    )(field, cons)


def solution(mesh):
    in_specs = (
        P(None, "slab", "plane", None),
        P(None, "slab", "plane", None),
        P("slab", "plane", None),
        P(None, "slab", "plane", None),
        P("slab", "plane"),
        P("slab", "plane", None),
    )
    out_specs = (
        P(None, "slab", "plane", None),
        P(None, "slab", "plane", None),
        P("slab", "plane", None),
    )
    slabs, planes = mesh.shape["slab"], mesh.shape["plane"]

    def run(start_disp, load, shift, coarse, aggregate, consistency):
        sizes = (
            start_disp.shape[1] // slabs, start_disp.shape[2] // planes, start_disp.shape[3],
            coarse.shape[1] // slabs, coarse.shape[2] // planes, slabs, planes,
        )
        return jax.shard_map(
            functools.partial(body, sizes), mesh=mesh, in_specs=in_specs, out_specs=out_specs,
            check_vma=False,
        )(start_disp, load, shift, coarse, aggregate, consistency)

    return run
```

```python
import functools

import jax
import jax.numpy as jnp
from jax import lax
from jax.experimental import pallas as pl
from jax.experimental.pallas import tpu as pltpu
from jax.sharding import PartitionSpec as P

DEGREE = 4
THETA = 4.5
DELTA_C = 3.5
SIGMA = THETA / DELTA_C
MESH = pl.DeviceIdType.MESH
OFF = 8
SIDES = ((0, 1), (0, -1), (1, 1), (1, -1), (-1, 1), (-1, -1), (1, 0), (-1, 0))
VMEM_BYTES = 56 * 1024 * 1024
ROWS_OUT = 4
LOW_SIDES = ((0, 1), (1, 1), (1, 0))


def edge(step, first, count, width=1):
    if step > 0:
        return pl.ds(first + count - width, width), pl.ds(first - width, width)
    if step < 0:
        return pl.ds(first, width), pl.ds(first + count, width)
    return pl.ds(first, count), pl.ds(first, count)


def box_z(x):
    lane = lax.broadcasted_iota(jnp.int32, x.shape, x.ndim - 1)
    depth = x.shape[-1]
    below = jnp.where(lane == 0, 0.0, pltpu.roll(x, 1, x.ndim - 1))
    above = jnp.where(lane == depth - 1, 0.0, pltpu.roll(x, depth - 1, x.ndim - 1))
    return x + below + above


def next_z(x):
    return pltpu.roll(x, x.shape[-1] - 1, x.ndim - 1)


def previous_z(x):
    return pltpu.roll(x, 1, x.ndim - 1)


def smooth(sizes, *refs):
    nx, ny, depth, kx, ky, slabs, planes = sizes
    (start_hbm, load_hbm, shift_hbm, coarse_hbm, agg_hbm, cons_hbm, final, cons,
     start, load, shift, table, agg, earlier, resid, resid_sent, in_sem, send_sem, recv_sem) = refs
    fields = [earlier.at[n] for n in range(DEGREE)]
    slab = lax.axis_index("slab")
    plane = lax.axis_index("plane")

    def exists(step_x, step_y):
        x, y = slab + step_x, plane + step_y
        return (x >= 0) & (x < slabs) & (y >= 0) & (y < planes)

    loads = [
        pltpu.make_async_copy(coarse_hbm, table.at[:, pl.ds(1, kx), pl.ds(0, ky)], in_sem.at[0]),
        pltpu.make_async_copy(agg_hbm, agg, in_sem.at[1]),
        pltpu.make_async_copy(start_hbm, start, in_sem.at[2]),
        pltpu.make_async_copy(cons_hbm, cons.at[pl.ds(1, nx), pl.ds(OFF, ny)], in_sem.at[3]),
        pltpu.make_async_copy(
            load_hbm, load.at[:, pl.ds(1, nx), pl.ds(OFF, ny)], in_sem.at[4]
        ),
        pltpu.make_async_copy(shift_hbm, shift.at[pl.ds(1, nx), pl.ds(OFF, ny)], in_sem.at[5]),
    ]
    for copy in loads:
        copy.start()

    zero_table = jnp.zeros((3, 8, depth), jnp.float32)
    for a in range(kx + 2):
        table[:, a, ky:ky + 8, :] = zero_table
    table[:, 0, 0:ky, :] = zero_table
    table[:, kx + 1, 0:ky, :] = zero_table

    for field in (fields[0], fields[2]):
        for i in range(nx + 4):
            if i < 2 or i >= nx + 2:
                field[:, i] = jnp.zeros((3, ny + 16, depth), jnp.float32)
            else:
                field[:, i, 0:OFF, :] = zero_table
                field[:, i, OFF + ny:OFF + ny + 8, :] = zero_table

    barrier = pltpu.get_barrier_semaphore()
    for step_x, step_y in SIDES:
        @pl.when(exists(step_x, step_y))
        def _():
            pl.semaphore_signal(
                barrier, inc=1, device_id=(slab + step_x, plane + step_y), device_id_type=MESH
            )

    near_x = 1 + (slab > 0).astype(jnp.int32) + (slab < slabs - 1).astype(jnp.int32)
    near_y = 1 + (plane > 0).astype(jnp.int32) + (plane < planes - 1).astype(jnp.int32)
    pl.semaphore_wait(barrier, near_x * near_y - 1)

    def remote(source, target, phase, side):
        step_x, step_y = SIDES[side]
        return pltpu.make_async_remote_copy(
            src_ref=source, dst_ref=target,
            send_sem=send_sem.at[phase, side], recv_sem=recv_sem.at[phase, side],
            device_id=(slab + step_x, plane + step_y), device_id_type=MESH,
        )

    def start_all(make, phase, sides=SIDES):
        for side, (step_x, step_y) in enumerate(SIDES):
            if (step_x, step_y) in sides:
                @pl.when(exists(step_x, step_y))
                def _():
                    remote(*make(step_x, step_y), phase, side).start()

    def wait_arrived(make, phase, sides=SIDES):
        for side, (step_x, step_y) in enumerate(SIDES):
            if (step_x, step_y) in sides:
                @pl.when(exists(-step_x, -step_y))
                def _():
                    remote(*make(step_x, step_y), phase, side).wait_recv()

    def wait_sent(make, phase, sides=SIDES):
        for side, (step_x, step_y) in enumerate(SIDES):
            if (step_x, step_y) in sides:
                @pl.when(exists(step_x, step_y))
                def _():
                    remote(*make(step_x, step_y), phase, side).wait_send()

    def coarse_edge(step_x, step_y):
        from_x, to_x = edge(step_x, 1, kx)
        from_y, to_y = edge(step_y, 0, ky)
        from_x = pl.ds(from_x.start - 1, from_x.size)
        if step_y > 0:
            to_y = pl.ds(ky + 7, 1)
        return coarse_hbm.at[:, from_x, from_y], table.at[:, to_x, to_y]

    def input_edge(source, target):
        lead = (slice(None),) * (len(source.shape) - 3)

        def make(step_x, step_y):
            from_x, to_x = edge(step_x, 1, nx)
            from_y, to_y = edge(step_y, OFF, ny)
            from_x = pl.ds(from_x.start - 1, from_x.size)
            from_y = pl.ds(from_y.start - OFF, from_y.size)
            return source.at[lead + (from_x, from_y)], target.at[lead + (to_x, to_y)]
        return make

    def field_edge(field, width):
        def make(step_x, step_y):
            from_x, to_x = edge(step_x, width, nx, width)
            from_y, to_y = edge(step_y, OFF, ny, width)
            return field.at[:, from_x, from_y], field.at[:, to_x, to_y]
        return make

    coarse_go = (coarse_edge, 0)
    load_go = (input_edge(load_hbm, load), 1)
    shift_go = (input_edge(shift_hbm, shift), 2)
    cons_go = (input_edge(cons_hbm, cons), 3, LOW_SIDES)
    first_go = (field_edge(fields[0], 2), 4)
    middle_go = (field_edge(fields[2], 2), 5)
    resid_go = (field_edge(resid_sent, 1), 6)
    final_go = (field_edge(final, 1), 7)
    start_all(*coarse_go)
    start_all(*load_go)
    start_all(*shift_go)
    start_all(*cons_go)

    loads[1].wait()
    cols = ky * planes
    whole = agg[...]
    if cols & (cols - 1) == 0:
        row_a = lax.shift_right_logical(whole, cols.bit_length() - 1)
    else:
        row_a = lax.div(whole, cols)
    place = (row_a - (slab * kx - 1)) * (ky + 8)
    col_b = whole - row_a * cols - plane * ky
    place = (place + jnp.where(col_b < 0, ky + 7, col_b)).astype(jnp.float32)
    deep = (kx + 2) * (ky + 8)
    own = lax.broadcasted_iota(jnp.int32, (ny, ny), 0) == lax.broadcasted_iota(jnp.int32, (ny, ny), 1)
    slots = lax.broadcasted_iota(jnp.int32, (ny, deep), 1).astype(jnp.float32)
    picks = []
    for i in range(nx):
        column = jnp.sum(jnp.where(own, place[i:i + 1, :], 0.0), axis=1, keepdims=True)
        picks.append((column == slots).astype(jnp.bfloat16))
    pick = jnp.concatenate(picks, axis=0)
    loads[0].wait()
    loads[2].wait()
    wait_arrived(*coarse_go)
    for c in range(3):
        rest = table[c].reshape(deep, depth)
        moved = None
        for _ in range(3):
            part = rest.astype(jnp.bfloat16)
            rest = rest - part.astype(jnp.float32)
            piece = jnp.dot(pick, part, preferred_element_type=jnp.float32)
            moved = piece if moved is None else moved + piece
        fields[0][c, 2:nx + 2, OFF:OFF + ny, :] = start[c] + moved.reshape(nx, ny, depth)

    start_all(*first_go)
    loads[4].wait()
    loads[5].wait()
    wait_arrived(*load_go)
    wait_arrived(*shift_go)
    wait_arrived(*first_go)

    rows = nx // 2 + 1
    first_x, first_y = slab * nx, plane * ny
    lines = lax.broadcasted_iota(jnp.int32, (rows, ny + 8, depth), 1) + (first_y - 1)
    across = lax.broadcasted_iota(jnp.int32, (rows, ny + 8, depth), 0) + (first_x - 1)
    in_mesh_y = (lines >= 0) & (lines < ny * planes)

    def stencil(phase, c, first, count, top, tall):
        field = fields[phase]
        span = pl.ds(first - 1, count + 2)
        along_y = (
            field[c, span, pl.ds(top - 1, tall), :]
            + field[c, span, pl.ds(top, tall), :]
            + field[c, span, pl.ds(top + 1, tall), :]
        )
        boxed = box_z(along_y[:-2] + along_y[1:-1] + along_y[2:])
        centre = field[c, pl.ds(first, count), pl.ds(top, tall), :]
        here = shift[pl.ds(first - 1, count), pl.ds(top, tall), :]
        return centre, (3.0 + here) * centre - boxed * (1.0 / 3.0)

    rho = 1.0 / SIGMA
    keep, gain = 0.0, 1.0 / THETA
    for phase in range(DEGREE):
        if phase:
            rho_new = 1.0 / (2.0 * SIGMA - rho)
            keep, gain = rho_new * rho, 2.0 * rho_new / DELTA_C
            rho = rho_new
        if phase == 2:
            wait_arrived(*middle_go)
            wait_arrived(*resid_go)

        def wide(at, carry):
            c = at // 2
            first = 1 + (at % 2) * rows
            centre, applied = stencil(phase, c, first, rows, OFF - 1, ny + 8)
            where = (c, pl.ds(first - 1, rows), pl.ds(OFF - 1, ny + 8))
            left = (load if phase == 0 else resid_sent)[where] - applied
            direction = gain * left
            if phase:
                direction = direction + keep * centre
            node_x = across + (first - 1)
            inside = in_mesh_y & (node_x >= 0) & (node_x < nx * slabs)
            resid[where] = left
            fields[phase + 1][c, pl.ds(first, rows), pl.ds(OFF - 1, ny + 8), :] = jnp.where(
                inside, direction, 0.0
            )
            return carry

        def narrow(c, carry):
            centre, applied = stencil(phase, c, 2, nx, OFF, ny)
            where = (c, pl.ds(1, nx), pl.ds(OFF, ny))
            inner = (c, pl.ds(2, nx), pl.ds(OFF, ny))
            left = resid[where] - applied
            direction = keep * centre + gain * left
            if phase < DEGREE - 1:
                resid_sent[where] = left
                fields[phase + 1][inner] = direction
            else:
                for n in range(DEGREE):
                    direction = direction + fields[n][inner]
                final[where] = direction
            return carry

        if phase % 2 == 0:
            lax.fori_loop(0, 6, wide, 0)
        else:
            lax.fori_loop(0, 3, narrow, 0)
        if phase == 1:
            start_all(*middle_go)
            start_all(*resid_go)
    start_all(*final_go)

    loads[3].wait()
    wait_arrived(*cons_go)
    wait_arrived(*final_go)
    for go in (coarse_go, load_go, shift_go, cons_go, first_go, middle_go, resid_go, final_go):
        wait_sent(*go)


def stresses(sizes, field, cons, disp_out, rec_out, ind_out, rec, ind, out_sem):
    nx, ny, depth, kx, ky, slabs, planes = sizes
    first_x = lax.axis_index("slab") * nx
    first_y = lax.axis_index("plane") * ny
    total_x, total_y = nx * slabs, ny * planes
    tall = ny + 8
    lane = lax.broadcasted_iota(jnp.int32, (tall, depth), 1)
    node_y = first_y - 1 + lax.broadcasted_iota(jnp.int32, (tall, depth), 0)
    valid_y = (node_y >= 0) & (node_y <= total_y - 2) & (lane <= depth - 2)
    lane = lax.broadcasted_iota(jnp.int32, (ny, depth), 1)
    node_y = first_y + lax.broadcasted_iota(jnp.int32, (ny, depth), 0)

    def half(ok):
        return jnp.where(ok, 0.5, 1.0)

    scale_y = half((node_y >= 1) & (node_y <= total_y - 2)) * half((lane >= 1) & (lane <= depth - 2))

    inner = field.at[:, pl.ds(1, nx), pl.ds(OFF, ny)]
    whole = pltpu.make_async_copy(inner, disp_out, out_sem.at[0])
    whole.start()

    def part(n):
        here = pl.ds(n * ROWS_OUT, ROWS_OUT)
        return (
            pltpu.make_async_copy(rec.at[:, here], rec_out.at[:, here], out_sem.at[1 + 2 * n]),
            pltpu.make_async_copy(ind.at[here], ind_out.at[here], out_sem.at[2 + 2 * n]),
        )

    def corner_sums(c, i):
        low = field[c, i, pl.ds(OFF - 1, tall), :]
        high = field[c, i, pl.ds(OFF, tall), :]
        return low + high, high - low

    def element_row(i):
        grad_x, grad_y, grad_z = [], [], []
        for c in range(3):
            sum_a, diff_a = corner_sums(c, i)
            sum_b, diff_b = corner_sums(c, i + 1)
            gx, gy, gz = sum_b - sum_a, diff_a + diff_b, sum_a + sum_b
            grad_x.append(0.25 * (gx + next_z(gx)))
            grad_y.append(0.25 * (gy + next_z(gy)))
            grad_z.append(0.25 * (next_z(gz) - gz))
        exx, eyy, ezz = grad_x[0], grad_y[1], grad_z[2]
        exy = 0.5 * (grad_y[0] + grad_x[1])
        eyz = 0.5 * (grad_z[1] + grad_y[2])
        ezx = 0.5 * (grad_x[2] + grad_z[0])
        trace = exx + eyy + ezz
        third = trace * (1.0 / 3.0)
        sxx, syy, szz = exx - third, eyy - third, ezz - third
        equiv = (2.0 / 3.0) * (
            sxx * sxx + syy * syy + szz * szz + 2.0 * (exy * exy + eyz * eyz + ezx * ezx)
        )
        visc = cons[i, pl.ds(OFF - 1, tall), :] * jnp.exp(-0.425 * jnp.log(0.01 + 3.0 * equiv))
        twice = 2.0 * visc
        bulk = 4.0 * trace
        sig = [twice * sxx + bulk, twice * syy + bulk, twice * szz + bulk,
               twice * exy, twice * eyz, twice * ezx]
        norm_sq = (
            sig[0] * sig[0] + sig[1] * sig[1] + sig[2] * sig[2]
            + 2.0 * (sig[3] * sig[3] + sig[4] * sig[4] + sig[5] * sig[5])
        )
        node_x = first_x - 1 + i
        valid = valid_y & (node_x >= 0) & (node_x <= total_x - 2)
        summed = []
        for one in sig + [norm_sq]:
            one = jnp.where(valid, one, 0.0)
            one = one[0:ny] + one[1:ny + 1]
            summed.append(one + previous_z(one))
        return tuple(summed)

    def row(i, before):
        after = element_row(i)
        node_x = first_x + i - 1
        inside = ((node_x >= 1) & (node_x <= total_x - 2)).astype(jnp.float32)
        scale = scale_y * (1.0 - 0.5 * inside)
        total = [(a + b) * scale for a, b in zip(before, after)]
        for n in range(6):
            rec[n, i - 1] = total[n]
        ind[i - 1] = total[6] - (
            total[0] * total[0] + total[1] * total[1] + total[2] * total[2]
            + 2.0 * (total[3] * total[3] + total[4] * total[4] + total[5] * total[5])
        )
        return after

    carry = element_row(0)
    for n in range(nx // ROWS_OUT):
        carry = lax.fori_loop(1 + n * ROWS_OUT, 1 + (n + 1) * ROWS_OUT, row, carry, unroll=True)
        for copy in part(n):
            copy.start()
    whole.wait()
    for n in range(nx // ROWS_OUT):
        for copy in part(n):
            copy.wait()


def body(sizes, *blocks):
    nx, ny, depth, kx, ky, slabs, planes = sizes
    hbm = pl.BlockSpec(memory_space=pltpu.HBM)
    vmem = pl.BlockSpec(memory_space=pltpu.VMEM)
    f32 = jnp.float32
    padded = (
        jax.ShapeDtypeStruct((3, nx + 2, ny + 16, depth), f32),
        jax.ShapeDtypeStruct((nx + 1, ny + 16, depth), f32),
    )
    field, cons = pl.pallas_call(
        functools.partial(smooth, sizes),
        out_shape=padded,
        in_specs=[hbm] * 6,
        out_specs=(vmem,) * 2,
        scratch_shapes=[
            pltpu.VMEM((3, nx, ny, depth), f32),
            pltpu.VMEM((3, nx + 2, ny + 16, depth), f32),
            pltpu.VMEM((nx + 2, ny + 16, depth), f32),
            pltpu.VMEM((3, kx + 2, ky + 8, depth), f32),
            pltpu.VMEM((nx, ny), jnp.int32),
            pltpu.VMEM((DEGREE, 3, nx + 4, ny + 16, depth), f32),
            pltpu.VMEM((3, nx + 2, ny + 16, depth), f32),
            pltpu.VMEM((3, nx + 2, ny + 16, depth), f32),
            pltpu.SemaphoreType.DMA((6,)),
            pltpu.SemaphoreType.DMA((8, len(SIDES))),
            pltpu.SemaphoreType.DMA((8, len(SIDES))),
        ],
        compiler_params=pltpu.CompilerParams(
            collective_id=0, has_side_effects=True, vmem_limit_bytes=VMEM_BYTES
        ),
    )(*blocks)
    outs = (
        jax.ShapeDtypeStruct((3, nx, ny, depth), f32),
        jax.ShapeDtypeStruct((6, nx, ny, depth), f32),
        jax.ShapeDtypeStruct((nx, ny, depth), f32),
    )
    return pl.pallas_call(
        functools.partial(stresses, sizes),
        out_shape=outs,
        in_specs=[vmem] * 2,
        out_specs=(hbm,) * 3,
        scratch_shapes=[
            pltpu.VMEM(outs[1].shape, f32),
            pltpu.VMEM(outs[2].shape, f32),
            pltpu.SemaphoreType.DMA((1 + 2 * (nx // ROWS_OUT),)),
        ],
        compiler_params=pltpu.CompilerParams(vmem_limit_bytes=VMEM_BYTES),
    )(field, cons)


def solution(mesh):
    in_specs = (
        P(None, "slab", "plane", None),
        P(None, "slab", "plane", None),
        P("slab", "plane", None),
        P(None, "slab", "plane", None),
        P("slab", "plane"),
        P("slab", "plane", None),
    )
    out_specs = (
        P(None, "slab", "plane", None),
        P(None, "slab", "plane", None),
        P("slab", "plane", None),
    )
    slabs, planes = mesh.shape["slab"], mesh.shape["plane"]

    def run(start_disp, load, shift, coarse, aggregate, consistency):
        sizes = (
            start_disp.shape[1] // slabs, start_disp.shape[2] // planes, start_disp.shape[3],
            coarse.shape[1] // slabs, coarse.shape[2] // planes, slabs, planes,
        )
        return jax.shard_map(
            functools.partial(body, sizes), mesh=mesh, in_specs=in_specs, out_specs=out_specs,
            check_vma=False,
        )(start_disp, load, shift, coarse, aggregate, consistency)

    return run
```

```python
import functools

import jax
import jax.numpy as jnp
from jax import lax
from jax.experimental import pallas as pl
from jax.experimental.pallas import tpu as pltpu
from jax.sharding import PartitionSpec as P

DEGREE = 4
THETA = 4.5
DELTA_C = 3.5
SIGMA = THETA / DELTA_C
MESH = pl.DeviceIdType.MESH
OFF = 8
SIDES = ((1, 1), (1, -1), (-1, 1), (-1, -1), (0, 1), (0, -1), (1, 0), (-1, 0))
VMEM_BYTES = 56 * 1024 * 1024
ROWS_OUT = 4
LOW_SIDES = ((0, 1), (1, 1), (1, 0))


def edge(step, first, count, width=1):
    if step > 0:
        return pl.ds(first + count - width, width), pl.ds(first - width, width)
    if step < 0:
        return pl.ds(first, width), pl.ds(first + count, width)
    return pl.ds(first, count), pl.ds(first, count)


def box_z(x):
    lane = lax.broadcasted_iota(jnp.int32, x.shape, x.ndim - 1)
    depth = x.shape[-1]
    below = jnp.where(lane == 0, 0.0, pltpu.roll(x, 1, x.ndim - 1))
    above = jnp.where(lane == depth - 1, 0.0, pltpu.roll(x, depth - 1, x.ndim - 1))
    return x + below + above


def next_z(x):
    return pltpu.roll(x, x.shape[-1] - 1, x.ndim - 1)


def previous_z(x):
    return pltpu.roll(x, 1, x.ndim - 1)


def smooth(sizes, *refs):
    nx, ny, depth, kx, ky, slabs, planes = sizes
    (start_hbm, load_hbm, shift_hbm, coarse_hbm, agg_hbm, cons_hbm, final, cons,
     start, load, shift, table, agg, earlier, resid, resid_sent, in_sem, send_sem, recv_sem) = refs
    fields = [earlier.at[n] for n in range(DEGREE)]
    slab = lax.axis_index("slab")
    plane = lax.axis_index("plane")

    def exists(step_x, step_y):
        x, y = slab + step_x, plane + step_y
        return (x >= 0) & (x < slabs) & (y >= 0) & (y < planes)

    loads = [
        pltpu.make_async_copy(coarse_hbm, table.at[:, pl.ds(1, kx), pl.ds(0, ky)], in_sem.at[0]),
        pltpu.make_async_copy(agg_hbm, agg, in_sem.at[1]),
        pltpu.make_async_copy(start_hbm, start, in_sem.at[2]),
        pltpu.make_async_copy(cons_hbm, cons.at[pl.ds(1, nx), pl.ds(OFF, ny)], in_sem.at[3]),
        pltpu.make_async_copy(
            load_hbm, load.at[:, pl.ds(1, nx), pl.ds(OFF, ny)], in_sem.at[4]
        ),
        pltpu.make_async_copy(shift_hbm, shift.at[pl.ds(1, nx), pl.ds(OFF, ny)], in_sem.at[5]),
    ]
    for copy in loads:
        copy.start()

    zero_table = jnp.zeros((3, 8, depth), jnp.float32)
    for a in range(kx + 2):
        table[:, a, ky:ky + 8, :] = zero_table
    table[:, 0, 0:ky, :] = zero_table
    table[:, kx + 1, 0:ky, :] = zero_table

    for field in (fields[0], fields[2]):
        for i in range(nx + 4):
            if i < 2 or i >= nx + 2:
                field[:, i] = jnp.zeros((3, ny + 16, depth), jnp.float32)
            else:
                field[:, i, 0:OFF, :] = zero_table
                field[:, i, OFF + ny:OFF + ny + 8, :] = zero_table

    barrier = pltpu.get_barrier_semaphore()
    for step_x, step_y in SIDES:
        @pl.when(exists(step_x, step_y))
        def _():
            pl.semaphore_signal(
                barrier, inc=1, device_id=(slab + step_x, plane + step_y), device_id_type=MESH
            )

    near_x = 1 + (slab > 0).astype(jnp.int32) + (slab < slabs - 1).astype(jnp.int32)
    near_y = 1 + (plane > 0).astype(jnp.int32) + (plane < planes - 1).astype(jnp.int32)
    pl.semaphore_wait(barrier, near_x * near_y - 1)

    def remote(source, target, phase, side):
        step_x, step_y = SIDES[side]
        return pltpu.make_async_remote_copy(
            src_ref=source, dst_ref=target,
            send_sem=send_sem.at[phase, side], recv_sem=recv_sem.at[phase, side],
            device_id=(slab + step_x, plane + step_y), device_id_type=MESH,
        )

    def start_all(make, phase, sides=SIDES):
        for side, (step_x, step_y) in enumerate(SIDES):
            if (step_x, step_y) in sides:
                @pl.when(exists(step_x, step_y))
                def _():
                    remote(*make(step_x, step_y), phase, side).start()

    def wait_arrived(make, phase, sides=SIDES):
        for side, (step_x, step_y) in enumerate(SIDES):
            if (step_x, step_y) in sides:
                @pl.when(exists(-step_x, -step_y))
                def _():
                    remote(*make(step_x, step_y), phase, side).wait_recv()

    def wait_sent(make, phase, sides=SIDES):
        for side, (step_x, step_y) in enumerate(SIDES):
            if (step_x, step_y) in sides:
                @pl.when(exists(step_x, step_y))
                def _():
                    remote(*make(step_x, step_y), phase, side).wait_send()

    def coarse_edge(step_x, step_y):
        from_x, to_x = edge(step_x, 1, kx)
        from_y, to_y = edge(step_y, 0, ky)
        from_x = pl.ds(from_x.start - 1, from_x.size)
        if step_y > 0:
            to_y = pl.ds(ky + 7, 1)
        return coarse_hbm.at[:, from_x, from_y], table.at[:, to_x, to_y]

    def input_edge(source, target):
        lead = (slice(None),) * (len(source.shape) - 3)

        def make(step_x, step_y):
            from_x, to_x = edge(step_x, 1, nx)
            from_y, to_y = edge(step_y, OFF, ny)
            from_x = pl.ds(from_x.start - 1, from_x.size)
            from_y = pl.ds(from_y.start - OFF, from_y.size)
            return source.at[lead + (from_x, from_y)], target.at[lead + (to_x, to_y)]
        return make

    def field_edge(field, width):
        def make(step_x, step_y):
            from_x, to_x = edge(step_x, width, nx, width)
            from_y, to_y = edge(step_y, OFF, ny, width)
            return field.at[:, from_x, from_y], field.at[:, to_x, to_y]
        return make

    coarse_go = (coarse_edge, 0)
    load_go = (input_edge(load_hbm, load), 1)
    shift_go = (input_edge(shift_hbm, shift), 2)
    cons_go = (input_edge(cons_hbm, cons), 3, LOW_SIDES)
    first_go = (field_edge(fields[0], 2), 4)
    middle_go = (field_edge(fields[2], 2), 5)
    resid_go = (field_edge(resid_sent, 1), 6)
    final_go = (field_edge(final, 1), 7)
    start_all(*coarse_go)
    start_all(*load_go)
    start_all(*shift_go)
    start_all(*cons_go)

    loads[1].wait()
    cols = ky * planes
    whole = agg[...]
    if cols & (cols - 1) == 0:
        row_a = lax.shift_right_logical(whole, cols.bit_length() - 1)
    else:
        row_a = lax.div(whole, cols)
    place = (row_a - (slab * kx - 1)) * (ky + 8)
    col_b = whole - row_a * cols - plane * ky
    place = (place + jnp.where(col_b < 0, ky + 7, col_b)).astype(jnp.float32)
    deep = (kx + 2) * (ky + 8)
    own = lax.broadcasted_iota(jnp.int32, (ny, ny), 0) == lax.broadcasted_iota(jnp.int32, (ny, ny), 1)
    slots = lax.broadcasted_iota(jnp.int32, (ny, deep), 1).astype(jnp.float32)
    picks = []
    for i in range(nx):
        column = jnp.sum(jnp.where(own, place[i:i + 1, :], 0.0), axis=1, keepdims=True)
        picks.append((column == slots).astype(jnp.bfloat16))
    pick = jnp.concatenate(picks, axis=0)
    loads[0].wait()
    loads[2].wait()
    wait_arrived(*coarse_go)
    for c in range(3):
        rest = table[c].reshape(deep, depth)
        moved = None
        for _ in range(3):
            part = rest.astype(jnp.bfloat16)
            rest = rest - part.astype(jnp.float32)
            piece = jnp.dot(pick, part, preferred_element_type=jnp.float32)
            moved = piece if moved is None else moved + piece
        fields[0][c, 2:nx + 2, OFF:OFF + ny, :] = start[c] + moved.reshape(nx, ny, depth)

    start_all(*first_go)
    loads[4].wait()
    loads[5].wait()
    wait_arrived(*load_go)
    wait_arrived(*shift_go)
    wait_arrived(*first_go)

    rows = nx // 2 + 1
    first_x, first_y = slab * nx, plane * ny
    lines = lax.broadcasted_iota(jnp.int32, (rows, ny + 8, depth), 1) + (first_y - 1)
    across = lax.broadcasted_iota(jnp.int32, (rows, ny + 8, depth), 0) + (first_x - 1)
    in_mesh_y = (lines >= 0) & (lines < ny * planes)

    def stencil(phase, c, first, count, top, tall):
        field = fields[phase]
        span = pl.ds(first - 1, count + 2)
        along_y = (
            field[c, span, pl.ds(top - 1, tall), :]
            + field[c, span, pl.ds(top, tall), :]
            + field[c, span, pl.ds(top + 1, tall), :]
        )
        boxed = box_z(along_y[:-2] + along_y[1:-1] + along_y[2:])
        centre = field[c, pl.ds(first, count), pl.ds(top, tall), :]
        here = shift[pl.ds(first - 1, count), pl.ds(top, tall), :]
        return centre, (3.0 + here) * centre - boxed * (1.0 / 3.0)

    rho = 1.0 / SIGMA
    keep, gain = 0.0, 1.0 / THETA
    for phase in range(DEGREE):
        if phase:
            rho_new = 1.0 / (2.0 * SIGMA - rho)
            keep, gain = rho_new * rho, 2.0 * rho_new / DELTA_C
            rho = rho_new
        if phase == 2:
            wait_arrived(*middle_go)
            wait_arrived(*resid_go)

        def wide(at, carry):
            c = at // 2
            first = 1 + (at % 2) * rows
            centre, applied = stencil(phase, c, first, rows, OFF - 1, ny + 8)
            where = (c, pl.ds(first - 1, rows), pl.ds(OFF - 1, ny + 8))
            left = (load if phase == 0 else resid_sent)[where] - applied
            direction = gain * left
            if phase:
                direction = direction + keep * centre
            node_x = across + (first - 1)
            inside = in_mesh_y & (node_x >= 0) & (node_x < nx * slabs)
            resid[where] = left
            fields[phase + 1][c, pl.ds(first, rows), pl.ds(OFF - 1, ny + 8), :] = jnp.where(
                inside, direction, 0.0
            )
            return carry

        def narrow(c, carry):
            centre, applied = stencil(phase, c, 2, nx, OFF, ny)
            where = (c, pl.ds(1, nx), pl.ds(OFF, ny))
            inner = (c, pl.ds(2, nx), pl.ds(OFF, ny))
            left = resid[where] - applied
            direction = keep * centre + gain * left
            if phase < DEGREE - 1:
                resid_sent[where] = left
                fields[phase + 1][inner] = direction
            else:
                for n in range(DEGREE):
                    direction = direction + fields[n][inner]
                final[where] = direction
            return carry

        if phase % 2 == 0:
            lax.fori_loop(0, 6, wide, 0)
        else:
            lax.fori_loop(0, 3, narrow, 0)
        if phase == 1:
            start_all(*middle_go)
            start_all(*resid_go)
    start_all(*final_go)

    loads[3].wait()
    wait_arrived(*cons_go)
    for go in (coarse_go, load_go, shift_go, cons_go, first_go, middle_go, resid_go):
        wait_sent(*go)
    wait_arrived(*final_go)
    wait_sent(*final_go)


def stresses(sizes, field, cons, disp_out, rec_out, ind_out, rec, ind, out_sem):
    nx, ny, depth, kx, ky, slabs, planes = sizes
    first_x = lax.axis_index("slab") * nx
    first_y = lax.axis_index("plane") * ny
    total_x, total_y = nx * slabs, ny * planes
    tall = ny + 8
    lane = lax.broadcasted_iota(jnp.int32, (tall, depth), 1)
    node_y = first_y - 1 + lax.broadcasted_iota(jnp.int32, (tall, depth), 0)
    valid_y = (node_y >= 0) & (node_y <= total_y - 2) & (lane <= depth - 2)
    lane = lax.broadcasted_iota(jnp.int32, (ny, depth), 1)
    node_y = first_y + lax.broadcasted_iota(jnp.int32, (ny, depth), 0)

    def half(ok):
        return jnp.where(ok, 0.5, 1.0)

    scale_y = half((node_y >= 1) & (node_y <= total_y - 2)) * half((lane >= 1) & (lane <= depth - 2))

    inner = field.at[:, pl.ds(1, nx), pl.ds(OFF, ny)]
    whole = pltpu.make_async_copy(inner, disp_out, out_sem.at[0])
    whole.start()

    def part(n):
        here = pl.ds(n * ROWS_OUT, ROWS_OUT)
        return (
            pltpu.make_async_copy(rec.at[:, here], rec_out.at[:, here], out_sem.at[1 + 2 * n]),
            pltpu.make_async_copy(ind.at[here], ind_out.at[here], out_sem.at[2 + 2 * n]),
        )

    def corner_sums(c, i):
        low = field[c, i, pl.ds(OFF - 1, tall), :]
        high = field[c, i, pl.ds(OFF, tall), :]
        return low + high, high - low

    def element_row(i):
        grad_x, grad_y, grad_z = [], [], []
        for c in range(3):
            sum_a, diff_a = corner_sums(c, i)
            sum_b, diff_b = corner_sums(c, i + 1)
            gx, gy, gz = sum_b - sum_a, diff_a + diff_b, sum_a + sum_b
            grad_x.append(0.25 * (gx + next_z(gx)))
            grad_y.append(0.25 * (gy + next_z(gy)))
            grad_z.append(0.25 * (next_z(gz) - gz))
        exx, eyy, ezz = grad_x[0], grad_y[1], grad_z[2]
        exy = 0.5 * (grad_y[0] + grad_x[1])
        eyz = 0.5 * (grad_z[1] + grad_y[2])
        ezx = 0.5 * (grad_x[2] + grad_z[0])
        trace = exx + eyy + ezz
        third = trace * (1.0 / 3.0)
        sxx, syy, szz = exx - third, eyy - third, ezz - third
        equiv = (2.0 / 3.0) * (
            sxx * sxx + syy * syy + szz * szz + 2.0 * (exy * exy + eyz * eyz + ezx * ezx)
        )
        visc = cons[i, pl.ds(OFF - 1, tall), :] * jnp.exp(-0.425 * jnp.log(0.01 + 3.0 * equiv))
        twice = 2.0 * visc
        bulk = 4.0 * trace
        sig = [twice * sxx + bulk, twice * syy + bulk, twice * szz + bulk,
               twice * exy, twice * eyz, twice * ezx]
        norm_sq = (
            sig[0] * sig[0] + sig[1] * sig[1] + sig[2] * sig[2]
            + 2.0 * (sig[3] * sig[3] + sig[4] * sig[4] + sig[5] * sig[5])
        )
        node_x = first_x - 1 + i
        valid = valid_y & (node_x >= 0) & (node_x <= total_x - 2)
        summed = []
        for one in sig + [norm_sq]:
            one = jnp.where(valid, one, 0.0)
            one = one[0:ny] + one[1:ny + 1]
            summed.append(one + previous_z(one))
        return tuple(summed)

    def row(i, before):
        after = element_row(i)
        node_x = first_x + i - 1
        inside = ((node_x >= 1) & (node_x <= total_x - 2)).astype(jnp.float32)
        scale = scale_y * (1.0 - 0.5 * inside)
        total = [(a + b) * scale for a, b in zip(before, after)]
        for n in range(6):
            rec[n, i - 1] = total[n]
        ind[i - 1] = total[6] - (
            total[0] * total[0] + total[1] * total[1] + total[2] * total[2]
            + 2.0 * (total[3] * total[3] + total[4] * total[4] + total[5] * total[5])
        )
        return after

    carry = element_row(0)
    for n in range(nx // ROWS_OUT):
        carry = lax.fori_loop(1 + n * ROWS_OUT, 1 + (n + 1) * ROWS_OUT, row, carry, unroll=True)
        for copy in part(n):
            copy.start()
    whole.wait()
    for n in range(nx // ROWS_OUT):
        for copy in part(n):
            copy.wait()


def body(sizes, *blocks):
    nx, ny, depth, kx, ky, slabs, planes = sizes
    hbm = pl.BlockSpec(memory_space=pltpu.HBM)
    vmem = pl.BlockSpec(memory_space=pltpu.VMEM)
    f32 = jnp.float32
    padded = (
        jax.ShapeDtypeStruct((3, nx + 2, ny + 16, depth), f32),
        jax.ShapeDtypeStruct((nx + 1, ny + 16, depth), f32),
    )
    field, cons = pl.pallas_call(
        functools.partial(smooth, sizes),
        out_shape=padded,
        in_specs=[hbm] * 6,
        out_specs=(vmem,) * 2,
        scratch_shapes=[
            pltpu.VMEM((3, nx, ny, depth), f32),
            pltpu.VMEM((3, nx + 2, ny + 16, depth), f32),
            pltpu.VMEM((nx + 2, ny + 16, depth), f32),
            pltpu.VMEM((3, kx + 2, ky + 8, depth), f32),
            pltpu.VMEM((nx, ny), jnp.int32),
            pltpu.VMEM((DEGREE, 3, nx + 4, ny + 16, depth), f32),
            pltpu.VMEM((3, nx + 2, ny + 16, depth), f32),
            pltpu.VMEM((3, nx + 2, ny + 16, depth), f32),
            pltpu.SemaphoreType.DMA((6,)),
            pltpu.SemaphoreType.DMA((8, len(SIDES))),
            pltpu.SemaphoreType.DMA((8, len(SIDES))),
        ],
        compiler_params=pltpu.CompilerParams(
            collective_id=0, has_side_effects=True, vmem_limit_bytes=VMEM_BYTES
        ),
    )(*blocks)
    outs = (
        jax.ShapeDtypeStruct((3, nx, ny, depth), f32),
        jax.ShapeDtypeStruct((6, nx, ny, depth), f32),
        jax.ShapeDtypeStruct((nx, ny, depth), f32),
    )
    return pl.pallas_call(
        functools.partial(stresses, sizes),
        out_shape=outs,
        in_specs=[vmem] * 2,
        out_specs=(hbm,) * 3,
        scratch_shapes=[
            pltpu.VMEM(outs[1].shape, f32),
            pltpu.VMEM(outs[2].shape, f32),
            pltpu.SemaphoreType.DMA((1 + 2 * (nx // ROWS_OUT),)),
        ],
        compiler_params=pltpu.CompilerParams(vmem_limit_bytes=VMEM_BYTES),
    )(field, cons)


def solution(mesh):
    in_specs = (
        P(None, "slab", "plane", None),
        P(None, "slab", "plane", None),
        P("slab", "plane", None),
        P(None, "slab", "plane", None),
        P("slab", "plane"),
        P("slab", "plane", None),
    )
    out_specs = (
        P(None, "slab", "plane", None),
        P(None, "slab", "plane", None),
        P("slab", "plane", None),
    )
    slabs, planes = mesh.shape["slab"], mesh.shape["plane"]

    def run(start_disp, load, shift, coarse, aggregate, consistency):
        sizes = (
            start_disp.shape[1] // slabs, start_disp.shape[2] // planes, start_disp.shape[3],
            coarse.shape[1] // slabs, coarse.shape[2] // planes, slabs, planes,
        )
        return jax.shard_map(
            functools.partial(body, sizes), mesh=mesh, in_specs=in_specs, out_specs=out_specs,
            check_vma=False,
        )(start_disp, load, shift, coarse, aggregate, consistency)

    return run
```

```python
import functools

import jax
import jax.numpy as jnp
from jax import lax
from jax.experimental import pallas as pl
from jax.experimental.pallas import tpu as pltpu
from jax.sharding import PartitionSpec as P

DEGREE = 4
THETA = 4.5
DELTA_C = 3.5
SIGMA = THETA / DELTA_C
MESH = pl.DeviceIdType.MESH
OFF = 8
SIDES = ((1, 1), (1, -1), (-1, 1), (-1, -1), (0, 1), (0, -1), (1, 0), (-1, 0))
VMEM_BYTES = 56 * 1024 * 1024
ROWS_OUT = 4
LOW_SIDES = ((0, 1), (1, 1), (1, 0))


def edge(step, first, count, width=1):
    if step > 0:
        return pl.ds(first + count - width, width), pl.ds(first - width, width)
    if step < 0:
        return pl.ds(first, width), pl.ds(first + count, width)
    return pl.ds(first, count), pl.ds(first, count)


def box_z(x):
    lane = lax.broadcasted_iota(jnp.int32, x.shape, x.ndim - 1)
    depth = x.shape[-1]
    below = jnp.where(lane == 0, 0.0, pltpu.roll(x, 1, x.ndim - 1))
    above = jnp.where(lane == depth - 1, 0.0, pltpu.roll(x, depth - 1, x.ndim - 1))
    return x + below + above


def next_z(x):
    return pltpu.roll(x, x.shape[-1] - 1, x.ndim - 1)


def previous_z(x):
    return pltpu.roll(x, 1, x.ndim - 1)


def smooth(sizes, *refs):
    nx, ny, depth, kx, ky, slabs, planes = sizes
    (start_hbm, load_hbm, shift_hbm, coarse_hbm, agg_hbm, cons_hbm, final, cons,
     start, load, shift, table, agg, earlier, resid, resid_sent, smoothed,
     in_sem, send_sem, recv_sem) = refs
    fields = [earlier.at[n] for n in range(DEGREE)]
    slab = lax.axis_index("slab")
    plane = lax.axis_index("plane")

    def exists(step_x, step_y):
        x, y = slab + step_x, plane + step_y
        return (x >= 0) & (x < slabs) & (y >= 0) & (y < planes)

    loads = [
        pltpu.make_async_copy(coarse_hbm, table.at[:, pl.ds(1, kx), pl.ds(0, ky)], in_sem.at[0]),
        pltpu.make_async_copy(agg_hbm, agg, in_sem.at[1]),
        pltpu.make_async_copy(start_hbm, start, in_sem.at[2]),
        pltpu.make_async_copy(cons_hbm, cons.at[pl.ds(1, nx), pl.ds(OFF, ny)], in_sem.at[3]),
        pltpu.make_async_copy(
            load_hbm, load.at[:, pl.ds(1, nx), pl.ds(OFF, ny)], in_sem.at[4]
        ),
        pltpu.make_async_copy(shift_hbm, shift.at[pl.ds(1, nx), pl.ds(OFF, ny)], in_sem.at[5]),
    ]
    for copy in loads:
        copy.start()

    zero_table = jnp.zeros((3, 8, depth), jnp.float32)
    for a in range(kx + 2):
        table[:, a, ky:ky + 8, :] = zero_table
    table[:, 0, 0:ky, :] = zero_table
    table[:, kx + 1, 0:ky, :] = zero_table

    for field in (fields[0], fields[2]):
        for i in range(nx + 4):
            if i < 2 or i >= nx + 2:
                field[:, i] = jnp.zeros((3, ny + 16, depth), jnp.float32)
            else:
                field[:, i, 0:OFF, :] = zero_table
                field[:, i, OFF + ny:OFF + ny + 8, :] = zero_table

    barrier = pltpu.get_barrier_semaphore()
    for step_x, step_y in SIDES:
        @pl.when(exists(step_x, step_y))
        def _():
            pl.semaphore_signal(
                barrier, inc=1, device_id=(slab + step_x, plane + step_y), device_id_type=MESH
            )

    near_x = 1 + (slab > 0).astype(jnp.int32) + (slab < slabs - 1).astype(jnp.int32)
    near_y = 1 + (plane > 0).astype(jnp.int32) + (plane < planes - 1).astype(jnp.int32)
    pl.semaphore_wait(barrier, near_x * near_y - 1)

    def remote(source, target, phase, side):
        step_x, step_y = SIDES[side]
        return pltpu.make_async_remote_copy(
            src_ref=source, dst_ref=target,
            send_sem=send_sem.at[phase, side], recv_sem=recv_sem.at[phase, side],
            device_id=(slab + step_x, plane + step_y), device_id_type=MESH,
        )

    def start_all(make, phase, sides=SIDES):
        for side, (step_x, step_y) in enumerate(SIDES):
            if (step_x, step_y) in sides:
                @pl.when(exists(step_x, step_y))
                def _():
                    remote(*make(step_x, step_y), phase, side).start()

    def wait_arrived(make, phase, sides=SIDES):
        for side, (step_x, step_y) in enumerate(SIDES):
            if (step_x, step_y) in sides:
                @pl.when(exists(-step_x, -step_y))
                def _():
                    remote(*make(step_x, step_y), phase, side).wait_recv()

    def wait_sent(make, phase, sides=SIDES):
        for side, (step_x, step_y) in enumerate(SIDES):
            if (step_x, step_y) in sides:
                @pl.when(exists(step_x, step_y))
                def _():
                    remote(*make(step_x, step_y), phase, side).wait_send()

    def coarse_edge(step_x, step_y):
        from_x, to_x = edge(step_x, 1, kx)
        from_y, to_y = edge(step_y, 0, ky)
        from_x = pl.ds(from_x.start - 1, from_x.size)
        if step_y > 0:
            to_y = pl.ds(ky + 7, 1)
        return coarse_hbm.at[:, from_x, from_y], table.at[:, to_x, to_y]

    def input_edge(source, target):
        lead = (slice(None),) * (len(source.shape) - 3)

        def make(step_x, step_y):
            from_x, to_x = edge(step_x, 1, nx)
            from_y, to_y = edge(step_y, OFF, ny)
            from_x = pl.ds(from_x.start - 1, from_x.size)
            from_y = pl.ds(from_y.start - OFF, from_y.size)
            return source.at[lead + (from_x, from_y)], target.at[lead + (to_x, to_y)]
        return make

    def field_edge(field, width):
        def make(step_x, step_y):
            from_x, to_x = edge(step_x, width, nx, width)
            from_y, to_y = edge(step_y, OFF, ny, width)
            return field.at[:, from_x, from_y], field.at[:, to_x, to_y]
        return make

    coarse_go = (coarse_edge, 0)
    load_go = (input_edge(load_hbm, load), 1)
    shift_go = (input_edge(shift_hbm, shift), 2)
    cons_go = (input_edge(cons_hbm, cons), 3, LOW_SIDES)
    first_go = (field_edge(fields[0], 2), 4)
    middle_go = (field_edge(fields[2], 2), 5)
    resid_go = (field_edge(resid_sent, 1), 6)

    def final_edge(step_x, step_y):
        from_x, to_x = edge(step_x, 1, nx)
        from_y, to_y = edge(step_y, OFF, ny)
        from_x = pl.ds(from_x.start - 1, from_x.size)
        from_y = pl.ds(from_y.start - OFF, from_y.size)
        return smoothed.at[:, from_x, from_y], final.at[:, to_x, to_y]

    final_go = (final_edge, 7)
    own_final = pltpu.make_async_copy(
        smoothed, final.at[:, pl.ds(1, nx), pl.ds(OFF, ny)], in_sem.at[6]
    )
    start_all(*coarse_go)
    start_all(*load_go)
    start_all(*shift_go)
    start_all(*cons_go)

    loads[1].wait()
    cols = ky * planes
    whole = agg[...]
    if cols & (cols - 1) == 0:
        row_a = lax.shift_right_logical(whole, cols.bit_length() - 1)
    else:
        row_a = lax.div(whole, cols)
    place = (row_a - (slab * kx - 1)) * (ky + 8)
    col_b = whole - row_a * cols - plane * ky
    place = (place + jnp.where(col_b < 0, ky + 7, col_b)).astype(jnp.float32)
    deep = (kx + 2) * (ky + 8)
    own = lax.broadcasted_iota(jnp.int32, (ny, ny), 0) == lax.broadcasted_iota(jnp.int32, (ny, ny), 1)
    slots = lax.broadcasted_iota(jnp.int32, (ny, deep), 1).astype(jnp.float32)
    picks = []
    for i in range(nx):
        column = jnp.sum(jnp.where(own, place[i:i + 1, :], 0.0), axis=1, keepdims=True)
        picks.append((column == slots).astype(jnp.bfloat16))
    pick = jnp.concatenate(picks, axis=0)
    loads[0].wait()
    loads[2].wait()
    wait_arrived(*coarse_go)
    for c in range(3):
        rest = table[c].reshape(deep, depth)
        moved = None
        for _ in range(3):
            part = rest.astype(jnp.bfloat16)
            rest = rest - part.astype(jnp.float32)
            piece = jnp.dot(pick, part, preferred_element_type=jnp.float32)
            moved = piece if moved is None else moved + piece
        fields[0][c, 2:nx + 2, OFF:OFF + ny, :] = start[c] + moved.reshape(nx, ny, depth)

    start_all(*first_go)
    loads[4].wait()
    loads[5].wait()
    wait_arrived(*load_go)
    wait_arrived(*shift_go)
    wait_arrived(*first_go)

    rows = nx // 2 + 1
    first_x, first_y = slab * nx, plane * ny
    lines = lax.broadcasted_iota(jnp.int32, (rows, ny + 8, depth), 1) + (first_y - 1)
    across = lax.broadcasted_iota(jnp.int32, (rows, ny + 8, depth), 0) + (first_x - 1)
    in_mesh_y = (lines >= 0) & (lines < ny * planes)

    def stencil(phase, c, first, count, top, tall):
        field = fields[phase]
        span = pl.ds(first - 1, count + 2)
        along_y = (
            field[c, span, pl.ds(top - 1, tall), :]
            + field[c, span, pl.ds(top, tall), :]
            + field[c, span, pl.ds(top + 1, tall), :]
        )
        boxed = box_z(along_y[:-2] + along_y[1:-1] + along_y[2:])
        centre = field[c, pl.ds(first, count), pl.ds(top, tall), :]
        here = shift[pl.ds(first - 1, count), pl.ds(top, tall), :]
        return centre, (3.0 + here) * centre - boxed * (1.0 / 3.0)

    rho = 1.0 / SIGMA
    keep, gain = 0.0, 1.0 / THETA
    for phase in range(DEGREE):
        if phase:
            rho_new = 1.0 / (2.0 * SIGMA - rho)
            keep, gain = rho_new * rho, 2.0 * rho_new / DELTA_C
            rho = rho_new
        if phase == 2:
            wait_arrived(*middle_go)
            wait_arrived(*resid_go)

        def wide(at, carry):
            c = at // 2
            first = 1 + (at % 2) * rows
            centre, applied = stencil(phase, c, first, rows, OFF - 1, ny + 8)
            where = (c, pl.ds(first - 1, rows), pl.ds(OFF - 1, ny + 8))
            left = (load if phase == 0 else resid_sent)[where] - applied
            direction = gain * left
            if phase:
                direction = direction + keep * centre
            node_x = across + (first - 1)
            inside = in_mesh_y & (node_x >= 0) & (node_x < nx * slabs)
            resid[where] = left
            fields[phase + 1][c, pl.ds(first, rows), pl.ds(OFF - 1, ny + 8), :] = jnp.where(
                inside, direction, 0.0
            )
            return carry

        def narrow(c, carry):
            centre, applied = stencil(phase, c, 2, nx, OFF, ny)
            where = (c, pl.ds(1, nx), pl.ds(OFF, ny))
            inner = (c, pl.ds(2, nx), pl.ds(OFF, ny))
            left = resid[where] - applied
            direction = keep * centre + gain * left
            if phase < DEGREE - 1:
                resid_sent[where] = left
                fields[phase + 1][inner] = direction
            else:
                for n in range(DEGREE):
                    direction = direction + fields[n][inner]
                smoothed[c] = direction
            return carry

        if phase % 2 == 0:
            lax.fori_loop(0, 6, wide, 0)
        else:
            lax.fori_loop(0, 3, narrow, 0)
        if phase == 1:
            start_all(*middle_go)
            start_all(*resid_go)
    start_all(*final_go)
    own_final.start()

    loads[3].wait()
    wait_arrived(*cons_go)
    for go in (coarse_go, load_go, shift_go, cons_go, first_go, middle_go, resid_go):
        wait_sent(*go)
    own_final.wait()
    wait_arrived(*final_go)
    wait_sent(*final_go)


def stresses(sizes, field_hbm, cons_hbm, disp_out, rec_out, ind_out,
             field, cons, rec, ind, in_sem, out_sem):
    nx, ny, depth, kx, ky, slabs, planes = sizes
    first_x = lax.axis_index("slab") * nx
    first_y = lax.axis_index("plane") * ny
    total_x, total_y = nx * slabs, ny * planes
    tall = ny + 8
    lane = lax.broadcasted_iota(jnp.int32, (tall, depth), 1)
    node_y = first_y - 1 + lax.broadcasted_iota(jnp.int32, (tall, depth), 0)
    valid_y = (node_y >= 0) & (node_y <= total_y - 2) & (lane <= depth - 2)
    lane = lax.broadcasted_iota(jnp.int32, (ny, depth), 1)
    node_y = first_y + lax.broadcasted_iota(jnp.int32, (ny, depth), 0)

    def half(ok):
        return jnp.where(ok, 0.5, 1.0)

    scale_y = half((node_y >= 1) & (node_y <= total_y - 2)) * half((lane >= 1) & (lane <= depth - 2))

    def arriving(n):
        lines = pl.ds(OFF - 1, ny + 2)
        nodes = pl.ds(n * ROWS_OUT + 2, ROWS_OUT) if n else pl.ds(0, ROWS_OUT + 2)
        corners = pl.ds(n * ROWS_OUT + 1, ROWS_OUT) if n else pl.ds(0, ROWS_OUT + 1)
        return (
            pltpu.make_async_copy(
                field_hbm.at[:, nodes, lines], field.at[:, nodes, lines], in_sem.at[2 * n]
            ),
            pltpu.make_async_copy(
                cons_hbm.at[corners, lines], cons.at[corners, lines], in_sem.at[2 * n + 1]
            ),
        )

    for n in range(nx // ROWS_OUT):
        for copy in arriving(n):
            copy.start()
    inner = field_hbm.at[:, pl.ds(1, nx), pl.ds(OFF, ny)]
    whole = pltpu.make_async_copy(inner, disp_out, out_sem.at[0])
    whole.start()

    def part(n):
        here = pl.ds(n * ROWS_OUT, ROWS_OUT)
        return (
            pltpu.make_async_copy(rec.at[:, here], rec_out.at[:, here], out_sem.at[1 + 2 * n]),
            pltpu.make_async_copy(ind.at[here], ind_out.at[here], out_sem.at[2 + 2 * n]),
        )

    def corner_sums(c, i):
        low = field[c, i, pl.ds(OFF - 1, tall), :]
        high = field[c, i, pl.ds(OFF, tall), :]
        return low + high, high - low

    def element_row(i):
        grad_x, grad_y, grad_z = [], [], []
        for c in range(3):
            sum_a, diff_a = corner_sums(c, i)
            sum_b, diff_b = corner_sums(c, i + 1)
            gx, gy, gz = sum_b - sum_a, diff_a + diff_b, sum_a + sum_b
            grad_x.append(0.25 * (gx + next_z(gx)))
            grad_y.append(0.25 * (gy + next_z(gy)))
            grad_z.append(0.25 * (next_z(gz) - gz))
        exx, eyy, ezz = grad_x[0], grad_y[1], grad_z[2]
        exy = 0.5 * (grad_y[0] + grad_x[1])
        eyz = 0.5 * (grad_z[1] + grad_y[2])
        ezx = 0.5 * (grad_x[2] + grad_z[0])
        trace = exx + eyy + ezz
        third = trace * (1.0 / 3.0)
        sxx, syy, szz = exx - third, eyy - third, ezz - third
        equiv = (2.0 / 3.0) * (
            sxx * sxx + syy * syy + szz * szz + 2.0 * (exy * exy + eyz * eyz + ezx * ezx)
        )
        visc = cons[i, pl.ds(OFF - 1, tall), :] * jnp.exp(-0.425 * jnp.log(0.01 + 3.0 * equiv))
        twice = 2.0 * visc
        bulk = 4.0 * trace
        sig = [twice * sxx + bulk, twice * syy + bulk, twice * szz + bulk,
               twice * exy, twice * eyz, twice * ezx]
        norm_sq = (
            sig[0] * sig[0] + sig[1] * sig[1] + sig[2] * sig[2]
            + 2.0 * (sig[3] * sig[3] + sig[4] * sig[4] + sig[5] * sig[5])
        )
        node_x = first_x - 1 + i
        valid = valid_y & (node_x >= 0) & (node_x <= total_x - 2)
        summed = []
        for one in sig + [norm_sq]:
            one = jnp.where(valid, one, 0.0)
            one = one[0:ny] + one[1:ny + 1]
            summed.append(one + previous_z(one))
        return tuple(summed)

    def row(i, before):
        after = element_row(i)
        node_x = first_x + i - 1
        inside = ((node_x >= 1) & (node_x <= total_x - 2)).astype(jnp.float32)
        scale = scale_y * (1.0 - 0.5 * inside)
        total = [(a + b) * scale for a, b in zip(before, after)]
        for n in range(6):
            rec[n, i - 1] = total[n]
        ind[i - 1] = total[6] - (
            total[0] * total[0] + total[1] * total[1] + total[2] * total[2]
            + 2.0 * (total[3] * total[3] + total[4] * total[4] + total[5] * total[5])
        )
        return after

    carry = None
    for n in range(nx // ROWS_OUT):
        for copy in arriving(n):
            copy.wait()
        if n == 0:
            carry = element_row(0)
        carry = lax.fori_loop(1 + n * ROWS_OUT, 1 + (n + 1) * ROWS_OUT, row, carry, unroll=True)
        for copy in part(n):
            copy.start()
    whole.wait()
    for n in range(nx // ROWS_OUT):
        for copy in part(n):
            copy.wait()


def body(sizes, *blocks):
    nx, ny, depth, kx, ky, slabs, planes = sizes
    hbm = pl.BlockSpec(memory_space=pltpu.HBM)
    f32 = jnp.float32
    padded = (
        jax.ShapeDtypeStruct((3, nx + 2, ny + 16, depth), f32),
        jax.ShapeDtypeStruct((nx + 1, ny + 16, depth), f32),
    )
    field, cons = pl.pallas_call(
        functools.partial(smooth, sizes),
        out_shape=padded,
        in_specs=[hbm] * 6,
        out_specs=(hbm,) * 2,
        scratch_shapes=[
            pltpu.VMEM((3, nx, ny, depth), f32),
            pltpu.VMEM((3, nx + 2, ny + 16, depth), f32),
            pltpu.VMEM((nx + 2, ny + 16, depth), f32),
            pltpu.VMEM((3, kx + 2, ky + 8, depth), f32),
            pltpu.VMEM((nx, ny), jnp.int32),
            pltpu.VMEM((DEGREE, 3, nx + 4, ny + 16, depth), f32),
            pltpu.VMEM((3, nx + 2, ny + 16, depth), f32),
            pltpu.VMEM((3, nx + 2, ny + 16, depth), f32),
            pltpu.VMEM((3, nx, ny, depth), f32),
            pltpu.SemaphoreType.DMA((7,)),
            pltpu.SemaphoreType.DMA((8, len(SIDES))),
            pltpu.SemaphoreType.DMA((8, len(SIDES))),
        ],
        compiler_params=pltpu.CompilerParams(
            collective_id=0, has_side_effects=True, vmem_limit_bytes=VMEM_BYTES
        ),
    )(*blocks)
    outs = (
        jax.ShapeDtypeStruct((3, nx, ny, depth), f32),
        jax.ShapeDtypeStruct((6, nx, ny, depth), f32),
        jax.ShapeDtypeStruct((nx, ny, depth), f32),
    )
    return pl.pallas_call(
        functools.partial(stresses, sizes),
        out_shape=outs,
        in_specs=[hbm] * 2,
        out_specs=(hbm,) * 3,
        scratch_shapes=[
            pltpu.VMEM(padded[0].shape, f32),
            pltpu.VMEM(padded[1].shape, f32),
            pltpu.VMEM(outs[1].shape, f32),
            pltpu.VMEM(outs[2].shape, f32),
            pltpu.SemaphoreType.DMA((2 * (nx // ROWS_OUT),)),
            pltpu.SemaphoreType.DMA((1 + 2 * (nx // ROWS_OUT),)),
        ],
        compiler_params=pltpu.CompilerParams(vmem_limit_bytes=VMEM_BYTES),
    )(field, cons)


def solution(mesh):
    in_specs = (
        P(None, "slab", "plane", None),
        P(None, "slab", "plane", None),
        P("slab", "plane", None),
        P(None, "slab", "plane", None),
        P("slab", "plane"),
        P("slab", "plane", None),
    )
    out_specs = (
        P(None, "slab", "plane", None),
        P(None, "slab", "plane", None),
        P("slab", "plane", None),
    )
    slabs, planes = mesh.shape["slab"], mesh.shape["plane"]

    def run(start_disp, load, shift, coarse, aggregate, consistency):
        sizes = (
            start_disp.shape[1] // slabs, start_disp.shape[2] // planes, start_disp.shape[3],
            coarse.shape[1] // slabs, coarse.shape[2] // planes, slabs, planes,
        )
        return jax.shard_map(
            functools.partial(body, sizes), mesh=mesh, in_specs=in_specs, out_specs=out_specs,
            check_vma=False,
        )(start_disp, load, shift, coarse, aggregate, consistency)

    return run
```

```python
import functools

import jax
import jax.numpy as jnp
from jax import lax
from jax.experimental import pallas as pl
from jax.experimental.pallas import tpu as pltpu
from jax.sharding import PartitionSpec as P

DEGREE = 4
THETA = 4.5
DELTA_C = 3.5
SIGMA = THETA / DELTA_C
MESH = pl.DeviceIdType.MESH
OFF = 8
SIDES = ((1, 1), (1, -1), (-1, 1), (-1, -1), (0, 1), (0, -1), (1, 0), (-1, 0))
VMEM_BYTES = 56 * 1024 * 1024
ROWS_OUT = 4
LOW_SIDES = ((0, 1), (1, 1), (1, 0))


def edge(step, first, count, width=1):
    if step > 0:
        return pl.ds(first + count - width, width), pl.ds(first - width, width)
    if step < 0:
        return pl.ds(first, width), pl.ds(first + count, width)
    return pl.ds(first, count), pl.ds(first, count)


def box_z(x):
    lane = lax.broadcasted_iota(jnp.int32, x.shape, x.ndim - 1)
    depth = x.shape[-1]
    below = jnp.where(lane == 0, 0.0, pltpu.roll(x, 1, x.ndim - 1))
    above = jnp.where(lane == depth - 1, 0.0, pltpu.roll(x, depth - 1, x.ndim - 1))
    return x + below + above


def next_z(x):
    return pltpu.roll(x, x.shape[-1] - 1, x.ndim - 1)


def previous_z(x):
    return pltpu.roll(x, 1, x.ndim - 1)


def smooth(sizes, *refs):
    nx, ny, depth, kx, ky, slabs, planes = sizes
    (start_hbm, load_hbm, shift_hbm, coarse_hbm, agg_hbm, cons_hbm, final, cons,
     start, load, shift, table, agg, earlier, resid, resid_sent, smoothed,
     in_sem, send_sem, recv_sem) = refs
    fields = [earlier.at[n] for n in range(DEGREE)]
    slab = lax.axis_index("slab")
    plane = lax.axis_index("plane")

    def exists(step_x, step_y):
        x, y = slab + step_x, plane + step_y
        return (x >= 0) & (x < slabs) & (y >= 0) & (y < planes)

    loads = [
        pltpu.make_async_copy(coarse_hbm, table.at[:, pl.ds(1, kx), pl.ds(0, ky)], in_sem.at[0]),
        pltpu.make_async_copy(agg_hbm, agg, in_sem.at[1]),
        pltpu.make_async_copy(start_hbm, start, in_sem.at[2]),
        pltpu.make_async_copy(cons_hbm, cons.at[pl.ds(1, nx), pl.ds(OFF, ny)], in_sem.at[3]),
        pltpu.make_async_copy(
            load_hbm, load.at[:, pl.ds(1, nx), pl.ds(OFF, ny)], in_sem.at[4]
        ),
        pltpu.make_async_copy(shift_hbm, shift.at[pl.ds(1, nx), pl.ds(OFF, ny)], in_sem.at[5]),
    ]
    for copy in loads:
        copy.start()

    zero_table = jnp.zeros((3, 8, depth), jnp.float32)
    for a in range(kx + 2):
        table[:, a, ky:ky + 8, :] = zero_table
    table[:, 0, 0:ky, :] = zero_table
    table[:, kx + 1, 0:ky, :] = zero_table

    for field in (fields[0], fields[2]):
        for i in range(nx + 4):
            if i < 2 or i >= nx + 2:
                field[:, i] = jnp.zeros((3, ny + 16, depth), jnp.float32)
            else:
                field[:, i, 0:OFF, :] = zero_table
                field[:, i, OFF + ny:OFF + ny + 8, :] = zero_table

    barrier = pltpu.get_barrier_semaphore()
    for step_x, step_y in SIDES:
        @pl.when(exists(step_x, step_y))
        def _():
            pl.semaphore_signal(
                barrier, inc=1, device_id=(slab + step_x, plane + step_y), device_id_type=MESH
            )

    near_x = 1 + (slab > 0).astype(jnp.int32) + (slab < slabs - 1).astype(jnp.int32)
    near_y = 1 + (plane > 0).astype(jnp.int32) + (plane < planes - 1).astype(jnp.int32)
    pl.semaphore_wait(barrier, near_x * near_y - 1)

    def remote(source, target, phase, side):
        step_x, step_y = SIDES[side]
        return pltpu.make_async_remote_copy(
            src_ref=source, dst_ref=target,
            send_sem=send_sem.at[phase, side], recv_sem=recv_sem.at[phase, side],
            device_id=(slab + step_x, plane + step_y), device_id_type=MESH,
        )

    def start_all(make, phase, sides=SIDES):
        for side, (step_x, step_y) in enumerate(SIDES):
            if (step_x, step_y) in sides:
                @pl.when(exists(step_x, step_y))
                def _():
                    remote(*make(step_x, step_y), phase, side).start()

    def wait_arrived(make, phase, sides=SIDES):
        for side, (step_x, step_y) in enumerate(SIDES):
            if (step_x, step_y) in sides:
                @pl.when(exists(-step_x, -step_y))
                def _():
                    remote(*make(step_x, step_y), phase, side).wait_recv()

    def wait_sent(make, phase, sides=SIDES):
        for side, (step_x, step_y) in enumerate(SIDES):
            if (step_x, step_y) in sides:
                @pl.when(exists(step_x, step_y))
                def _():
                    remote(*make(step_x, step_y), phase, side).wait_send()

    def coarse_edge(step_x, step_y):
        from_x, to_x = edge(step_x, 1, kx)
        from_y, to_y = edge(step_y, 0, ky)
        from_x = pl.ds(from_x.start - 1, from_x.size)
        if step_y > 0:
            to_y = pl.ds(ky + 7, 1)
        return coarse_hbm.at[:, from_x, from_y], table.at[:, to_x, to_y]

    def input_edge(source, target):
        lead = (slice(None),) * (len(source.shape) - 3)

        def make(step_x, step_y):
            from_x, to_x = edge(step_x, 1, nx)
            from_y, to_y = edge(step_y, OFF, ny)
            from_x = pl.ds(from_x.start - 1, from_x.size)
            from_y = pl.ds(from_y.start - OFF, from_y.size)
            return source.at[lead + (from_x, from_y)], target.at[lead + (to_x, to_y)]
        return make

    def field_edge(field, width):
        def make(step_x, step_y):
            from_x, to_x = edge(step_x, width, nx, width)
            from_y, to_y = edge(step_y, OFF, ny, width)
            return field.at[:, from_x, from_y], field.at[:, to_x, to_y]
        return make

    coarse_go = (coarse_edge, 0)
    load_go = (input_edge(load_hbm, load), 1)
    shift_go = (input_edge(shift_hbm, shift), 2)
    cons_go = (input_edge(cons_hbm, cons), 3, LOW_SIDES)
    first_go = (field_edge(fields[0], 2), 4)
    middle_go = (field_edge(fields[2], 2), 5)
    resid_go = (field_edge(resid_sent, 1), 6)

    def final_edge(step_x, step_y):
        from_x, to_x = edge(step_x, 1, nx)
        from_y, to_y = edge(step_y, OFF, ny)
        from_x = pl.ds(from_x.start - 1, from_x.size)
        from_y = pl.ds(from_y.start - OFF, from_y.size)
        return smoothed.at[:, from_x, from_y], final.at[:, to_x, to_y]

    final_go = (final_edge, 7)
    own_final = pltpu.make_async_copy(
        smoothed, final.at[:, pl.ds(1, nx), pl.ds(OFF, ny)], in_sem.at[6]
    )
    start_all(*coarse_go)
    start_all(*load_go)
    start_all(*shift_go)
    start_all(*cons_go)

    loads[1].wait()
    cols = ky * planes
    whole = agg[...]
    if cols & (cols - 1) == 0:
        row_a = lax.shift_right_logical(whole, cols.bit_length() - 1)
    else:
        row_a = lax.div(whole, cols)
    place = (row_a - (slab * kx - 1)) * (ky + 8)
    col_b = whole - row_a * cols - plane * ky
    place = (place + jnp.where(col_b < 0, ky + 7, col_b)).astype(jnp.float32)
    deep = (kx + 2) * (ky + 8)
    own = lax.broadcasted_iota(jnp.int32, (ny, ny), 0) == lax.broadcasted_iota(jnp.int32, (ny, ny), 1)
    slots = lax.broadcasted_iota(jnp.int32, (ny, deep), 1).astype(jnp.float32)
    picks = []
    for i in range(nx):
        column = jnp.sum(jnp.where(own, place[i:i + 1, :], 0.0), axis=1, keepdims=True)
        picks.append((column == slots).astype(jnp.bfloat16))
    pick = jnp.concatenate(picks, axis=0)
    loads[0].wait()
    loads[2].wait()
    wait_arrived(*coarse_go)
    for c in range(3):
        rest = table[c].reshape(deep, depth)
        moved = None
        for _ in range(3):
            part = rest.astype(jnp.bfloat16)
            rest = rest - part.astype(jnp.float32)
            piece = jnp.dot(pick, part, preferred_element_type=jnp.float32)
            moved = piece if moved is None else moved + piece
        fields[0][c, 2:nx + 2, OFF:OFF + ny, :] = start[c] + moved.reshape(nx, ny, depth)

    start_all(*first_go)
    loads[4].wait()
    loads[5].wait()
    wait_arrived(*load_go)
    wait_arrived(*shift_go)
    wait_arrived(*first_go)

    rows = nx // 2 + 1
    first_x, first_y = slab * nx, plane * ny
    lines = lax.broadcasted_iota(jnp.int32, (rows, ny + 8, depth), 1) + (first_y - 1)
    across = lax.broadcasted_iota(jnp.int32, (rows, ny + 8, depth), 0) + (first_x - 1)
    in_mesh_y = (lines >= 0) & (lines < ny * planes)

    def stencil(phase, c, first, count, top, tall):
        field = fields[phase]
        span = pl.ds(first - 1, count + 2)
        along_y = (
            field[c, span, pl.ds(top - 1, tall), :]
            + field[c, span, pl.ds(top, tall), :]
            + field[c, span, pl.ds(top + 1, tall), :]
        )
        boxed = box_z(along_y[:-2] + along_y[1:-1] + along_y[2:])
        centre = field[c, pl.ds(first, count), pl.ds(top, tall), :]
        here = shift[pl.ds(first - 1, count), pl.ds(top, tall), :]
        return centre, (3.0 + here) * centre - boxed * (1.0 / 3.0)

    rho = 1.0 / SIGMA
    keep, gain = 0.0, 1.0 / THETA
    for phase in range(DEGREE):
        if phase:
            rho_new = 1.0 / (2.0 * SIGMA - rho)
            keep, gain = rho_new * rho, 2.0 * rho_new / DELTA_C
            rho = rho_new
        if phase == 2:
            wait_arrived(*middle_go)
            wait_arrived(*resid_go)

        def wide(at, carry):
            c = at // 2
            first = 1 + (at % 2) * rows
            centre, applied = stencil(phase, c, first, rows, OFF - 1, ny + 8)
            where = (c, pl.ds(first - 1, rows), pl.ds(OFF - 1, ny + 8))
            left = (load if phase == 0 else resid_sent)[where] - applied
            direction = gain * left
            if phase:
                direction = direction + keep * centre
            node_x = across + (first - 1)
            inside = in_mesh_y & (node_x >= 0) & (node_x < nx * slabs)
            resid[where] = left
            fields[phase + 1][c, pl.ds(first, rows), pl.ds(OFF - 1, ny + 8), :] = jnp.where(
                inside, direction, 0.0
            )
            return carry

        def narrow(c, carry):
            centre, applied = stencil(phase, c, 2, nx, OFF, ny)
            where = (c, pl.ds(1, nx), pl.ds(OFF, ny))
            inner = (c, pl.ds(2, nx), pl.ds(OFF, ny))
            left = resid[where] - applied
            direction = keep * centre + gain * left
            if phase < DEGREE - 1:
                resid_sent[where] = left
                fields[phase + 1][inner] = direction
            else:
                for n in range(DEGREE):
                    direction = direction + fields[n][inner]
                smoothed[c] = direction
            return carry

        if phase % 2 == 0:
            lax.fori_loop(0, 6, wide, 0)
        else:
            lax.fori_loop(0, 3, narrow, 0)
        if phase == 1:
            start_all(*middle_go)
            start_all(*resid_go)
    start_all(*final_go)
    own_final.start()

    loads[3].wait()
    wait_arrived(*cons_go)
    for go in (coarse_go, load_go, shift_go, cons_go, first_go, middle_go, resid_go):
        wait_sent(*go)
    own_final.wait()
    wait_arrived(*final_go)
    wait_sent(*final_go)


def stresses(sizes, field_hbm, cons_hbm, disp_out, rec_out, ind_out,
             field, cons, rec, ind, in_sem, out_sem):
    nx, ny, depth, kx, ky, slabs, planes = sizes
    first_x = lax.axis_index("slab") * nx
    first_y = lax.axis_index("plane") * ny
    total_x, total_y = nx * slabs, ny * planes
    tall = ny + 8
    lane = lax.broadcasted_iota(jnp.int32, (tall, depth), 1)
    node_y = first_y - 1 + lax.broadcasted_iota(jnp.int32, (tall, depth), 0)
    valid_y = (node_y >= 0) & (node_y <= total_y - 2) & (lane <= depth - 2)
    lane = lax.broadcasted_iota(jnp.int32, (ny, depth), 1)
    node_y = first_y + lax.broadcasted_iota(jnp.int32, (ny, depth), 0)

    def half(ok):
        return jnp.where(ok, 0.5, 1.0)

    scale_y = half((node_y >= 1) & (node_y <= total_y - 2)) * half((lane >= 1) & (lane <= depth - 2))

    def arriving(n):
        lines = pl.ds(OFF - 1, ny + 2)
        nodes = pl.ds(n * ROWS_OUT + 2, ROWS_OUT) if n else pl.ds(0, ROWS_OUT + 2)
        corners = pl.ds(n * ROWS_OUT + 1, ROWS_OUT) if n else pl.ds(0, ROWS_OUT + 1)
        return (
            pltpu.make_async_copy(
                field_hbm.at[:, nodes, lines], field.at[:, nodes, lines], in_sem.at[2 * n]
            ),
            pltpu.make_async_copy(
                cons_hbm.at[corners, lines], cons.at[corners, lines], in_sem.at[2 * n + 1]
            ),
        )

    for n in range(nx // ROWS_OUT):
        for copy in arriving(n):
            copy.start()

    def displaced(n):
        return pltpu.make_async_copy(
            field.at[:, pl.ds(n * ROWS_OUT + 1, ROWS_OUT), pl.ds(OFF, ny)],
            disp_out.at[:, pl.ds(n * ROWS_OUT, ROWS_OUT)], out_sem.at[3 * n],
        )

    def part(n):
        here = pl.ds(n * ROWS_OUT, ROWS_OUT)
        return (
            pltpu.make_async_copy(rec.at[:, here], rec_out.at[:, here], out_sem.at[3 * n + 1]),
            pltpu.make_async_copy(ind.at[here], ind_out.at[here], out_sem.at[3 * n + 2]),
        )

    def corner_sums(c, i):
        low = field[c, i, pl.ds(OFF - 1, tall), :]
        high = field[c, i, pl.ds(OFF, tall), :]
        return low + high, high - low

    def element_row(i):
        grad_x, grad_y, grad_z = [], [], []
        for c in range(3):
            sum_a, diff_a = corner_sums(c, i)
            sum_b, diff_b = corner_sums(c, i + 1)
            gx, gy, gz = sum_b - sum_a, diff_a + diff_b, sum_a + sum_b
            grad_x.append(0.25 * (gx + next_z(gx)))
            grad_y.append(0.25 * (gy + next_z(gy)))
            grad_z.append(0.25 * (next_z(gz) - gz))
        exx, eyy, ezz = grad_x[0], grad_y[1], grad_z[2]
        exy = 0.5 * (grad_y[0] + grad_x[1])
        eyz = 0.5 * (grad_z[1] + grad_y[2])
        ezx = 0.5 * (grad_x[2] + grad_z[0])
        trace = exx + eyy + ezz
        third = trace * (1.0 / 3.0)
        sxx, syy, szz = exx - third, eyy - third, ezz - third
        equiv = (2.0 / 3.0) * (
            sxx * sxx + syy * syy + szz * szz + 2.0 * (exy * exy + eyz * eyz + ezx * ezx)
        )
        visc = cons[i, pl.ds(OFF - 1, tall), :] * jnp.exp(-0.425 * jnp.log(0.01 + 3.0 * equiv))
        twice = 2.0 * visc
        bulk = 4.0 * trace
        sig = [twice * sxx + bulk, twice * syy + bulk, twice * szz + bulk,
               twice * exy, twice * eyz, twice * ezx]
        norm_sq = (
            sig[0] * sig[0] + sig[1] * sig[1] + sig[2] * sig[2]
            + 2.0 * (sig[3] * sig[3] + sig[4] * sig[4] + sig[5] * sig[5])
        )
        node_x = first_x - 1 + i
        valid = valid_y & (node_x >= 0) & (node_x <= total_x - 2)
        summed = []
        for one in sig + [norm_sq]:
            one = jnp.where(valid, one, 0.0)
            one = one[0:ny] + one[1:ny + 1]
            summed.append(one + previous_z(one))
        return tuple(summed)

    def row(i, before):
        after = element_row(i)
        node_x = first_x + i - 1
        inside = ((node_x >= 1) & (node_x <= total_x - 2)).astype(jnp.float32)
        scale = scale_y * (1.0 - 0.5 * inside)
        total = [(a + b) * scale for a, b in zip(before, after)]
        for n in range(6):
            rec[n, i - 1] = total[n]
        ind[i - 1] = total[6] - (
            total[0] * total[0] + total[1] * total[1] + total[2] * total[2]
            + 2.0 * (total[3] * total[3] + total[4] * total[4] + total[5] * total[5])
        )
        return after

    carry = None
    for n in range(nx // ROWS_OUT):
        for copy in arriving(n):
            copy.wait()
        displaced(n).start()
        if n == 0:
            carry = element_row(0)
        carry = lax.fori_loop(1 + n * ROWS_OUT, 1 + (n + 1) * ROWS_OUT, row, carry, unroll=True)
        for copy in part(n):
            copy.start()
    for n in range(nx // ROWS_OUT):
        displaced(n).wait()
        for copy in part(n):
            copy.wait()


def body(sizes, *blocks):
    nx, ny, depth, kx, ky, slabs, planes = sizes
    hbm = pl.BlockSpec(memory_space=pltpu.HBM)
    f32 = jnp.float32
    padded = (
        jax.ShapeDtypeStruct((3, nx + 2, ny + 16, depth), f32),
        jax.ShapeDtypeStruct((nx + 1, ny + 16, depth), f32),
    )
    field, cons = pl.pallas_call(
        functools.partial(smooth, sizes),
        out_shape=padded,
        in_specs=[hbm] * 6,
        out_specs=(hbm,) * 2,
        scratch_shapes=[
            pltpu.VMEM((3, nx, ny, depth), f32),
            pltpu.VMEM((3, nx + 2, ny + 16, depth), f32),
            pltpu.VMEM((nx + 2, ny + 16, depth), f32),
            pltpu.VMEM((3, kx + 2, ky + 8, depth), f32),
            pltpu.VMEM((nx, ny), jnp.int32),
            pltpu.VMEM((DEGREE, 3, nx + 4, ny + 16, depth), f32),
            pltpu.VMEM((3, nx + 2, ny + 16, depth), f32),
            pltpu.VMEM((3, nx + 2, ny + 16, depth), f32),
            pltpu.VMEM((3, nx, ny, depth), f32),
            pltpu.SemaphoreType.DMA((7,)),
            pltpu.SemaphoreType.DMA((8, len(SIDES))),
            pltpu.SemaphoreType.DMA((8, len(SIDES))),
        ],
        compiler_params=pltpu.CompilerParams(
            collective_id=0, has_side_effects=True, vmem_limit_bytes=VMEM_BYTES
        ),
    )(*blocks)
    outs = (
        jax.ShapeDtypeStruct((3, nx, ny, depth), f32),
        jax.ShapeDtypeStruct((6, nx, ny, depth), f32),
        jax.ShapeDtypeStruct((nx, ny, depth), f32),
    )
    return pl.pallas_call(
        functools.partial(stresses, sizes),
        out_shape=outs,
        in_specs=[hbm] * 2,
        out_specs=(hbm,) * 3,
        scratch_shapes=[
            pltpu.VMEM(padded[0].shape, f32),
            pltpu.VMEM(padded[1].shape, f32),
            pltpu.VMEM(outs[1].shape, f32),
            pltpu.VMEM(outs[2].shape, f32),
            pltpu.SemaphoreType.DMA((2 * (nx // ROWS_OUT),)),
            pltpu.SemaphoreType.DMA((3 * (nx // ROWS_OUT),)),
        ],
        compiler_params=pltpu.CompilerParams(vmem_limit_bytes=VMEM_BYTES),
    )(field, cons)


def solution(mesh):
    in_specs = (
        P(None, "slab", "plane", None),
        P(None, "slab", "plane", None),
        P("slab", "plane", None),
        P(None, "slab", "plane", None),
        P("slab", "plane"),
        P("slab", "plane", None),
    )
    out_specs = (
        P(None, "slab", "plane", None),
        P(None, "slab", "plane", None),
        P("slab", "plane", None),
    )
    slabs, planes = mesh.shape["slab"], mesh.shape["plane"]

    def run(start_disp, load, shift, coarse, aggregate, consistency):
        sizes = (
            start_disp.shape[1] // slabs, start_disp.shape[2] // planes, start_disp.shape[3],
            coarse.shape[1] // slabs, coarse.shape[2] // planes, slabs, planes,
        )
        return jax.shard_map(
            functools.partial(body, sizes), mesh=mesh, in_specs=in_specs, out_specs=out_specs,
            check_vma=False,
        )(start_disp, load, shift, coarse, aggregate, consistency)

    return run
```

```python
import functools

import jax
import jax.numpy as jnp
from jax import lax
from jax.experimental import pallas as pl
from jax.experimental.pallas import tpu as pltpu
from jax.sharding import PartitionSpec as P

DEGREE = 4
THETA = 4.5
DELTA_C = 3.5
SIGMA = THETA / DELTA_C
MESH = pl.DeviceIdType.MESH
OFF = 8
SIDES = ((1, 1), (1, -1), (-1, 1), (-1, -1), (0, 1), (0, -1), (1, 0), (-1, 0))
VMEM_BYTES = 56 * 1024 * 1024
ROWS_OUT = 4
LOW_SIDES = ((0, 1), (1, 1), (1, 0))


def edge(step, first, count, width=1):
    if step > 0:
        return pl.ds(first + count - width, width), pl.ds(first - width, width)
    if step < 0:
        return pl.ds(first, width), pl.ds(first + count, width)
    return pl.ds(first, count), pl.ds(first, count)


def box_z(x):
    lane = lax.broadcasted_iota(jnp.int32, x.shape, x.ndim - 1)
    depth = x.shape[-1]
    below = jnp.where(lane == 0, 0.0, pltpu.roll(x, 1, x.ndim - 1))
    above = jnp.where(lane == depth - 1, 0.0, pltpu.roll(x, depth - 1, x.ndim - 1))
    return x + below + above


def next_z(x):
    return pltpu.roll(x, x.shape[-1] - 1, x.ndim - 1)


def previous_z(x):
    return pltpu.roll(x, 1, x.ndim - 1)


def smooth(sizes, *refs):
    nx, ny, depth, kx, ky, slabs, planes = sizes
    (start_hbm, load_hbm, shift_hbm, coarse_hbm, agg_hbm, cons_hbm, final, cons,
     start, load, shift, table, agg, earlier, resid, resid_sent, smoothed,
     in_sem, send_sem, recv_sem) = refs
    fields = [earlier.at[n] for n in range(DEGREE)]
    slab = lax.axis_index("slab")
    plane = lax.axis_index("plane")

    def exists(step_x, step_y):
        x, y = slab + step_x, plane + step_y
        return (x >= 0) & (x < slabs) & (y >= 0) & (y < planes)

    loads = [
        pltpu.make_async_copy(coarse_hbm, table.at[:, pl.ds(1, kx), pl.ds(0, ky)], in_sem.at[0]),
        pltpu.make_async_copy(agg_hbm, agg, in_sem.at[1]),
        pltpu.make_async_copy(start_hbm, start, in_sem.at[2]),
        pltpu.make_async_copy(cons_hbm, cons.at[pl.ds(1, nx), pl.ds(OFF, ny)], in_sem.at[3]),
        pltpu.make_async_copy(
            load_hbm, load.at[:, pl.ds(1, nx), pl.ds(OFF, ny)], in_sem.at[4]
        ),
        pltpu.make_async_copy(shift_hbm, shift.at[pl.ds(1, nx), pl.ds(OFF, ny)], in_sem.at[5]),
    ]
    for n in (0, 1, 2, 4, 5, 3):
        loads[n].start()

    zero_table = jnp.zeros((3, 8, depth), jnp.float32)
    for a in range(kx + 2):
        table[:, a, ky:ky + 8, :] = zero_table
    table[:, 0, 0:ky, :] = zero_table
    table[:, kx + 1, 0:ky, :] = zero_table

    for field in (fields[0], fields[2]):
        for i in range(nx + 4):
            if i < 2 or i >= nx + 2:
                field[:, i] = jnp.zeros((3, ny + 16, depth), jnp.float32)
            else:
                field[:, i, 0:OFF, :] = zero_table
                field[:, i, OFF + ny:OFF + ny + 8, :] = zero_table

    barrier = pltpu.get_barrier_semaphore()
    for step_x, step_y in SIDES:
        @pl.when(exists(step_x, step_y))
        def _():
            pl.semaphore_signal(
                barrier, inc=1, device_id=(slab + step_x, plane + step_y), device_id_type=MESH
            )

    near_x = 1 + (slab > 0).astype(jnp.int32) + (slab < slabs - 1).astype(jnp.int32)
    near_y = 1 + (plane > 0).astype(jnp.int32) + (plane < planes - 1).astype(jnp.int32)
    pl.semaphore_wait(barrier, near_x * near_y - 1)

    def remote(source, target, phase, side):
        step_x, step_y = SIDES[side]
        return pltpu.make_async_remote_copy(
            src_ref=source, dst_ref=target,
            send_sem=send_sem.at[phase, side], recv_sem=recv_sem.at[phase, side],
            device_id=(slab + step_x, plane + step_y), device_id_type=MESH,
        )

    def start_all(make, phase, sides=SIDES):
        for side, (step_x, step_y) in enumerate(SIDES):
            if (step_x, step_y) in sides:
                @pl.when(exists(step_x, step_y))
                def _():
                    remote(*make(step_x, step_y), phase, side).start()

    def wait_arrived(make, phase, sides=SIDES):
        for side, (step_x, step_y) in enumerate(SIDES):
            if (step_x, step_y) in sides:
                @pl.when(exists(-step_x, -step_y))
                def _():
                    remote(*make(step_x, step_y), phase, side).wait_recv()

    def wait_sent(make, phase, sides=SIDES):
        for side, (step_x, step_y) in enumerate(SIDES):
            if (step_x, step_y) in sides:
                @pl.when(exists(step_x, step_y))
                def _():
                    remote(*make(step_x, step_y), phase, side).wait_send()

    def coarse_edge(step_x, step_y):
        from_x, to_x = edge(step_x, 1, kx)
        from_y, to_y = edge(step_y, 0, ky)
        from_x = pl.ds(from_x.start - 1, from_x.size)
        if step_y > 0:
            to_y = pl.ds(ky + 7, 1)
        return coarse_hbm.at[:, from_x, from_y], table.at[:, to_x, to_y]

    def input_edge(source, target):
        lead = (slice(None),) * (len(source.shape) - 3)

        def make(step_x, step_y):
            from_x, to_x = edge(step_x, 1, nx)
            from_y, to_y = edge(step_y, OFF, ny)
            from_x = pl.ds(from_x.start - 1, from_x.size)
            from_y = pl.ds(from_y.start - OFF, from_y.size)
            return source.at[lead + (from_x, from_y)], target.at[lead + (to_x, to_y)]
        return make

    def field_edge(field, width):
        def make(step_x, step_y):
            from_x, to_x = edge(step_x, width, nx, width)
            from_y, to_y = edge(step_y, OFF, ny, width)
            return field.at[:, from_x, from_y], field.at[:, to_x, to_y]
        return make

    coarse_go = (coarse_edge, 0)
    load_go = (input_edge(load_hbm, load), 1)
    shift_go = (input_edge(shift_hbm, shift), 2)
    cons_go = (input_edge(cons_hbm, cons), 3, LOW_SIDES)
    first_go = (field_edge(fields[0], 2), 4)
    middle_go = (field_edge(fields[2], 2), 5)
    resid_go = (field_edge(resid_sent, 1), 6)

    def final_edge(step_x, step_y):
        from_x, to_x = edge(step_x, 1, nx)
        from_y, to_y = edge(step_y, OFF, ny)
        from_x = pl.ds(from_x.start - 1, from_x.size)
        from_y = pl.ds(from_y.start - OFF, from_y.size)
        return smoothed.at[:, from_x, from_y], final.at[:, to_x, to_y]

    final_go = (final_edge, 7)
    own_final = pltpu.make_async_copy(
        smoothed, final.at[:, pl.ds(1, nx), pl.ds(OFF, ny)], in_sem.at[6]
    )
    start_all(*coarse_go)
    start_all(*load_go)
    start_all(*shift_go)
    start_all(*cons_go)

    loads[1].wait()
    cols = ky * planes
    whole = agg[...]
    if cols & (cols - 1) == 0:
        row_a = lax.shift_right_logical(whole, cols.bit_length() - 1)
    else:
        row_a = lax.div(whole, cols)
    place = (row_a - (slab * kx - 1)) * (ky + 8)
    col_b = whole - row_a * cols - plane * ky
    place = (place + jnp.where(col_b < 0, ky + 7, col_b)).astype(jnp.float32)
    deep = (kx + 2) * (ky + 8)
    own = lax.broadcasted_iota(jnp.int32, (ny, ny), 0) == lax.broadcasted_iota(jnp.int32, (ny, ny), 1)
    slots = lax.broadcasted_iota(jnp.int32, (ny, deep), 1).astype(jnp.float32)
    picks = []
    for i in range(nx):
        column = jnp.sum(jnp.where(own, place[i:i + 1, :], 0.0), axis=1, keepdims=True)
        picks.append((column == slots).astype(jnp.bfloat16))
    pick = jnp.concatenate(picks, axis=0)
    loads[0].wait()
    loads[2].wait()
    wait_arrived(*coarse_go)
    for c in range(3):
        rest = table[c].reshape(deep, depth)
        moved = None
        for _ in range(3):
            part = rest.astype(jnp.bfloat16)
            rest = rest - part.astype(jnp.float32)
            piece = jnp.dot(pick, part, preferred_element_type=jnp.float32)
            moved = piece if moved is None else moved + piece
        fields[0][c, 2:nx + 2, OFF:OFF + ny, :] = start[c] + moved.reshape(nx, ny, depth)

    start_all(*first_go)
    loads[4].wait()
    loads[5].wait()
    wait_arrived(*load_go)
    wait_arrived(*shift_go)
    wait_arrived(*first_go)

    rows = nx // 2 + 1
    first_x, first_y = slab * nx, plane * ny
    lines = lax.broadcasted_iota(jnp.int32, (rows, ny + 8, depth), 1) + (first_y - 1)
    across = lax.broadcasted_iota(jnp.int32, (rows, ny + 8, depth), 0) + (first_x - 1)
    in_mesh_y = (lines >= 0) & (lines < ny * planes)

    def stencil(phase, c, first, count, top, tall):
        field = fields[phase]
        span = pl.ds(first - 1, count + 2)
        along_y = (
            field[c, span, pl.ds(top - 1, tall), :]
            + field[c, span, pl.ds(top, tall), :]
            + field[c, span, pl.ds(top + 1, tall), :]
        )
        boxed = box_z(along_y[:-2] + along_y[1:-1] + along_y[2:])
        centre = field[c, pl.ds(first, count), pl.ds(top, tall), :]
        here = shift[pl.ds(first - 1, count), pl.ds(top, tall), :]
        return centre, (3.0 + here) * centre - boxed * (1.0 / 3.0)

    rho = 1.0 / SIGMA
    keep, gain = 0.0, 1.0 / THETA
    for phase in range(DEGREE):
        if phase:
            rho_new = 1.0 / (2.0 * SIGMA - rho)
            keep, gain = rho_new * rho, 2.0 * rho_new / DELTA_C
            rho = rho_new
        if phase == 2:
            wait_arrived(*middle_go)
            wait_arrived(*resid_go)

        def wide(at, carry):
            c = at // 2
            first = 1 + (at % 2) * rows
            centre, applied = stencil(phase, c, first, rows, OFF - 1, ny + 8)
            where = (c, pl.ds(first - 1, rows), pl.ds(OFF - 1, ny + 8))
            left = (load if phase == 0 else resid_sent)[where] - applied
            direction = gain * left
            if phase:
                direction = direction + keep * centre
            node_x = across + (first - 1)
            inside = in_mesh_y & (node_x >= 0) & (node_x < nx * slabs)
            resid[where] = left
            fields[phase + 1][c, pl.ds(first, rows), pl.ds(OFF - 1, ny + 8), :] = jnp.where(
                inside, direction, 0.0
            )
            return carry

        def narrow(c, carry):
            centre, applied = stencil(phase, c, 2, nx, OFF, ny)
            where = (c, pl.ds(1, nx), pl.ds(OFF, ny))
            inner = (c, pl.ds(2, nx), pl.ds(OFF, ny))
            left = resid[where] - applied
            direction = keep * centre + gain * left
            if phase < DEGREE - 1:
                resid_sent[where] = left
                fields[phase + 1][inner] = direction
            else:
                for n in range(DEGREE):
                    direction = direction + fields[n][inner]
                smoothed[c] = direction
            return carry

        if phase % 2 == 0:
            lax.fori_loop(0, 6, wide, 0, unroll=True)
        else:
            lax.fori_loop(0, 3, narrow, 0, unroll=True)
        if phase == 1:
            start_all(*middle_go)
            start_all(*resid_go)
    start_all(*final_go)
    own_final.start()

    loads[3].wait()
    wait_arrived(*cons_go)
    for go in (coarse_go, load_go, shift_go, cons_go, first_go, middle_go, resid_go):
        wait_sent(*go)
    own_final.wait()
    wait_arrived(*final_go)
    wait_sent(*final_go)


def stresses(sizes, field_hbm, cons_hbm, disp_out, rec_out, ind_out,
             field, cons, rec, ind, in_sem, out_sem):
    nx, ny, depth, kx, ky, slabs, planes = sizes
    first_x = lax.axis_index("slab") * nx
    first_y = lax.axis_index("plane") * ny
    total_x, total_y = nx * slabs, ny * planes
    tall = ny + 8
    lane = lax.broadcasted_iota(jnp.int32, (tall, depth), 1)
    node_y = first_y - 1 + lax.broadcasted_iota(jnp.int32, (tall, depth), 0)
    valid_y = (node_y >= 0) & (node_y <= total_y - 2) & (lane <= depth - 2)
    lane = lax.broadcasted_iota(jnp.int32, (ny, depth), 1)
    node_y = first_y + lax.broadcasted_iota(jnp.int32, (ny, depth), 0)

    def half(ok):
        return jnp.where(ok, 0.5, 1.0)

    scale_y = half((node_y >= 1) & (node_y <= total_y - 2)) * half((lane >= 1) & (lane <= depth - 2))

    def arriving(n):
        lines = pl.ds(OFF - 1, ny + 2)
        nodes = pl.ds(n * ROWS_OUT + 2, ROWS_OUT) if n else pl.ds(0, ROWS_OUT + 2)
        corners = pl.ds(n * ROWS_OUT + 1, ROWS_OUT) if n else pl.ds(0, ROWS_OUT + 1)
        return (
            pltpu.make_async_copy(
                field_hbm.at[:, nodes, lines], field.at[:, nodes, lines], in_sem.at[2 * n]
            ),
            pltpu.make_async_copy(
                cons_hbm.at[corners, lines], cons.at[corners, lines], in_sem.at[2 * n + 1]
            ),
        )

    for n in range(nx // ROWS_OUT):
        for copy in arriving(n):
            copy.start()

    def displaced(n):
        return pltpu.make_async_copy(
            field.at[:, pl.ds(n * ROWS_OUT + 1, ROWS_OUT), pl.ds(OFF, ny)],
            disp_out.at[:, pl.ds(n * ROWS_OUT, ROWS_OUT)], out_sem.at[3 * n],
        )

    def part(n):
        here = pl.ds(n * ROWS_OUT, ROWS_OUT)
        return (
            pltpu.make_async_copy(rec.at[:, here], rec_out.at[:, here], out_sem.at[3 * n + 1]),
            pltpu.make_async_copy(ind.at[here], ind_out.at[here], out_sem.at[3 * n + 2]),
        )

    def corner_sums(c, i):
        low = field[c, i, pl.ds(OFF - 1, tall), :]
        high = field[c, i, pl.ds(OFF, tall), :]
        return low + high, high - low

    def element_row(i):
        grad_x, grad_y, grad_z = [], [], []
        for c in range(3):
            sum_a, diff_a = corner_sums(c, i)
            sum_b, diff_b = corner_sums(c, i + 1)
            gx, gy, gz = sum_b - sum_a, diff_a + diff_b, sum_a + sum_b
            grad_x.append(0.25 * (gx + next_z(gx)))
            grad_y.append(0.25 * (gy + next_z(gy)))
            grad_z.append(0.25 * (next_z(gz) - gz))
        exx, eyy, ezz = grad_x[0], grad_y[1], grad_z[2]
        exy = 0.5 * (grad_y[0] + grad_x[1])
        eyz = 0.5 * (grad_z[1] + grad_y[2])
        ezx = 0.5 * (grad_x[2] + grad_z[0])
        trace = exx + eyy + ezz
        third = trace * (1.0 / 3.0)
        sxx, syy, szz = exx - third, eyy - third, ezz - third
        equiv = (2.0 / 3.0) * (
            sxx * sxx + syy * syy + szz * szz + 2.0 * (exy * exy + eyz * eyz + ezx * ezx)
        )
        visc = cons[i, pl.ds(OFF - 1, tall), :] * jnp.exp(-0.425 * jnp.log(0.01 + 3.0 * equiv))
        twice = 2.0 * visc
        bulk = 4.0 * trace
        sig = [twice * sxx + bulk, twice * syy + bulk, twice * szz + bulk,
               twice * exy, twice * eyz, twice * ezx]
        norm_sq = (
            sig[0] * sig[0] + sig[1] * sig[1] + sig[2] * sig[2]
            + 2.0 * (sig[3] * sig[3] + sig[4] * sig[4] + sig[5] * sig[5])
        )
        node_x = first_x - 1 + i
        valid = valid_y & (node_x >= 0) & (node_x <= total_x - 2)
        summed = []
        for one in sig + [norm_sq]:
            one = jnp.where(valid, one, 0.0)
            one = one[0:ny] + one[1:ny + 1]
            summed.append(one + previous_z(one))
        return tuple(summed)

    def row(i, before):
        after = element_row(i)
        node_x = first_x + i - 1
        inside = ((node_x >= 1) & (node_x <= total_x - 2)).astype(jnp.float32)
        scale = scale_y * (1.0 - 0.5 * inside)
        total = [(a + b) * scale for a, b in zip(before, after)]
        for n in range(6):
            rec[n, i - 1] = total[n]
        ind[i - 1] = total[6] - (
            total[0] * total[0] + total[1] * total[1] + total[2] * total[2]
            + 2.0 * (total[3] * total[3] + total[4] * total[4] + total[5] * total[5])
        )
        return after

    carry = None
    for n in range(nx // ROWS_OUT):
        for copy in arriving(n):
            copy.wait()
        displaced(n).start()
        if n == 0:
            carry = element_row(0)
        carry = lax.fori_loop(1 + n * ROWS_OUT, 1 + (n + 1) * ROWS_OUT, row, carry, unroll=True)
        for copy in part(n):
            copy.start()
    for n in range(nx // ROWS_OUT):
        displaced(n).wait()
        for copy in part(n):
            copy.wait()


def body(sizes, *blocks):
    nx, ny, depth, kx, ky, slabs, planes = sizes
    hbm = pl.BlockSpec(memory_space=pltpu.HBM)
    f32 = jnp.float32
    padded = (
        jax.ShapeDtypeStruct((3, nx + 2, ny + 16, depth), f32),
        jax.ShapeDtypeStruct((nx + 1, ny + 16, depth), f32),
    )
    field, cons = pl.pallas_call(
        functools.partial(smooth, sizes),
        out_shape=padded,
        in_specs=[hbm] * 6,
        out_specs=(hbm,) * 2,
        scratch_shapes=[
            pltpu.VMEM((3, nx, ny, depth), f32),
            pltpu.VMEM((3, nx + 2, ny + 16, depth), f32),
            pltpu.VMEM((nx + 2, ny + 16, depth), f32),
            pltpu.VMEM((3, kx + 2, ky + 8, depth), f32),
            pltpu.VMEM((nx, ny), jnp.int32),
            pltpu.VMEM((DEGREE, 3, nx + 4, ny + 16, depth), f32),
            pltpu.VMEM((3, nx + 2, ny + 16, depth), f32),
            pltpu.VMEM((3, nx + 2, ny + 16, depth), f32),
            pltpu.VMEM((3, nx, ny, depth), f32),
            pltpu.SemaphoreType.DMA((7,)),
            pltpu.SemaphoreType.DMA((8, len(SIDES))),
            pltpu.SemaphoreType.DMA((8, len(SIDES))),
        ],
        compiler_params=pltpu.CompilerParams(
            collective_id=0, has_side_effects=True, vmem_limit_bytes=VMEM_BYTES
        ),
    )(*blocks)
    outs = (
        jax.ShapeDtypeStruct((3, nx, ny, depth), f32),
        jax.ShapeDtypeStruct((6, nx, ny, depth), f32),
        jax.ShapeDtypeStruct((nx, ny, depth), f32),
    )
    return pl.pallas_call(
        functools.partial(stresses, sizes),
        out_shape=outs,
        in_specs=[hbm] * 2,
        out_specs=(hbm,) * 3,
        scratch_shapes=[
            pltpu.VMEM(padded[0].shape, f32),
            pltpu.VMEM(padded[1].shape, f32),
            pltpu.VMEM(outs[1].shape, f32),
            pltpu.VMEM(outs[2].shape, f32),
            pltpu.SemaphoreType.DMA((2 * (nx // ROWS_OUT),)),
            pltpu.SemaphoreType.DMA((3 * (nx // ROWS_OUT),)),
        ],
        compiler_params=pltpu.CompilerParams(vmem_limit_bytes=VMEM_BYTES),
    )(field, cons)


def solution(mesh):
    in_specs = (
        P(None, "slab", "plane", None),
        P(None, "slab", "plane", None),
        P("slab", "plane", None),
        P(None, "slab", "plane", None),
        P("slab", "plane"),
        P("slab", "plane", None),
    )
    out_specs = (
        P(None, "slab", "plane", None),
        P(None, "slab", "plane", None),
        P("slab", "plane", None),
    )
    slabs, planes = mesh.shape["slab"], mesh.shape["plane"]

    def run(start_disp, load, shift, coarse, aggregate, consistency):
        sizes = (
            start_disp.shape[1] // slabs, start_disp.shape[2] // planes, start_disp.shape[3],
            coarse.shape[1] // slabs, coarse.shape[2] // planes, slabs, planes,
        )
        return jax.shard_map(
            functools.partial(body, sizes), mesh=mesh, in_specs=in_specs, out_specs=out_specs,
            check_vma=False,
        )(start_disp, load, shift, coarse, aggregate, consistency)

    return run
```

```python
import functools

import jax
import jax.numpy as jnp
from jax import lax
from jax.experimental import pallas as pl
from jax.experimental.pallas import tpu as pltpu
from jax.sharding import PartitionSpec as P

DEGREE = 4
THETA = 4.5
DELTA_C = 3.5
SIGMA = THETA / DELTA_C
MESH = pl.DeviceIdType.MESH
OFF = 8
SIDES = ((1, 1), (1, -1), (-1, 1), (-1, -1), (0, 1), (0, -1), (1, 0), (-1, 0))
VMEM_BYTES = 56 * 1024 * 1024
ROWS_OUT = 4
LOW_SIDES = ((0, 1), (1, 1), (1, 0))


def edge(step, first, count, width=1):
    if step > 0:
        return pl.ds(first + count - width, width), pl.ds(first - width, width)
    if step < 0:
        return pl.ds(first, width), pl.ds(first + count, width)
    return pl.ds(first, count), pl.ds(first, count)


def box_z(x):
    lane = lax.broadcasted_iota(jnp.int32, x.shape, x.ndim - 1)
    depth = x.shape[-1]
    below = jnp.where(lane == 0, 0.0, pltpu.roll(x, 1, x.ndim - 1))
    above = jnp.where(lane == depth - 1, 0.0, pltpu.roll(x, depth - 1, x.ndim - 1))
    return x + below + above


def next_z(x):
    return pltpu.roll(x, x.shape[-1] - 1, x.ndim - 1)


def previous_z(x):
    return pltpu.roll(x, 1, x.ndim - 1)


def smooth(sizes, *refs):
    nx, ny, depth, kx, ky, slabs, planes = sizes
    (start_hbm, load_hbm, shift_hbm, coarse_hbm, agg_hbm, cons_hbm, final, cons,
     start, load, shift, table, agg, earlier, resid, resid_sent, smoothed,
     in_sem, send_sem, recv_sem) = refs
    fields = [earlier.at[n] for n in range(DEGREE)]
    slab = lax.axis_index("slab")
    plane = lax.axis_index("plane")

    def exists(step_x, step_y):
        x, y = slab + step_x, plane + step_y
        return (x >= 0) & (x < slabs) & (y >= 0) & (y < planes)

    loads = [
        pltpu.make_async_copy(coarse_hbm, table.at[:, pl.ds(1, kx), pl.ds(0, ky)], in_sem.at[0]),
        pltpu.make_async_copy(agg_hbm, agg, in_sem.at[1]),
        pltpu.make_async_copy(start_hbm, start, in_sem.at[2]),
        pltpu.make_async_copy(cons_hbm, cons.at[pl.ds(1, nx), pl.ds(OFF, ny)], in_sem.at[3]),
        pltpu.make_async_copy(
            load_hbm, load.at[:, pl.ds(1, nx), pl.ds(OFF, ny)], in_sem.at[4]
        ),
        pltpu.make_async_copy(shift_hbm, shift.at[pl.ds(1, nx), pl.ds(OFF, ny)], in_sem.at[5]),
    ]
    for n in (0, 1, 2, 4, 5, 3):
        loads[n].start()

    zero_table = jnp.zeros((3, 8, depth), jnp.float32)
    for a in range(kx + 2):
        table[:, a, ky:ky + 8, :] = zero_table
    table[:, 0, 0:ky, :] = zero_table
    table[:, kx + 1, 0:ky, :] = zero_table

    for field in (fields[0], fields[2]):
        for i in range(nx + 4):
            if i < 2 or i >= nx + 2:
                field[:, i] = jnp.zeros((3, ny + 16, depth), jnp.float32)
            else:
                field[:, i, 0:OFF, :] = zero_table
                field[:, i, OFF + ny:OFF + ny + 8, :] = zero_table

    barrier = pltpu.get_barrier_semaphore()
    for step_x, step_y in SIDES:
        @pl.when(exists(step_x, step_y))
        def _():
            pl.semaphore_signal(
                barrier, inc=1, device_id=(slab + step_x, plane + step_y), device_id_type=MESH
            )

    near_x = 1 + (slab > 0).astype(jnp.int32) + (slab < slabs - 1).astype(jnp.int32)
    near_y = 1 + (plane > 0).astype(jnp.int32) + (plane < planes - 1).astype(jnp.int32)
    pl.semaphore_wait(barrier, near_x * near_y - 1)

    def remote(source, target, phase, side):
        step_x, step_y = SIDES[side]
        return pltpu.make_async_remote_copy(
            src_ref=source, dst_ref=target,
            send_sem=send_sem.at[phase, side], recv_sem=recv_sem.at[phase, side],
            device_id=(slab + step_x, plane + step_y), device_id_type=MESH,
        )

    def start_all(make, phase, sides=SIDES):
        for side, (step_x, step_y) in enumerate(SIDES):
            if (step_x, step_y) in sides:
                @pl.when(exists(step_x, step_y))
                def _():
                    remote(*make(step_x, step_y), phase, side).start()

    def wait_arrived(make, phase, sides=SIDES):
        for side, (step_x, step_y) in enumerate(SIDES):
            if (step_x, step_y) in sides:
                @pl.when(exists(-step_x, -step_y))
                def _():
                    remote(*make(step_x, step_y), phase, side).wait_recv()

    def wait_sent(make, phase, sides=SIDES):
        for side, (step_x, step_y) in enumerate(SIDES):
            if (step_x, step_y) in sides:
                @pl.when(exists(step_x, step_y))
                def _():
                    remote(*make(step_x, step_y), phase, side).wait_send()

    def coarse_edge(step_x, step_y):
        from_x, to_x = edge(step_x, 1, kx)
        from_y, to_y = edge(step_y, 0, ky)
        from_x = pl.ds(from_x.start - 1, from_x.size)
        if step_y > 0:
            to_y = pl.ds(ky + 7, 1)
        return coarse_hbm.at[:, from_x, from_y], table.at[:, to_x, to_y]

    def input_edge(source, target):
        lead = (slice(None),) * (len(source.shape) - 3)

        def make(step_x, step_y):
            from_x, to_x = edge(step_x, 1, nx)
            from_y, to_y = edge(step_y, OFF, ny)
            from_x = pl.ds(from_x.start - 1, from_x.size)
            from_y = pl.ds(from_y.start - OFF, from_y.size)
            return source.at[lead + (from_x, from_y)], target.at[lead + (to_x, to_y)]
        return make

    def field_edge(field, width):
        def make(step_x, step_y):
            from_x, to_x = edge(step_x, width, nx, width)
            from_y, to_y = edge(step_y, OFF, ny, width)
            return field.at[:, from_x, from_y], field.at[:, to_x, to_y]
        return make

    coarse_go = (coarse_edge, 0)
    load_go = (input_edge(load_hbm, load), 1)
    shift_go = (input_edge(shift_hbm, shift), 2)
    cons_go = (input_edge(cons_hbm, cons), 3, LOW_SIDES)
    first_go = (field_edge(fields[0], 2), 4)
    middle_go = (field_edge(fields[2], 2), 5)
    resid_go = (field_edge(resid_sent, 1), 6)

    def final_edge(step_x, step_y):
        from_x, to_x = edge(step_x, 1, nx)
        from_y, to_y = edge(step_y, OFF, ny)
        from_x = pl.ds(from_x.start - 1, from_x.size)
        from_y = pl.ds(from_y.start - OFF, from_y.size)
        return smoothed.at[:, from_x, from_y], final.at[:, to_x, to_y]

    final_go = (final_edge, 7)
    own_final = pltpu.make_async_copy(
        smoothed, final.at[:, pl.ds(1, nx), pl.ds(OFF, ny)], in_sem.at[6]
    )
    start_all(*coarse_go)
    start_all(*load_go)
    start_all(*shift_go)

    loads[1].wait()
    cols = ky * planes
    whole = agg[...]
    if cols & (cols - 1) == 0:
        row_a = lax.shift_right_logical(whole, cols.bit_length() - 1)
    else:
        row_a = lax.div(whole, cols)
    place = (row_a - (slab * kx - 1)) * (ky + 8)
    col_b = whole - row_a * cols - plane * ky
    place = (place + jnp.where(col_b < 0, ky + 7, col_b)).astype(jnp.float32)
    deep = (kx + 2) * (ky + 8)
    own = lax.broadcasted_iota(jnp.int32, (ny, ny), 0) == lax.broadcasted_iota(jnp.int32, (ny, ny), 1)
    slots = lax.broadcasted_iota(jnp.int32, (ny, deep), 1).astype(jnp.float32)
    picks = []
    for i in range(nx):
        column = jnp.sum(jnp.where(own, place[i:i + 1, :], 0.0), axis=1, keepdims=True)
        picks.append((column == slots).astype(jnp.bfloat16))
    pick = jnp.concatenate(picks, axis=0)
    loads[0].wait()
    loads[2].wait()
    wait_arrived(*coarse_go)
    for c in range(3):
        rest = table[c].reshape(deep, depth)
        moved = None
        for _ in range(3):
            part = rest.astype(jnp.bfloat16)
            rest = rest - part.astype(jnp.float32)
            piece = jnp.dot(pick, part, preferred_element_type=jnp.float32)
            moved = piece if moved is None else moved + piece
        fields[0][c, 2:nx + 2, OFF:OFF + ny, :] = start[c] + moved.reshape(nx, ny, depth)

    start_all(*first_go)
    start_all(*cons_go)
    loads[4].wait()
    loads[5].wait()
    wait_arrived(*load_go)
    wait_arrived(*shift_go)
    wait_arrived(*first_go)

    rows = nx // 2 + 1
    first_x, first_y = slab * nx, plane * ny
    lines = lax.broadcasted_iota(jnp.int32, (rows, ny + 8, depth), 1) + (first_y - 1)
    across = lax.broadcasted_iota(jnp.int32, (rows, ny + 8, depth), 0) + (first_x - 1)
    in_mesh_y = (lines >= 0) & (lines < ny * planes)

    def stencil(phase, c, first, count, top, tall):
        field = fields[phase]
        span = pl.ds(first - 1, count + 2)
        along_y = (
            field[c, span, pl.ds(top - 1, tall), :]
            + field[c, span, pl.ds(top, tall), :]
            + field[c, span, pl.ds(top + 1, tall), :]
        )
        boxed = box_z(along_y[:-2] + along_y[1:-1] + along_y[2:])
        centre = field[c, pl.ds(first, count), pl.ds(top, tall), :]
        here = shift[pl.ds(first - 1, count), pl.ds(top, tall), :]
        return centre, (3.0 + here) * centre - boxed * (1.0 / 3.0)

    rho = 1.0 / SIGMA
    keep, gain = 0.0, 1.0 / THETA
    for phase in range(DEGREE):
        if phase:
            rho_new = 1.0 / (2.0 * SIGMA - rho)
            keep, gain = rho_new * rho, 2.0 * rho_new / DELTA_C
            rho = rho_new
        if phase == 2:
            wait_arrived(*middle_go)
            wait_arrived(*resid_go)

        def wide(at, carry):
            c = at // 2
            first = 1 + (at % 2) * rows
            centre, applied = stencil(phase, c, first, rows, OFF - 1, ny + 8)
            where = (c, pl.ds(first - 1, rows), pl.ds(OFF - 1, ny + 8))
            left = (load if phase == 0 else resid_sent)[where] - applied
            direction = gain * left
            if phase:
                direction = direction + keep * centre
            node_x = across + (first - 1)
            inside = in_mesh_y & (node_x >= 0) & (node_x < nx * slabs)
            resid[where] = left
            fields[phase + 1][c, pl.ds(first, rows), pl.ds(OFF - 1, ny + 8), :] = jnp.where(
                inside, direction, 0.0
            )
            return carry

        def narrow(c, carry):
            centre, applied = stencil(phase, c, 2, nx, OFF, ny)
            where = (c, pl.ds(1, nx), pl.ds(OFF, ny))
            inner = (c, pl.ds(2, nx), pl.ds(OFF, ny))
            left = resid[where] - applied
            direction = keep * centre + gain * left
            if phase < DEGREE - 1:
                resid_sent[where] = left
                fields[phase + 1][inner] = direction
            else:
                for n in range(DEGREE):
                    direction = direction + fields[n][inner]
                smoothed[c] = direction
            return carry

        if phase % 2 == 0:
            lax.fori_loop(0, 6, wide, 0, unroll=True)
        else:
            lax.fori_loop(0, 3, narrow, 0, unroll=True)
        if phase == 1:
            start_all(*middle_go)
            start_all(*resid_go)
    start_all(*final_go)
    own_final.start()

    loads[3].wait()
    wait_arrived(*cons_go)
    for go in (coarse_go, load_go, shift_go, cons_go, first_go, middle_go, resid_go):
        wait_sent(*go)
    own_final.wait()
    wait_arrived(*final_go)
    wait_sent(*final_go)


def stresses(sizes, field_hbm, cons_hbm, disp_out, rec_out, ind_out,
             field, cons, rec, ind, in_sem, out_sem):
    nx, ny, depth, kx, ky, slabs, planes = sizes
    first_x = lax.axis_index("slab") * nx
    first_y = lax.axis_index("plane") * ny
    total_x, total_y = nx * slabs, ny * planes
    tall = ny + 8
    lane = lax.broadcasted_iota(jnp.int32, (tall, depth), 1)
    node_y = first_y - 1 + lax.broadcasted_iota(jnp.int32, (tall, depth), 0)
    valid_y = (node_y >= 0) & (node_y <= total_y - 2) & (lane <= depth - 2)
    lane = lax.broadcasted_iota(jnp.int32, (ny, depth), 1)
    node_y = first_y + lax.broadcasted_iota(jnp.int32, (ny, depth), 0)

    def half(ok):
        return jnp.where(ok, 0.5, 1.0)

    scale_y = half((node_y >= 1) & (node_y <= total_y - 2)) * half((lane >= 1) & (lane <= depth - 2))

    def arriving(n):
        lines = pl.ds(OFF - 1, ny + 2)
        nodes = pl.ds(n * ROWS_OUT + 2, ROWS_OUT) if n else pl.ds(0, ROWS_OUT + 2)
        corners = pl.ds(n * ROWS_OUT + 1, ROWS_OUT) if n else pl.ds(0, ROWS_OUT + 1)
        return (
            pltpu.make_async_copy(
                field_hbm.at[:, nodes, lines], field.at[:, nodes, lines], in_sem.at[2 * n]
            ),
            pltpu.make_async_copy(
                cons_hbm.at[corners, lines], cons.at[corners, lines], in_sem.at[2 * n + 1]
            ),
        )

    for n in range(nx // ROWS_OUT):
        for copy in arriving(n):
            copy.start()

    def displaced(n):
        return pltpu.make_async_copy(
            field.at[:, pl.ds(n * ROWS_OUT + 1, ROWS_OUT), pl.ds(OFF, ny)],
            disp_out.at[:, pl.ds(n * ROWS_OUT, ROWS_OUT)], out_sem.at[3 * n],
        )

    def part(n):
        here = pl.ds(n * ROWS_OUT, ROWS_OUT)
        return (
            pltpu.make_async_copy(rec.at[:, here], rec_out.at[:, here], out_sem.at[3 * n + 1]),
            pltpu.make_async_copy(ind.at[here], ind_out.at[here], out_sem.at[3 * n + 2]),
        )

    def corner_sums(c, i):
        low = field[c, i, pl.ds(OFF - 1, tall), :]
        high = field[c, i, pl.ds(OFF, tall), :]
        return low + high, high - low

    def element_row(i):
        grad_x, grad_y, grad_z = [], [], []
        for c in range(3):
            sum_a, diff_a = corner_sums(c, i)
            sum_b, diff_b = corner_sums(c, i + 1)
            gx, gy, gz = sum_b - sum_a, diff_a + diff_b, sum_a + sum_b
            grad_x.append(0.25 * (gx + next_z(gx)))
            grad_y.append(0.25 * (gy + next_z(gy)))
            grad_z.append(0.25 * (next_z(gz) - gz))
        exx, eyy, ezz = grad_x[0], grad_y[1], grad_z[2]
        exy = 0.5 * (grad_y[0] + grad_x[1])
        eyz = 0.5 * (grad_z[1] + grad_y[2])
        ezx = 0.5 * (grad_x[2] + grad_z[0])
        trace = exx + eyy + ezz
        third = trace * (1.0 / 3.0)
        sxx, syy, szz = exx - third, eyy - third, ezz - third
        equiv = (2.0 / 3.0) * (
            sxx * sxx + syy * syy + szz * szz + 2.0 * (exy * exy + eyz * eyz + ezx * ezx)
        )
        visc = cons[i, pl.ds(OFF - 1, tall), :] * jnp.exp(-0.425 * jnp.log(0.01 + 3.0 * equiv))
        twice = 2.0 * visc
        bulk = 4.0 * trace
        sig = [twice * sxx + bulk, twice * syy + bulk, twice * szz + bulk,
               twice * exy, twice * eyz, twice * ezx]
        norm_sq = (
            sig[0] * sig[0] + sig[1] * sig[1] + sig[2] * sig[2]
            + 2.0 * (sig[3] * sig[3] + sig[4] * sig[4] + sig[5] * sig[5])
        )
        node_x = first_x - 1 + i
        valid = valid_y & (node_x >= 0) & (node_x <= total_x - 2)
        summed = []
        for one in sig + [norm_sq]:
            one = jnp.where(valid, one, 0.0)
            one = one[0:ny] + one[1:ny + 1]
            summed.append(one + previous_z(one))
        return tuple(summed)

    def row(i, before):
        after = element_row(i)
        node_x = first_x + i - 1
        inside = ((node_x >= 1) & (node_x <= total_x - 2)).astype(jnp.float32)
        scale = scale_y * (1.0 - 0.5 * inside)
        total = [(a + b) * scale for a, b in zip(before, after)]
        for n in range(6):
            rec[n, i - 1] = total[n]
        ind[i - 1] = total[6] - (
            total[0] * total[0] + total[1] * total[1] + total[2] * total[2]
            + 2.0 * (total[3] * total[3] + total[4] * total[4] + total[5] * total[5])
        )
        return after

    carry = None
    for n in range(nx // ROWS_OUT):
        for copy in arriving(n):
            copy.wait()
        displaced(n).start()
        if n == 0:
            carry = element_row(0)
        carry = lax.fori_loop(1 + n * ROWS_OUT, 1 + (n + 1) * ROWS_OUT, row, carry, unroll=True)
        for copy in part(n):
            copy.start()
    for n in range(nx // ROWS_OUT):
        displaced(n).wait()
        for copy in part(n):
            copy.wait()


def body(sizes, *blocks):
    nx, ny, depth, kx, ky, slabs, planes = sizes
    hbm = pl.BlockSpec(memory_space=pltpu.HBM)
    f32 = jnp.float32
    padded = (
        jax.ShapeDtypeStruct((3, nx + 2, ny + 16, depth), f32),
        jax.ShapeDtypeStruct((nx + 1, ny + 16, depth), f32),
    )
    field, cons = pl.pallas_call(
        functools.partial(smooth, sizes),
        out_shape=padded,
        in_specs=[hbm] * 6,
        out_specs=(hbm,) * 2,
        scratch_shapes=[
            pltpu.VMEM((3, nx, ny, depth), f32),
            pltpu.VMEM((3, nx + 2, ny + 16, depth), f32),
            pltpu.VMEM((nx + 2, ny + 16, depth), f32),
            pltpu.VMEM((3, kx + 2, ky + 8, depth), f32),
            pltpu.VMEM((nx, ny), jnp.int32),
            pltpu.VMEM((DEGREE, 3, nx + 4, ny + 16, depth), f32),
            pltpu.VMEM((3, nx + 2, ny + 16, depth), f32),
            pltpu.VMEM((3, nx + 2, ny + 16, depth), f32),
            pltpu.VMEM((3, nx, ny, depth), f32),
            pltpu.SemaphoreType.DMA((7,)),
            pltpu.SemaphoreType.DMA((8, len(SIDES))),
            pltpu.SemaphoreType.DMA((8, len(SIDES))),
        ],
        compiler_params=pltpu.CompilerParams(
            collective_id=0, has_side_effects=True, vmem_limit_bytes=VMEM_BYTES
        ),
    )(*blocks)
    outs = (
        jax.ShapeDtypeStruct((3, nx, ny, depth), f32),
        jax.ShapeDtypeStruct((6, nx, ny, depth), f32),
        jax.ShapeDtypeStruct((nx, ny, depth), f32),
    )
    return pl.pallas_call(
        functools.partial(stresses, sizes),
        out_shape=outs,
        in_specs=[hbm] * 2,
        out_specs=(hbm,) * 3,
        scratch_shapes=[
            pltpu.VMEM(padded[0].shape, f32),
            pltpu.VMEM(padded[1].shape, f32),
            pltpu.VMEM(outs[1].shape, f32),
            pltpu.VMEM(outs[2].shape, f32),
            pltpu.SemaphoreType.DMA((2 * (nx // ROWS_OUT),)),
            pltpu.SemaphoreType.DMA((3 * (nx // ROWS_OUT),)),
        ],
        compiler_params=pltpu.CompilerParams(vmem_limit_bytes=VMEM_BYTES),
    )(field, cons)


def solution(mesh):
    in_specs = (
        P(None, "slab", "plane", None),
        P(None, "slab", "plane", None),
        P("slab", "plane", None),
        P(None, "slab", "plane", None),
        P("slab", "plane"),
        P("slab", "plane", None),
    )
    out_specs = (
        P(None, "slab", "plane", None),
        P(None, "slab", "plane", None),
        P("slab", "plane", None),
    )
    slabs, planes = mesh.shape["slab"], mesh.shape["plane"]

    def run(start_disp, load, shift, coarse, aggregate, consistency):
        sizes = (
            start_disp.shape[1] // slabs, start_disp.shape[2] // planes, start_disp.shape[3],
            coarse.shape[1] // slabs, coarse.shape[2] // planes, slabs, planes,
        )
        return jax.shard_map(
            functools.partial(body, sizes), mesh=mesh, in_specs=in_specs, out_specs=out_specs,
            check_vma=False,
        )(start_disp, load, shift, coarse, aggregate, consistency)

    return run
```
